32 devices in a mesh: fsdp: 16 (over z, y, x), dp: 2 (over core).
Axes of the slice: x: 2, y: 2, z: 4, core: 2. Of those that a mesh axis runs over, the one named last changes fastest.
Arguments:
- image_states: bfloat16 [32, 325, 768], P(('fsdp', 'dp')), may hold values from -6 to 6
- text_states: bfloat16 [32, 513, 768], P(('fsdp', 'dp')), may hold values from -6 to 6
- size_group: int32 [32], P(('fsdp', 'dp')), may hold values from 0 to 1
- caption_len: int32 [32], P(('fsdp', 'dp')), may hold values from 16 to 512, as said below
- cotangent: bfloat16 [32, 839, 768], P(('fsdp', 'dp')), may hold values from -6 to 6
- image_proj: bfloat16 [768, 768], P('fsdp'), may hold values from -0.21875 to 0.21875
- image_bias: bfloat16 [768], P('fsdp'), may hold values from -1.75 to 1.75
- text_proj: bfloat16 [768, 768], P('fsdp'), may hold values from -0.21875 to 0.21875
- text_bias: bfloat16 [768], P('fsdp'), may hold values from -1.75 to 1.75
- cls_token: bfloat16 [768], P('fsdp'), may hold values from -6 to 6
- first_gain: bfloat16 [768], P('fsdp'), may hold values from 0.5 to 1.5
- first_shift: bfloat16 [768], P('fsdp'), may hold values from -1.75 to 1.75
- query_proj: bfloat16 [768, 768], P('fsdp'), may hold values from -0.21875 to 0.21875
- query_bias: bfloat16 [768], P('fsdp'), may hold values from -1.75 to 1.75
- key_proj: bfloat16 [768, 768], P('fsdp'), may hold values from -0.21875 to 0.21875
- value_proj: bfloat16 [768, 768], P('fsdp'), may hold values from -0.21875 to 0.21875
- value_bias: bfloat16 [768], P('fsdp'), may hold values from -0.1875 to 0.1875
- output_proj: bfloat16 [768, 768], P('fsdp'), may hold values from -4 to 4
- output_bias: bfloat16 [768], P('fsdp'), may hold values from -1.75 to 1.75
- second_gain: bfloat16 [768], P('fsdp'), may hold values from 0.5 to 1.5
- second_shift: bfloat16 [768], P('fsdp'), may hold values from -1.75 to 1.75
- hidden_proj: bfloat16 [768, 3072], P('fsdp'), may hold values from -0.21875 to 0.21875
- hidden_bias: bfloat16 [3072], P('fsdp'), may hold values from -1.75 to 1.75
- return_proj: bfloat16 [3072, 768], P('fsdp'), may hold values from -0.109375 to 0.109375
- return_bias: bfloat16 [768], P('fsdp'), may hold values from -1.75 to 1.75
Outputs:
- layer_out: bfloat16 [32, 839, 768], P(('fsdp', 'dp'))
- image_grad: float32 [32, 325, 768], P(('fsdp', 'dp'))
- text_grad: float32 [32, 513, 768], P(('fsdp', 'dp'))
- grad_image_proj: float32 [768, 768], P('fsdp')
- grad_image_bias: float32 [768], P('fsdp')
- grad_text_proj: float32 [768, 768], P('fsdp')
- grad_text_bias: float32 [768], P('fsdp')
- grad_cls_token: float32 [768], P('fsdp')
- grad_first_gain: float32 [768], P('fsdp')
- grad_first_shift: float32 [768], P('fsdp')
- grad_query_proj: float32 [768, 768], P('fsdp')
- grad_query_bias: float32 [768], P('fsdp')
- grad_key_proj: float32 [768, 768], P('fsdp')
- grad_value_proj: float32 [768, 768], P('fsdp')
- grad_value_bias: float32 [768], P('fsdp')
- grad_output_proj: float32 [768, 768], P('fsdp')
- grad_output_bias: float32 [768], P('fsdp')
- grad_second_gain: float32 [768], P('fsdp')
- grad_second_shift: float32 [768], P('fsdp')
- grad_hidden_proj: float32 [768, 3072], P('fsdp')
- grad_hidden_bias: float32 [3072], P('fsdp')
- grad_return_proj: float32 [3072, 768], P('fsdp')
- grad_return_bias: float32 [768], P('fsdp')
The draws below stay inside these ranges and needn't reach their ends.
Inputs may be any that keep to these rules, and one draw needn't show every extreme that they name: `size_group`: 1 marks an item with 325 image rows in use, 0 one with the first 197. The caption tokens of each item fill its first caption_len text slots.
All inputs are finite; a program needn't handle non-finite values.
Results may differ from the reference program's by a relative error of at most 0.014.
Values may be sent and summed in bfloat16 or wider, within the bound.
No kernel may reach another device: no remote copies, remote signals or barrier semaphores. Data moves between devices by JAX's collectives and lax.ppermute only.
A program may use at most 192 MiB of HBM per device.

```python
import jax
import jax.numpy as jnp
from jax import lax

D = 768
HEADS = 12
HEAD_DIM = 64
FF = 3072
PATCH_BIG = 325
PATCH_SMALL = 197
TEXT = 512
ROWS = 839
ITEMS = 32


def draw_caption_len(key, part):
    key = jax.random.fold_in(key, 7)
    base_key, order_key = jax.random.split(key)
    shortest = max(1, TEXT // 32)
    lengths = jax.random.randint(base_key, (ITEMS,), shortest, TEXT + 1, dtype=jnp.int32)
    order = jax.random.permutation(order_key, ITEMS)
    lengths = lengths.at[order[0]].set(TEXT)
    lengths = lengths.at[order[1]].set(shortest)
    return lengths


def plant(values, own_key, least, top_value):
    shape = values.shape
    index_at = [jax.random.randint(jax.random.fold_in(own_key, axis), (), 0, shape[axis]) for axis in range(len(shape))]
    values = values.at[tuple(index_at)].set(least)
    longest = shape.index(max(shape))
    index_at[longest] = (index_at[longest] + 1) % shape[longest]
    return values.at[tuple(index_at)].set(top_value)


def steps_of(own_key, dims, pieces, least, high):
    level, own = 1.0, jax.random.fold_in(own_key, 6)
    for axis_at, blocks in pieces:
        draws = jnp.exp(jax.random.uniform(jax.random.fold_in(own, axis_at), (blocks,), jnp.float32, least / len(pieces), high / len(pieces)))
        level = level * jnp.repeat(draws, dims[axis_at] // blocks).reshape([-1 if axis == axis_at else 1 for axis in range(len(dims))])
    return level


def centred(rng, dims, deviation, bound, cuts=(), kind=jnp.bfloat16):
    array = deviation * jax.random.normal(rng, dims, jnp.float32)
    if cuts:
        array = array * steps_of(rng, dims, cuts, -0.22, 0.18)
    return jnp.clip(array, -bound, bound).astype(kind)


def setup_inputs(seed: int = 0) -> dict:
    key_list = jax.random.split(jax.random.key(seed), 26)
    return {
        "image_states": centred(key_list[0], (ITEMS, PATCH_BIG, D), 1.0, 6.0, ((0, 32),)),
        "text_states": centred(key_list[1], (ITEMS, TEXT + 1, D), 1.0, 6.0, ((0, 32),)),
        "size_group": plant(jax.random.randint(key_list[2], (ITEMS,), 0, 2), jax.random.fold_in(key_list[2], 1), 0, 1).astype(jnp.int32),
        "caption_len": draw_caption_len(jax.random.fold_in(key_list[25], 71), 0),
        "cotangent": centred(key_list[4], (ITEMS, ROWS, D), 1.0, 6.0, ((0, 32),)),
        "image_proj": centred(key_list[5], (D, D), D ** -0.5, 0.21875, ((0, 16),)),
        "image_bias": centred(key_list[6], (D,), 0.3, 1.75, ((0, 16),)),
        "text_proj": centred(key_list[7], (D, D), D ** -0.5, 0.21875, ((0, 16),)),
        "text_bias": centred(key_list[8], (D,), 0.3, 1.75, ((0, 16),)),
        "cls_token": centred(key_list[9], (D,), 1.0, 6.0, ((0, 16),)),
        "first_gain": jnp.clip(1.0 + 0.1 * jax.random.normal(key_list[10], (D,), jnp.float32), 0.5, 1.5).astype(jnp.bfloat16),
        "first_shift": centred(key_list[11], (D,), 0.3, 1.75, ((0, 16),)),
        "query_proj": centred(key_list[12], (D, D), D ** -0.5, 0.21875, ((0, 16),)),
        "query_bias": centred(key_list[13], (D,), 0.3, 1.75, ((0, 16),)),
        "key_proj": centred(key_list[14], (D, D), D ** -0.5, 0.21875, ((0, 16),)),
        "value_proj": centred(key_list[15], (D, D), D ** -0.5, 0.21875, ((0, 16),)),
        "value_bias": centred(key_list[16], (D,), 0.03, 0.1875, ((0, 16),)),
        "output_proj": centred(key_list[17], (D, D), (max(1, D * 3 // ROWS)) ** -0.5, 4.0, ((0, 16),)),
        "output_bias": centred(key_list[18], (D,), 0.3, 1.75, ((0, 16),)),
        "second_gain": jnp.clip(1.0 + 0.1 * jax.random.normal(key_list[19], (D,), jnp.float32), 0.5, 1.5).astype(jnp.bfloat16),
        "second_shift": centred(key_list[20], (D,), 0.3, 1.75, ((0, 16),)),
        "hidden_proj": centred(key_list[21], (D, FF), D ** -0.5, 0.21875, ((0, 16),)),
        "hidden_bias": centred(key_list[22], (FF,), 0.3, 1.75, ((0, 16),)),
        "return_proj": centred(key_list[23], (FF, D), FF ** -0.5, 0.109375, ((0, 16),)),
        "return_bias": centred(key_list[24], (D,), 0.3, 1.75, ((0, 16),)),
    }


EPSILON = 1e-06
NEGATIVE = -1e+30
HIGHEST = lax.Precision.HIGHEST

@jax.custom_vjp
def low(v):
    return lax.optimization_barrier(v.astype(jnp.bfloat16)).astype(jnp.float32)

@jax.custom_vjp
def low_back(v):
    return v

def low_keep(v):
    return (low(v), None)

def low_pass(kept, grad):
    return (grad,)

def back_keep(v):
    return (v, None)

def back_low(kept, grad):
    return (low(grad),)
low.defvjp(low_keep, low_pass)
low_back.defvjp(back_keep, back_low)

def product(left, right):
    return jnp.dot(left, right, precision=HIGHEST, preferred_element_type=jnp.float32)

def layer_norm(values, gain, shift):
    centered = values - lax.optimization_barrier(jnp.mean(values, -1, keepdims=True))
    scaled = centered * lax.rsqrt(lax.optimization_barrier(jnp.mean(centered * centered, -1, keepdims=True)) + EPSILON)
    return scaled * gain + shift

def key_mask(size_code, length, row_count):
    position = jnp.arange(row_count, dtype=jnp.int32)
    patches = jnp.where(size_code == 1, PATCH_BIG, PATCH_SMALL).astype(jnp.int32)
    image_live = (position >= 1) & (position <= patches)
    text_live = (position >= 1 + PATCH_BIG) & (position < 1 + PATCH_BIG + length)
    return (position == 0) | image_live | text_live

def item_forward(params, image_rows, text_rows, size_code, length):
    image_proj, image_bias, text_proj, text_bias, cls_token, first_gain, first_shift, query_proj, query_bias, key_proj, value_proj, value_bias, output_proj, output_bias, second_gain, second_shift, hidden_proj, hidden_bias, return_proj, return_bias = params
    image_part = low_back(product(image_rows, image_proj) + image_bias)
    text_part = low_back(product(text_rows, text_proj) + text_bias)
    embedded = jnp.concatenate([cls_token[None, :], image_part, text_part], 0)
    row_count = embedded.shape[0]
    normed = low(layer_norm(embedded, first_gain, first_shift))
    queries = low(low_back(product(normed, query_proj) + query_bias))
    keys_all = low(low_back(product(normed, key_proj)))
    values_all = low(low_back(product(normed, value_proj) + value_bias))

    def by_heads(values):
        return values.reshape(row_count, HEADS, HEAD_DIM)
    scores = jnp.einsum('qhd,khd->hqk', by_heads(queries), by_heads(keys_all), precision=HIGHEST) * HEAD_DIM ** (-0.5)
    key_live = key_mask(size_code, length, row_count)
    scores = low_back(jnp.where(key_live[None, None, :], scores, NEGATIVE))
    row_top = lax.optimization_barrier(jnp.max(scores, -1, keepdims=True))
    exps = jnp.exp(scores - row_top)
    prob_rows = low(exps / lax.optimization_barrier(jnp.sum(exps, -1, keepdims=True)))
    mixed_heads = jnp.einsum('hqk,khd->qhd', prob_rows, by_heads(values_all), precision=HIGHEST)
    attended = low(low_back(mixed_heads.reshape(row_count, HEADS * HEAD_DIM)))
    middle = embedded + low_back(product(attended, output_proj) + output_bias)
    second = low(layer_norm(middle, second_gain, second_shift))
    inner_pre = low_back(product(second, hidden_proj) + hidden_bias)
    activated = low(jax.nn.gelu(inner_pre, approximate=False))
    return middle + low_back(product(activated, return_proj) + return_bias)

def reference(image_states, text_states, size_group, caption_len, cotangent, image_proj, image_bias, text_proj, text_bias, cls_token, first_gain, first_shift, query_proj, query_bias, key_proj, value_proj, value_bias, output_proj, output_bias, second_gain, second_shift, hidden_proj, hidden_bias, return_proj, return_bias):
    params = tuple((weight.astype(jnp.float32) for weight in (image_proj, image_bias, text_proj, text_bias, cls_token, first_gain, first_shift, query_proj, query_bias, key_proj, value_proj, value_bias, output_proj, output_bias, second_gain, second_shift, hidden_proj, hidden_bias, return_proj, return_bias)))
    images = image_states.astype(jnp.float32)
    text_all = text_states.astype(jnp.float32)
    item_count = images.shape[0]
    per_block = 4
    code_rows = size_group.reshape(item_count // per_block, per_block)
    length_rows = caption_len.reshape(item_count // per_block, per_block)

    def forward(params, images, text_all):

        def block_forward(block):
            image_block, text_block, code_block, length_block = block
            return jax.vmap(lambda image_rows, text_rows, size_code, length: item_forward(params, image_rows, text_rows, size_code, length))(image_block, text_block, code_block, length_block)
        blocks = (images.reshape((item_count // per_block, per_block) + images.shape[1:]), text_all.reshape((item_count // per_block, per_block) + text_all.shape[1:]), code_rows, length_rows)
        outcome = lax.map(jax.checkpoint(block_forward), blocks)
        return outcome.reshape((item_count,) + outcome.shape[2:])
    outcome, pullback = jax.vjp(forward, params, images, text_all)
    param_grads, image_grad, text_grad = pullback(cotangent.astype(jnp.float32))
    return (outcome.astype(jnp.bfloat16), image_grad, text_grad, param_grads[0], param_grads[1], param_grads[2], param_grads[3], param_grads[4], param_grads[5], param_grads[6], param_grads[7], param_grads[8], param_grads[9], param_grads[10], param_grads[11], param_grads[12], param_grads[13], param_grads[14], param_grads[15], param_grads[16], param_grads[17], param_grads[18], param_grads[19])
```

```python
import functools
import math

import jax
import jax.numpy as jnp
from jax import lax
from jax.experimental import pallas as pl
from jax.experimental.pallas import tpu as pltpu
from jax.sharding import PartitionSpec as P

HEADS = 12
HEAD_DIM = 64
PATCH_BIG = 325
PATCH_SMALL = 197


EPSILON = 1e-06
NEGATIVE = -1e30


def matmul(left, right):
    return jnp.dot(left, right, preferred_element_type=jnp.float32)


def left_product(left, right):
    return lax.dot_general(
        left, right, (((0,), (0,)), ((), ())), preferred_element_type=jnp.float32
    )


def right_product(left, right):
    return lax.dot_general(
        left, right, (((1,), (1,)), ((), ())), preferred_element_type=jnp.float32
    )


def to_low(values):
    return values.astype(jnp.bfloat16)


def column_sum(values):
    return jnp.sum(values.astype(jnp.float32), 0)


def gelu_exact(values):
    return jax.nn.gelu(values, approximate=False)


def layer_norm(values, gain, shift):
    centered = values - jnp.mean(values, -1, keepdims=True)
    scaled = centered * lax.rsqrt(jnp.mean(centered * centered, -1, keepdims=True) + EPSILON)
    return scaled * gain + shift


def key_mask(size_code, length, row_count):
    position = jnp.arange(row_count, dtype=jnp.int32)
    patches = jnp.where(size_code == 1, PATCH_BIG, PATCH_SMALL).astype(jnp.int32)
    image_live = (position >= 1) & (position <= patches)
    text_live = (position >= 1 + PATCH_BIG) & (position < 1 + PATCH_BIG + length)
    return (position == 0) | image_live | text_live


def head_slice(source, offset, span_width, per_group):
    part = lax.dynamic_slice_in_dim(source, offset, span_width, 1)
    return part.reshape(source.shape[0], per_group, HEAD_DIM)


def attend_forward(queries, keys_all, values_all, key_live):
    row_count = queries.shape[0]
    per_group = math.gcd(HEADS, 4)
    span_width = per_group * HEAD_DIM
    factor = HEAD_DIM ** (-0.5)

    def one_group(group_index, running):
        attended, totals = running
        offset = group_index * span_width
        query_part = head_slice(queries, offset, span_width, per_group)
        key_part = head_slice(keys_all, offset, span_width, per_group)
        value_part = head_slice(values_all, offset, span_width, per_group)
        scores = (
            jnp.einsum("qhd,khd->hqk", query_part, key_part, preferred_element_type=jnp.float32)
            * factor
        )
        scores = jnp.where(key_live, scores, NEGATIVE)
        row_top = jnp.max(scores, -1, keepdims=True)
        exps = jnp.exp(scores - row_top)
        row_total = jnp.sum(exps, -1, keepdims=True)
        prob_rows = to_low(exps / row_total)
        mixed_heads = jnp.einsum(
            "hqk,khd->qhd", prob_rows, value_part, preferred_element_type=jnp.float32
        )
        attended = lax.dynamic_update_slice_in_dim(
            attended, to_low(mixed_heads.reshape(row_count, span_width)), offset, 1
        )
        log_total = (row_top + jnp.log(row_total))[:, :, 0]
        totals = lax.dynamic_update_slice_in_dim(totals, log_total, group_index * per_group, 0)
        return (attended, totals)

    initial = (
        jnp.zeros((row_count, HEADS * HEAD_DIM), jnp.bfloat16),
        jnp.zeros((HEADS, row_count), jnp.float32),
    )
    return lax.fori_loop(0, HEADS // per_group, one_group, initial)


def attend_backward(queries, keys_all, values_all, key_live, totals, incoming):
    row_count = queries.shape[0]
    per_group = math.gcd(HEADS, 4)
    span_width = per_group * HEAD_DIM
    factor = HEAD_DIM ** (-0.5)

    def one_group(group_index, running):
        query_grad, key_grad, value_grad = running
        offset = group_index * span_width
        query_part = head_slice(queries, offset, span_width, per_group)
        key_part = head_slice(keys_all, offset, span_width, per_group)
        value_part = head_slice(values_all, offset, span_width, per_group)
        incoming_part = head_slice(incoming, offset, span_width, per_group)
        log_total = lax.dynamic_slice_in_dim(totals, group_index * per_group, per_group, 0)
        scores = (
            jnp.einsum("qhd,khd->hqk", query_part, key_part, preferred_element_type=jnp.float32)
            * factor
        )
        scores = jnp.where(key_live, scores, NEGATIVE)
        prob_rows = jnp.exp(scores - log_total[:, :, None])
        value_part_grad = jnp.einsum(
            "hqk,qhd->khd", to_low(prob_rows), incoming_part, preferred_element_type=jnp.float32
        )
        prob_grad = jnp.einsum(
            "qhd,khd->hqk", incoming_part, value_part, preferred_element_type=jnp.float32
        )
        score_grad = to_low(
            prob_rows * (prob_grad - jnp.sum(prob_rows * prob_grad, -1, keepdims=True))
        )
        query_part_grad = (
            jnp.einsum("hqk,khd->qhd", score_grad, key_part, preferred_element_type=jnp.float32)
            * factor
        )
        key_part_grad = (
            jnp.einsum("hqk,qhd->khd", score_grad, query_part, preferred_element_type=jnp.float32)
            * factor
        )
        query_grad = lax.dynamic_update_slice_in_dim(
            query_grad, to_low(query_part_grad.reshape(row_count, span_width)), offset, 1
        )
        key_grad = lax.dynamic_update_slice_in_dim(
            key_grad, to_low(key_part_grad.reshape(row_count, span_width)), offset, 1
        )
        value_grad = lax.dynamic_update_slice_in_dim(
            value_grad, to_low(value_part_grad.reshape(row_count, span_width)), offset, 1
        )
        return (query_grad, key_grad, value_grad)

    empty_grad = jnp.zeros((row_count, HEADS * HEAD_DIM), jnp.bfloat16)
    return lax.fori_loop(0, HEADS // per_group, one_group, (empty_grad, empty_grad, empty_grad))


def item_forward(weights, image_rows, text_rows, size_code, length):
    (
        image_proj,
        image_bias,
        text_proj,
        text_bias,
        cls_token,
        first_gain,
        first_shift,
        query_proj,
        query_bias,
        key_proj,
        value_proj,
        value_bias,
        output_proj,
        output_bias,
        second_gain,
        second_shift,
        hidden_proj,
        hidden_bias,
        return_proj,
        return_bias,
    ) = weights
    image_part = matmul(image_rows, image_proj) + image_bias.astype(jnp.float32)
    text_part = matmul(text_rows, text_proj) + text_bias.astype(jnp.float32)
    embedded = jnp.concatenate([cls_token.astype(jnp.float32)[None, :], image_part, text_part], 0)
    normed = to_low(
        layer_norm(embedded, first_gain.astype(jnp.float32), first_shift.astype(jnp.float32))
    )
    queries = to_low(matmul(normed, query_proj) + query_bias.astype(jnp.float32))
    keys_all = to_low(matmul(normed, key_proj))
    values_all = to_low(matmul(normed, value_proj) + value_bias.astype(jnp.float32))
    key_live = key_mask(size_code, length, embedded.shape[0])
    attended, totals = attend_forward(queries, keys_all, values_all, key_live)
    middle = embedded + matmul(attended, output_proj) + output_bias.astype(jnp.float32)
    second = to_low(
        layer_norm(middle, second_gain.astype(jnp.float32), second_shift.astype(jnp.float32))
    )
    inner_pre = matmul(second, hidden_proj) + hidden_bias.astype(jnp.float32)
    activated = to_low(gelu_exact(inner_pre))
    result = middle + matmul(activated, return_proj) + return_bias.astype(jnp.float32)
    kept_rows = (
        embedded,
        normed,
        queries,
        keys_all,
        values_all,
        attended,
        totals,
        middle,
        second,
        inner_pre,
        activated,
    )
    return (to_low(result), kept_rows)


def item_backward(weights, image_rows, text_rows, size_code, length, kept_rows, out_grad):
    (
        image_proj,
        image_bias,
        text_proj,
        text_bias,
        cls_token,
        first_gain,
        first_shift,
        query_proj,
        query_bias,
        key_proj,
        value_proj,
        value_bias,
        output_proj,
        output_bias,
        second_gain,
        second_shift,
        hidden_proj,
        hidden_bias,
        return_proj,
        return_bias,
    ) = weights
    (
        embedded,
        normed,
        queries,
        keys_all,
        values_all,
        attended,
        totals,
        middle,
        second,
        inner_pre,
        activated,
    ) = kept_rows
    grad_return_proj = left_product(activated, out_grad)
    grad_return_bias = column_sum(out_grad)
    activated_grad = right_product(out_grad, return_proj)
    unused_value, gelu_pull = jax.vjp(gelu_exact, inner_pre)
    inner_grad = to_low(gelu_pull(activated_grad)[0])
    grad_hidden_proj = left_product(second, inner_grad)
    grad_hidden_bias = column_sum(inner_grad)
    second_grad = right_product(inner_grad, hidden_proj)
    unused_norm, second_pull = jax.vjp(
        layer_norm, middle, second_gain.astype(jnp.float32), second_shift.astype(jnp.float32)
    )
    middle_part, grad_second_gain, grad_second_shift = second_pull(second_grad)
    middle_grad = out_grad.astype(jnp.float32) + middle_part
    branch_grad = to_low(middle_grad)
    grad_output_proj = left_product(attended, branch_grad)
    grad_output_bias = column_sum(branch_grad)
    attended_grad = to_low(right_product(branch_grad, output_proj))
    key_live = key_mask(size_code, length, embedded.shape[0])
    query_grad, key_grad, value_grad = attend_backward(
        queries, keys_all, values_all, key_live, totals, attended_grad
    )
    grad_query_proj = left_product(normed, query_grad)
    grad_query_bias = column_sum(query_grad)
    grad_key_proj = left_product(normed, key_grad)
    grad_value_proj = left_product(normed, value_grad)
    grad_value_bias = column_sum(value_grad)
    normed_grad = (
        right_product(query_grad, query_proj)
        + right_product(key_grad, key_proj)
        + right_product(value_grad, value_proj)
    )
    unused_first, first_pull = jax.vjp(
        layer_norm, embedded, first_gain.astype(jnp.float32), first_shift.astype(jnp.float32)
    )
    embedded_part, grad_first_gain, grad_first_shift = first_pull(normed_grad)
    embedded_grad = middle_grad + embedded_part
    grad_cls_token = embedded_grad[0]
    image_low = to_low(embedded_grad[1 : 1 + PATCH_BIG])
    text_low = to_low(embedded_grad[1 + PATCH_BIG :])
    image_grad = right_product(image_low, image_proj)
    text_grad = right_product(text_low, text_proj)
    grad_image_proj = left_product(image_rows, image_low)
    grad_image_bias = column_sum(image_low)
    grad_text_proj = left_product(text_rows, text_low)
    grad_text_bias = column_sum(text_low)
    grads = (
        grad_image_proj,
        grad_image_bias,
        grad_text_proj,
        grad_text_bias,
        grad_cls_token,
        grad_first_gain,
        grad_first_shift,
        grad_query_proj,
        grad_query_bias,
        grad_key_proj,
        grad_value_proj,
        grad_value_bias,
        grad_output_proj,
        grad_output_bias,
        grad_second_gain,
        grad_second_shift,
        grad_hidden_proj,
        grad_hidden_bias,
        grad_return_proj,
        grad_return_bias,
    )
    return (image_grad, text_grad, grads)


MATRICES = (0, 2, 7, 9, 10, 12, 16, 18)
VECTORS = (1, 3, 4, 5, 6, 8, 11, 13, 14, 15, 19, 17)
LANES = 384
VEC_ROWS = 16
GATHER_CHUNKS = ((0, 2, "vec"), (7, 9, 10), (12, 16), (18,))
SCATTER_CHUNKS = ((18,), (16,), (12, 7, 9, 10), (0, 2, "vec"))
BOTH = ("fsdp", "dp")


class Place:
    def __init__(self):
        self.core = lax.axis_index("dp")
        chip = lax.axis_index("fsdp")
        self.x, self.y, self.z = chip & 1, (chip >> 1) & 1, chip >> 2

    def scalars(self):
        return jnp.stack([self.core, self.x, self.y, self.z]).astype(jnp.int32)


def swap_cores(values):
    return lax.ppermute(values, "dp", [(0, 1), (1, 0)])


def to_chip(values, mask_zero, mask_one):
    pairs = []
    for chip in range(16):
        pairs.append((chip * 2, (chip ^ mask_zero) * 2))
        pairs.append((chip * 2 + 1, (chip ^ mask_one) * 2 + 1))
    return lax.ppermute(values, BOTH, pairs)


def sub_blocks(weight_index):
    return 4 if weight_index == 16 else 1


def block_rows(shards, weight_index):
    if weight_index == "vec":
        return VEC_ROWS
    return shards[weight_index].shape[0] * sub_blocks(weight_index)


def half_of(shard, core, weight_index):
    count = sub_blocks(weight_index)
    width = count * LANES
    half = lax.dynamic_slice_in_dim(shard, core * width, width, 1)
    if count > 1:
        half = jnp.concatenate([half[:, s * LANES : (s + 1) * LANES] for s in range(count)], 0)
    return half


def assemble_kernel(layout, place_ref, s8, r8, s8p, r8p, *outs):
    core, x, y = place_ref[0], place_ref[1], place_ref[2]

    def fill(zero_s, zero_r, one_s, one_r):
        for (offset, rows, count, is_vec), out in zip(layout, outs):
            for s in range(count):
                first = slice(offset + s * rows, offset + (s + 1) * rows)
                columns = slice(s * LANES, (s + 1) * LANES)
                for z in range(4):
                    for b in range(2):
                        out[z, y, b, :, columns] = zero_s[z, b, first, :]
                        out[z, 1 - y, b, :, columns] = zero_r[z, b, first, :]
                if is_vec:
                    continue
                columns = slice((count + s) * LANES, (count + s + 1) * LANES)
                for z in range(4):
                    for b in range(2):
                        out[z, b, x, :, columns] = one_s[z, b, first, :]
                        out[z, b, 1 - x, :, columns] = one_r[z, b, first, :]

    @pl.when(core == 0)
    def _():
        fill(s8, r8, s8p, r8p)

    @pl.when(core == 1)
    def _():
        fill(s8p, r8p, s8, r8)


def assemble(place, pieces, shards, chunk):
    layout, shapes, offset = [], [], 0
    for index in chunk:
        if index == "vec":
            rows, count, columns = VEC_ROWS, 1, LANES
        else:
            rows, columns = shards[index].shape
            count = sub_blocks(index)
        layout.append((offset, rows, count, index == "vec"))
        offset += rows * count
        shapes.append(jax.ShapeDtypeStruct((4, 2, 2, rows, columns), jnp.bfloat16))
    fast = pl.BlockSpec(memory_space=pltpu.VMEM)
    return pl.pallas_call(
        functools.partial(assemble_kernel, tuple(layout)),
        out_shape=tuple(shapes),
        in_specs=[pl.BlockSpec(memory_space=pltpu.SMEM)] + [fast] * 4,
        out_specs=tuple(fast for _ in shapes),
        compiler_params=pltpu.CompilerParams(vmem_limit_bytes=48 * 2**20),
    )(place.scalars(), *pieces)


def gather_chunk(place, shards, chunk, vec):
    parts = [vec if i == "vec" else half_of(shards[i], place.core, i) for i in chunk]
    own = jnp.concatenate(parts, 0) if len(parts) > 1 else parts[0]
    others = [to_chip(own, 4 * step, 4 * step) for step in (1, 2, 3)]
    along_z = in_order([own] + others, place.z)
    beside = to_chip(along_z, 1, 2)
    mine = jnp.where(place.core == 0, place.x, place.y)
    s8 = jnp.where(mine == 0, jnp.stack([along_z, beside], 1), jnp.stack([beside, along_z], 1))
    r8 = to_chip(s8, 2, 1)
    s8p, r8p = swap_cores(s8), swap_cores(r8)
    outs = assemble(place, (s8, r8, s8p, r8p), shards, chunk)
    return {i: out.reshape(-1, out.shape[-1]) for i, out in zip(chunk, outs)}


def in_order(relative, z):
    a, b, c, d = relative
    low = z & 1
    e, f = jnp.where(low == 0, a, b), jnp.where(low == 0, b, a)
    g, h = jnp.where(low == 0, c, d), jnp.where(low == 0, d, c)
    high = (z >> 1) == 0
    return jnp.stack(
        [jnp.where(high, e, g), jnp.where(high, f, h), jnp.where(high, g, e), jnp.where(high, h, f)]
    )


def gather_fast(shards):
    place = Place()
    flat = jnp.concatenate([shards[i] for i in VECTORS])
    vec = jnp.pad(flat, (0, VEC_ROWS * LANES - flat.shape[0])).reshape(VEC_ROWS, LANES)
    whole = {}
    for chunk in GATHER_CHUNKS:
        whole.update(gather_chunk(place, shards, chunk, vec))
    vectors = whole["vec"].reshape(16, VEC_ROWS * LANES)
    at = 0
    for i in VECTORS:
        width = shards[i].shape[0]
        whole[i] = vectors[:, at : at + width].reshape(-1)
        at += width
    return tuple(whole[i] for i in range(20))


def halves(place, grad, index, shards):
    grad = to_low(grad)
    if index == "vec":
        return grad, grad
    count = sub_blocks(index)
    width = count * LANES
    made = []
    for core in (place.core, 1 - place.core):
        half = lax.dynamic_slice_in_dim(grad, core * width, width, 1)
        half = half.reshape(16, shards[index].shape[0], width)
        if count > 1:
            half = jnp.concatenate([half[:, :, s * LANES : (s + 1) * LANES] for s in range(count)], 1)
        made.append(half)
    return tuple(made)


def add_low(*values):
    total = values[0].astype(jnp.float32)
    for value in values[1:]:
        total = total + value.astype(jnp.float32)
    return to_low(total)


def pick(values, at, axis):
    return lax.dynamic_index_in_dim(values, at, axis, keepdims=False)


def scatter_chunk(place, grads, chunk, shards):
    pairs = [halves(place, grads[i], i, shards) for i in chunk]
    keep = jnp.concatenate([p[0] for p in pairs], 1) if len(pairs) > 1 else pairs[0][0]
    send = jnp.concatenate([p[1] for p in pairs], 1) if len(pairs) > 1 else pairs[0][1]
    got = swap_cores(send)
    rows = keep.shape[1]
    keep, got = (v.reshape(4, 4, rows, LANES) for v in (keep, got))
    zero = place.core == 0
    x, y = place.x, place.y
    near = [jnp.where(zero, 2 * y + s, 2 * s + x) for s in (0, 1)]
    far = [jnp.where(zero, 2 * (1 - y) + s, 2 * s + (1 - x)) for s in (0, 1)]
    sent = jnp.stack([add_low(pick(keep, q, 1), pick(got, q, 1)) for q in far], 1)
    kept = jnp.stack([add_low(pick(keep, q, 1), pick(got, q, 1)) for q in near], 1)
    got = to_chip(sent, 2, 1)
    mine = jnp.where(zero, x, y)
    sent = add_low(pick(kept, 1 - mine, 1), pick(got, 1 - mine, 1))
    kept = add_low(pick(kept, mine, 1), pick(got, mine, 1))
    got = to_chip(sent, 1, 2)
    total = add_low(kept, got)
    arrived = [to_chip(pick(total, place.z ^ s, 0), 4 * s, 4 * s) for s in (1, 2, 3)]
    final = add_low(pick(total, place.z, 0), *arrived)
    other = swap_cores(final)
    left = jnp.where(zero, final, other).astype(jnp.float32)
    right = jnp.where(zero, other, final).astype(jnp.float32)
    result, at = {}, 0
    for index in chunk:
        if index == "vec":
            result[index] = left[at : at + VEC_ROWS].reshape(-1)
            at += VEC_ROWS
            continue
        rows, count = shards[index].shape[0], sub_blocks(index)
        pieces = []
        for side in (left, right):
            for s in range(count):
                pieces.append(side[at + s * rows : at + (s + 1) * rows])
        result[index] = jnp.concatenate(pieces, 1)
        at += rows * count
    return result


def scatter_fast(grads, shards):
    place = Place()
    grads = dict(enumerate(grads))
    flat = jnp.concatenate([grads[i].reshape(16, -1) for i in VECTORS], 1)
    flat = jnp.pad(flat, ((0, 0), (0, VEC_ROWS * LANES - flat.shape[1])))
    grads["vec"] = flat.reshape(16, VEC_ROWS, LANES)
    owned = {}
    for chunk in SCATTER_CHUNKS:
        owned.update(scatter_chunk(place, grads, chunk, shards))
    at = 0
    for i in VECTORS:
        width = shards[i].shape[0]
        owned[i] = owned["vec"][at : at + width]
        at += width
    return tuple(owned[i] for i in range(20))


def gather_any(shards):
    return tuple(lax.all_gather(shard, "fsdp", axis=0, tiled=True) for shard in shards)


def scatter_any(grads):
    pieces = [lax.psum_scatter(g, "fsdp", scatter_dimension=0, tiled=True) for g in grads]
    return tuple(lax.psum(to_low(p), "dp").astype(jnp.float32) for p in pieces)


def on_device(
    chips,
    cores,
    image_states,
    text_states,
    size_group,
    caption_len,
    cotangent,
    image_proj,
    image_bias,
    text_proj,
    text_bias,
    cls_token,
    first_gain,
    first_shift,
    query_proj,
    query_bias,
    key_proj,
    value_proj,
    value_bias,
    output_proj,
    output_bias,
    second_gain,
    second_shift,
    hidden_proj,
    hidden_bias,
    return_proj,
    return_bias,
):
    shards = (
        image_proj,
        image_bias,
        text_proj,
        text_bias,
        cls_token,
        first_gain,
        first_shift,
        query_proj,
        query_bias,
        key_proj,
        value_proj,
        value_bias,
        output_proj,
        output_bias,
        second_gain,
        second_shift,
        hidden_proj,
        hidden_bias,
        return_proj,
        return_bias,
    )
    by_permutes = chips == 16 and cores == 2
    weights = gather_fast(shards) if by_permutes else gather_any(shards)
    results, summed = [], None
    for item in range(image_states.shape[0]):
        image_rows, text_rows = image_states[item], text_states[item]
        code, length = size_group[item], caption_len[item]
        result, kept_rows = item_forward(weights, image_rows, text_rows, code, length)
        image_grad, text_grad, grads = item_backward(
            weights, image_rows, text_rows, code, length, kept_rows, cotangent[item]
        )
        results.append((result, image_grad, text_grad))
        summed = grads if summed is None else jax.tree.map(jnp.add, summed, grads)
    owned = scatter_fast(summed, shards) if by_permutes else scatter_any(summed)
    return tuple(jnp.stack(parts) for parts in zip(*results)) + owned


def solution(mesh):
    placed = (
        P(("fsdp", "dp"), None, None),
        P(("fsdp", "dp"), None, None),
        P(("fsdp", "dp")),
        P(("fsdp", "dp")),
        P(("fsdp", "dp"), None, None),
        P("fsdp", None),
        P("fsdp"),
        P("fsdp", None),
        P("fsdp"),
        P("fsdp"),
        P("fsdp"),
        P("fsdp"),
        P("fsdp", None),
        P("fsdp"),
        P("fsdp", None),
        P("fsdp", None),
        P("fsdp"),
        P("fsdp", None),
        P("fsdp"),
        P("fsdp"),
        P("fsdp"),
        P("fsdp", None),
        P("fsdp"),
        P("fsdp", None),
        P("fsdp"),
    )
    chips, cores = mesh.shape["fsdp"], mesh.shape["dp"]
    return jax.shard_map(
        functools.partial(on_device, chips, cores),
        mesh=mesh,
        in_specs=placed,
        out_specs=(
            P(("fsdp", "dp"), None, None),
            P(("fsdp", "dp"), None, None),
            P(("fsdp", "dp"), None, None),
            P("fsdp", None),
            P("fsdp"),
            P("fsdp", None),
            P("fsdp"),
            P("fsdp"),
            P("fsdp"),
            P("fsdp"),
            P("fsdp", None),
            P("fsdp"),
            P("fsdp", None),
            P("fsdp", None),
            P("fsdp"),
            P("fsdp", None),
            P("fsdp"),
            P("fsdp"),
            P("fsdp"),
            P("fsdp", None),
            P("fsdp"),
            P("fsdp", None),
            P("fsdp"),
        ),
        check_vma=False,
    )
```

```python
import functools
import math

import jax
import jax.numpy as jnp
from jax import lax
from jax.experimental import pallas as pl
from jax.experimental.pallas import tpu as pltpu
from jax.sharding import PartitionSpec as P

HEADS = 12
HEAD_DIM = 64
PATCH_BIG = 325
PATCH_SMALL = 197


EPSILON = 1e-06
NEGATIVE = -1e30


def matmul(left, right):
    return jnp.dot(left, right, preferred_element_type=jnp.float32)


def left_product(left, right):
    return lax.dot_general(
        left, right, (((0,), (0,)), ((), ())), preferred_element_type=jnp.float32
    )


def right_product(left, right):
    return lax.dot_general(
        left, right, (((1,), (1,)), ((), ())), preferred_element_type=jnp.float32
    )


def to_low(values):
    return values.astype(jnp.bfloat16)


def column_sum(values):
    return jnp.sum(values.astype(jnp.float32), 0)


def gelu_exact(values):
    return jax.nn.gelu(values, approximate=False)


def layer_norm(values, gain, shift):
    centered = values - jnp.mean(values, -1, keepdims=True)
    scaled = centered * lax.rsqrt(jnp.mean(centered * centered, -1, keepdims=True) + EPSILON)
    return scaled * gain + shift


def key_mask(size_code, length, row_count):
    position = jnp.arange(row_count, dtype=jnp.int32)
    patches = jnp.where(size_code == 1, PATCH_BIG, PATCH_SMALL).astype(jnp.int32)
    image_live = (position >= 1) & (position <= patches)
    text_live = (position >= 1 + PATCH_BIG) & (position < 1 + PATCH_BIG + length)
    return (position == 0) | image_live | text_live


def head_slice(source, offset, span_width, per_group):
    part = lax.dynamic_slice_in_dim(source, offset, span_width, 1)
    return part.reshape(source.shape[0], per_group, HEAD_DIM)


def attend_forward(queries, keys_all, values_all, key_live):
    row_count = queries.shape[0]
    per_group = math.gcd(HEADS, 4)
    span_width = per_group * HEAD_DIM
    factor = HEAD_DIM ** (-0.5)

    def one_group(group_index, running):
        attended, totals = running
        offset = group_index * span_width
        query_part = head_slice(queries, offset, span_width, per_group)
        key_part = head_slice(keys_all, offset, span_width, per_group)
        value_part = head_slice(values_all, offset, span_width, per_group)
        scores = (
            jnp.einsum("qhd,khd->hqk", query_part, key_part, preferred_element_type=jnp.float32)
            * factor
        )
        scores = jnp.where(key_live, scores, NEGATIVE)
        row_top = jnp.max(scores, -1, keepdims=True)
        exps = jnp.exp(scores - row_top)
        row_total = jnp.sum(exps, -1, keepdims=True)
        prob_rows = to_low(exps / row_total)
        mixed_heads = jnp.einsum(
            "hqk,khd->qhd", prob_rows, value_part, preferred_element_type=jnp.float32
        )
        attended = lax.dynamic_update_slice_in_dim(
            attended, to_low(mixed_heads.reshape(row_count, span_width)), offset, 1
        )
        log_total = (row_top + jnp.log(row_total))[:, :, 0]
        totals = lax.dynamic_update_slice_in_dim(totals, log_total, group_index * per_group, 0)
        return (attended, totals)

    initial = (
        jnp.zeros((row_count, HEADS * HEAD_DIM), jnp.bfloat16),
        jnp.zeros((HEADS, row_count), jnp.float32),
    )
    return lax.fori_loop(0, HEADS // per_group, one_group, initial)


def attend_backward(queries, keys_all, values_all, key_live, totals, incoming):
    row_count = queries.shape[0]
    per_group = math.gcd(HEADS, 4)
    span_width = per_group * HEAD_DIM
    factor = HEAD_DIM ** (-0.5)

    def one_group(group_index, running):
        query_grad, key_grad, value_grad = running
        offset = group_index * span_width
        query_part = head_slice(queries, offset, span_width, per_group)
        key_part = head_slice(keys_all, offset, span_width, per_group)
        value_part = head_slice(values_all, offset, span_width, per_group)
        incoming_part = head_slice(incoming, offset, span_width, per_group)
        log_total = lax.dynamic_slice_in_dim(totals, group_index * per_group, per_group, 0)
        scores = (
            jnp.einsum("qhd,khd->hqk", query_part, key_part, preferred_element_type=jnp.float32)
            * factor
        )
        scores = jnp.where(key_live, scores, NEGATIVE)
        prob_rows = jnp.exp(scores - log_total[:, :, None])
        value_part_grad = jnp.einsum(
            "hqk,qhd->khd", to_low(prob_rows), incoming_part, preferred_element_type=jnp.float32
        )
        prob_grad = jnp.einsum(
            "qhd,khd->hqk", incoming_part, value_part, preferred_element_type=jnp.float32
        )
        score_grad = to_low(
            prob_rows * (prob_grad - jnp.sum(prob_rows * prob_grad, -1, keepdims=True))
        )
        query_part_grad = (
            jnp.einsum("hqk,khd->qhd", score_grad, key_part, preferred_element_type=jnp.float32)
            * factor
        )
        key_part_grad = (
            jnp.einsum("hqk,qhd->khd", score_grad, query_part, preferred_element_type=jnp.float32)
            * factor
        )
        query_grad = lax.dynamic_update_slice_in_dim(
            query_grad, to_low(query_part_grad.reshape(row_count, span_width)), offset, 1
        )
        key_grad = lax.dynamic_update_slice_in_dim(
            key_grad, to_low(key_part_grad.reshape(row_count, span_width)), offset, 1
        )
        value_grad = lax.dynamic_update_slice_in_dim(
            value_grad, to_low(value_part_grad.reshape(row_count, span_width)), offset, 1
        )
        return (query_grad, key_grad, value_grad)

    empty_grad = jnp.zeros((row_count, HEADS * HEAD_DIM), jnp.bfloat16)
    return lax.fori_loop(0, HEADS // per_group, one_group, (empty_grad, empty_grad, empty_grad))


def item_forward(weights, image_rows, text_rows, size_code, length):
    (
        image_proj,
        image_bias,
        text_proj,
        text_bias,
        cls_token,
        first_gain,
        first_shift,
        query_proj,
        query_bias,
        key_proj,
        value_proj,
        value_bias,
        output_proj,
        output_bias,
        second_gain,
        second_shift,
        hidden_proj,
        hidden_bias,
        return_proj,
        return_bias,
    ) = weights
    image_part = matmul(image_rows, image_proj) + image_bias.astype(jnp.float32)
    text_part = matmul(text_rows, text_proj) + text_bias.astype(jnp.float32)
    embedded = jnp.concatenate([cls_token.astype(jnp.float32)[None, :], image_part, text_part], 0)
    normed = to_low(
        layer_norm(embedded, first_gain.astype(jnp.float32), first_shift.astype(jnp.float32))
    )
    queries = to_low(matmul(normed, query_proj) + query_bias.astype(jnp.float32))
    keys_all = to_low(matmul(normed, key_proj))
    values_all = to_low(matmul(normed, value_proj) + value_bias.astype(jnp.float32))
    key_live = key_mask(size_code, length, embedded.shape[0])
    attended, totals = attend_forward(queries, keys_all, values_all, key_live)
    middle = embedded + matmul(attended, output_proj) + output_bias.astype(jnp.float32)
    second = to_low(
        layer_norm(middle, second_gain.astype(jnp.float32), second_shift.astype(jnp.float32))
    )
    inner_pre = matmul(second, hidden_proj) + hidden_bias.astype(jnp.float32)
    activated = to_low(gelu_exact(inner_pre))
    result = middle + matmul(activated, return_proj) + return_bias.astype(jnp.float32)
    kept_rows = (
        embedded,
        normed,
        queries,
        keys_all,
        values_all,
        attended,
        totals,
        middle,
        second,
        inner_pre,
        activated,
    )
    return (to_low(result), kept_rows)


def item_backward(weights, image_rows, text_rows, size_code, length, kept_rows, out_grad):
    (
        image_proj,
        image_bias,
        text_proj,
        text_bias,
        cls_token,
        first_gain,
        first_shift,
        query_proj,
        query_bias,
        key_proj,
        value_proj,
        value_bias,
        output_proj,
        output_bias,
        second_gain,
        second_shift,
        hidden_proj,
        hidden_bias,
        return_proj,
        return_bias,
    ) = weights
    (
        embedded,
        normed,
        queries,
        keys_all,
        values_all,
        attended,
        totals,
        middle,
        second,
        inner_pre,
        activated,
    ) = kept_rows
    grad_return_proj = left_product(activated, out_grad)
    grad_return_bias = column_sum(out_grad)
    activated_grad = right_product(out_grad, return_proj)
    unused_value, gelu_pull = jax.vjp(gelu_exact, inner_pre)
    inner_grad = to_low(gelu_pull(activated_grad)[0])
    grad_hidden_proj = left_product(second, inner_grad)
    grad_hidden_bias = column_sum(inner_grad)
    second_grad = right_product(inner_grad, hidden_proj)
    unused_norm, second_pull = jax.vjp(
        layer_norm, middle, second_gain.astype(jnp.float32), second_shift.astype(jnp.float32)
    )
    middle_part, grad_second_gain, grad_second_shift = second_pull(second_grad)
    middle_grad = out_grad.astype(jnp.float32) + middle_part
    branch_grad = to_low(middle_grad)
    grad_output_proj = left_product(attended, branch_grad)
    grad_output_bias = column_sum(branch_grad)
    attended_grad = to_low(right_product(branch_grad, output_proj))
    key_live = key_mask(size_code, length, embedded.shape[0])
    query_grad, key_grad, value_grad = attend_backward(
        queries, keys_all, values_all, key_live, totals, attended_grad
    )
    grad_query_proj = left_product(normed, query_grad)
    grad_query_bias = column_sum(query_grad)
    grad_key_proj = left_product(normed, key_grad)
    grad_value_proj = left_product(normed, value_grad)
    grad_value_bias = column_sum(value_grad)
    normed_grad = (
        right_product(query_grad, query_proj)
        + right_product(key_grad, key_proj)
        + right_product(value_grad, value_proj)
    )
    unused_first, first_pull = jax.vjp(
        layer_norm, embedded, first_gain.astype(jnp.float32), first_shift.astype(jnp.float32)
    )
    embedded_part, grad_first_gain, grad_first_shift = first_pull(normed_grad)
    embedded_grad = middle_grad + embedded_part
    grad_cls_token = embedded_grad[0]
    image_low = to_low(embedded_grad[1 : 1 + PATCH_BIG])
    text_low = to_low(embedded_grad[1 + PATCH_BIG :])
    image_grad = right_product(image_low, image_proj)
    text_grad = right_product(text_low, text_proj)
    grad_image_proj = left_product(image_rows, image_low)
    grad_image_bias = column_sum(image_low)
    grad_text_proj = left_product(text_rows, text_low)
    grad_text_bias = column_sum(text_low)
    grads = (
        grad_image_proj,
        grad_image_bias,
        grad_text_proj,
        grad_text_bias,
        grad_cls_token,
        grad_first_gain,
        grad_first_shift,
        grad_query_proj,
        grad_query_bias,
        grad_key_proj,
        grad_value_proj,
        grad_value_bias,
        grad_output_proj,
        grad_output_bias,
        grad_second_gain,
        grad_second_shift,
        grad_hidden_proj,
        grad_hidden_bias,
        grad_return_proj,
        grad_return_bias,
    )
    return (image_grad, text_grad, grads)


VECTORS = (1, 3, 4, 5, 6, 8, 11, 13, 14, 15, 19, 17)
LANES = 384
VEC_ROWS = 16
GATHER_CHUNKS = ((0, 2, "vec"), (7, 9, 10), (12, 16, 18))
SCATTER_CHUNKS = ((18, 16), (12, 7, 9, 10), (0, 2, "vec"))
BOTH = ("fsdp", "dp")
WIDTH = 768
HIDDEN = 3072
IMAGE = 325
TEXTS = 513
ROWS = 839
KEYS = 848
PADDED = 896
LOW = jnp.bfloat16
FULL = jnp.float32
COST_SCALE = 0.3
FAST = pl.BlockSpec(memory_space=pltpu.VMEM)
SCALARS = pl.BlockSpec(memory_space=pltpu.SMEM)


def cost(micros):
    return pl.CostEstimate(
        flops=int(micros * COST_SCALE * 1e9), bytes_accessed=1024, transcendentals=0
    )


class Place:
    def __init__(self):
        self.core = lax.axis_index("dp")
        chip = lax.axis_index("fsdp")
        self.x, self.y, self.z = chip & 1, (chip >> 1) & 1, chip >> 2
        self.scalars = jnp.stack([self.core, self.x, self.y, self.z]).astype(jnp.int32)


def shape(dims, kind=LOW):
    return jax.ShapeDtypeStruct(dims, kind)


def call(kernel, micros, outs, *args, scratch=(), limit=60):
    specs = [SCALARS if a.dtype == jnp.int32 else FAST for a in args]
    return pl.pallas_call(
        kernel,
        out_shape=tuple(outs),
        in_specs=specs,
        out_specs=tuple(FAST for _ in outs),
        scratch_shapes=list(scratch),
        compiler_params=pltpu.CompilerParams(vmem_limit_bytes=limit * 2**20),
        cost_estimate=cost(micros),
    )(*args)


def after(values, *others):
    return lax.optimization_barrier((values, others))[0]


def settle(*values):
    return lax.optimization_barrier(values)


def swap_cores(values):
    with jax.named_scope("between_cores"):
        return lax.ppermute(values, "dp", [(0, 1), (1, 0)])


def to_chip(values, mask_zero, mask_one):
    pairs = []
    for chip in range(16):
        pairs.append((chip * 2, (chip ^ mask_zero) * 2))
        pairs.append((chip * 2 + 1, (chip ^ mask_one) * 2 + 1))
    with jax.named_scope(f"chips_{mask_zero}_{mask_one}"):
        return lax.ppermute(values, BOTH, pairs)


def sub_blocks(index):
    return 4 if index == 16 else 1


def block_rows(index):
    return {"vec": VEC_ROWS, 16: 192, 18: 192}.get(index, 48)


def layout_of(chunk):
    made, offset = {}, 0
    for index in chunk:
        made[index] = offset
        offset += block_rows(index)
    return made, offset


def pack_kernel(chunk, at_ref, *refs):
    core = at_ref[0]
    out, ins = refs[len(chunk) if "vec" not in chunk else len(chunk) - 1 + 12], refs
    offset = 0
    for place, index in enumerate(chunk):
        if index == "vec":
            rows = refs[-1]
            rows[...] = jnp.zeros_like(rows)
            for row in range(12):
                source = ins[place + row]
                rows[row : row + 1, 0 : source.shape[1]] = source[...].astype(FULL)
            out[offset : offset + VEC_ROWS, :] = rows[...].astype(LOW)
            continue
        count = sub_blocks(index)
        rows = ins[place].shape[0]
        for s in range(count):
            first = pl.multiple_of((core * count + s) * LANES, LANES)
            out[offset : offset + rows, :] = ins[place][:, pl.ds(first, LANES)]
            offset += rows


def pack(place, shards, chunk):
    rows = sum(block_rows(i) for i in chunk)
    ins = [shards[i] for i in chunk if i != "vec"]
    scratch = ()
    if "vec" in chunk:
        ins += [shards[i].reshape(1, -1) for i in VECTORS]
        scratch = (pltpu.VMEM((VEC_ROWS, LANES), FULL),)
    kernel = functools.partial(pack_kernel, chunk)
    return call(kernel, 1, [shape((rows, LANES))], place.scalars, *ins, scratch=scratch)[0]


def all_z(own):
    return [own] + [to_chip(own, 4 * s, 4 * s) for s in (1, 2, 3)]


def unpack(at_ref, pieces, targets):
    core, x, y, z = at_ref[0], at_ref[1], at_ref[2], at_ref[3]

    def fill(zero_s, zero_r, one_s, one_r):
        for offset, count, is_vec, out in targets:
            rows = out.shape[3]
            for s in range(count):
                first = slice(offset + s * rows, offset + (s + 1) * rows)
                left = slice(s * LANES, (s + 1) * LANES)
                right = slice((count + s) * LANES, (count + s + 1) * LANES)
                for far in range(4):
                    plane = z ^ far
                    for b in range(2):
                        out[plane, y, x ^ b, :, left] = zero_s[b, far, first, :]
                        out[plane, 1 - y, x ^ b, :, left] = zero_r[b, far, first, :]
                        if not is_vec:
                            out[plane, y ^ b, x, :, right] = one_s[b, far, first, :]
                            out[plane, y ^ b, 1 - x, :, right] = one_r[b, far, first, :]

    s8, r8, s8p, r8p = pieces

    @pl.when(core == 0)
    def _():
        fill(s8, r8, s8p, r8p)

    @pl.when(core == 1)
    def _():
        fill(s8p, r8p, s8, r8)


def square(ref):
    return ref[...].reshape(16 * ref.shape[3], ref.shape[4])


def row_chunks(step, total=ROWS):
    return [slice(a, min(a + step, total)) for a in range(0, total, step)]


def standard(values):
    centered = values - jnp.mean(values, -1, keepdims=True)
    scale = lax.rsqrt(jnp.mean(centered * centered, -1, keepdims=True) + EPSILON)
    return centered * scale, scale


def norm_back(values, gain, incoming):
    unit, scale = standard(values)
    f = incoming * gain
    back = (f - jnp.mean(f, -1, keepdims=True) - unit * jnp.mean(f * unit, -1, keepdims=True)) * scale
    return back, unit


def sum_rows(values):
    return jnp.sum(values.astype(FULL), 0, keepdims=True)


def embed_kernel(at, image, text, s8, r8, s8p, r8p, w_image, w_text, vec, hid, embedded, normed, small):
    unpack(
        at,
        (s8, r8, s8p, r8p),
        ((0, 1, False, w_image), (48, 1, False, w_text), (96, 1, True, small)),
    )
    for f in range(16):
        piece = small[f >> 2, (f >> 1) & 1, f & 1].astype(FULL)
        vec[:, f * 48 : (f + 1) * 48] = piece[:, :48]
        hid[:, f * 192 : (f + 1) * 192] = piece[11:12, :192]
    embedded[0:1, :] = vec[2:3, :]
    embedded[1 : 1 + IMAGE, :] = matmul(image[...], square(w_image)) + vec[0:1, :]
    embedded[1 + IMAGE : ROWS, :] = matmul(text[...], square(w_text)) + vec[1:2, :]
    for rows in row_chunks(64):
        unit, unused_scale = standard(embedded[rows, :])
        normed[rows, :] = to_low(unit * vec[3:4, :] + vec[4:5, :])


def embed(place, image, text, pieces):
    block = (4, 2, 2, 48, WIDTH)
    outs = [
        shape(block),
        shape(block),
        shape((VEC_ROWS, WIDTH), FULL),
        shape((1, HIDDEN), FULL),
        shape((ROWS, WIDTH), FULL),
        shape((ROWS, WIDTH)),
    ]
    scratch = (pltpu.VMEM((4, 2, 2, VEC_ROWS, LANES), LOW),)
    return call(embed_kernel, 5.5, outs, place.scalars, image, text, *pieces, scratch=scratch)


def qkv_kernel(at, normed, vec, s8, r8, s8p, r8p, wq, wk, wv, q, k, v):
    unpack(
        at,
        (s8, r8, s8p, r8p),
        ((0, 1, False, wq), (48, 1, False, wk), (96, 1, False, wv)),
    )
    rows = normed[...]
    for out in (q, k, v):
        out[832:PADDED, :] = jnp.zeros((PADDED - 832, WIDTH), LOW)
    low = to_low(matmul(rows, square(wq)) + vec[5:6, :])
    q[0:ROWS, :] = to_low(low.astype(FULL) * HEAD_DIM**-0.5)
    k[0:ROWS, :] = to_low(matmul(rows, square(wk)))
    v[0:ROWS, :] = to_low(matmul(rows, square(wv)) + vec[6:7, :])


def qkv(place, normed, vec, pieces):
    outs = [shape((4, 2, 2, 48, WIDTH))] * 3 + [shape((PADDED, WIDTH))] * 3
    return call(qkv_kernel, 7, outs, place.scalars, normed, vec, *pieces)


def mask_column(live):
    position = lax.broadcasted_iota(jnp.int32, (KEYS, 1), 0)
    patches = jnp.where(live[0] == 1, PATCH_BIG, PATCH_SMALL).astype(jnp.int32)
    image_live = (position >= 1) & (position <= patches)
    text_live = (position >= 1 + PATCH_BIG) & (position < 1 + PATCH_BIG + live[1])
    return jnp.where((position == 0) | image_live | text_live, 0.0, NEGATIVE).astype(FULL)


QUERY_CHUNKS = ((0, 256), (256, 256), (512, 256), (768, 128))


def one_head(ref_value, head):
    lane = lax.broadcasted_iota(jnp.int32, ref_value.shape, 1)
    keep = (lane < HEAD_DIM) if head == 0 else (lane >= HEAD_DIM)
    return jnp.where(keep, ref_value, jnp.zeros_like(ref_value))


def attend_kernel(live, q, k, v, attended, totals):
    bias = mask_column(live)
    keys = [one_head(k[0:KEYS, :], h) for h in range(2)]
    values_t = jnp.transpose(v[0:KEYS, :].astype(FULL)).astype(LOW)
    totals[...] = jnp.zeros_like(totals)
    for start, width in QUERY_CHUNKS:
        part = q[start : start + width, :]
        mixed = []
        for h in range(2):
            scores = right_product(keys[h], part) + bias
            top = jnp.max(scores, 0, keepdims=True)
            exps = jnp.exp(scores - top)
            total = jnp.sum(exps, 0, keepdims=True)
            out = matmul(values_t[h * HEAD_DIM : (h + 1) * HEAD_DIM, :], to_low(exps))
            mixed.append(out * (1.0 / total))
            totals[0, h : h + 1, start : start + width] = top + jnp.log(total)
        attended[start : start + width, :] = to_low(jnp.transpose(jnp.concatenate(mixed, 0)))


def attend(live, q, k, v, first, count, earlier=()):
    spec = pl.BlockSpec((PADDED, 2 * HEAD_DIM), lambda i: (0, i + first))
    anywhere = pl.BlockSpec(memory_space=pl.ANY)

    def kernel(live, q, k, v, *refs):
        attend_kernel(live, q, k, v, *refs[-2:])

    return pl.pallas_call(
        kernel,
        grid=(count,),
        out_shape=(shape((PADDED, WIDTH)), shape((HEADS // 2, 8, PADDED), FULL)),
        in_specs=[SCALARS] + [spec] * 3 + [anywhere] * len(earlier),
        out_specs=(spec, pl.BlockSpec((1, 8, PADDED), lambda i: (i + first, 0, 0))),
        input_output_aliases={4 + n: n for n in range(len(earlier))},
        compiler_params=pltpu.CompilerParams(vmem_limit_bytes=32 * 2**20),
        cost_estimate=cost(5 * count),
    )(live, q, k, v, *earlier)


def attend_back_kernel(live, q, k, v, incoming, totals, q_grad, k_grad, v_grad):
    bias = mask_column(live)
    keys = [one_head(k[0:KEYS, :], h) for h in range(2)]
    values = [one_head(v[0:KEYS, :], h) for h in range(2)]
    keys_t = jnp.transpose(k[0:KEYS, :].astype(FULL)).astype(LOW)
    k_sum, v_sum = [None, None], [None, None]
    for start, width in QUERY_CHUNKS:
        part = q[start : start + width, :]
        grad = incoming[start : start + width, :]
        mixed = []
        for h in range(2):
            scores = right_product(keys[h], part) + bias
            probs = jnp.exp(scores - totals[0, h : h + 1, start : start + width])
            prob_grad = right_product(values[h], grad)
            along = jnp.sum(probs * prob_grad, 0, keepdims=True)
            score_grad = to_low(probs * (prob_grad - along))
            v_part = matmul(to_low(probs), grad)
            k_part = matmul(score_grad, part)
            v_sum[h] = v_part if v_sum[h] is None else v_sum[h] + v_part
            k_sum[h] = k_part if k_sum[h] is None else k_sum[h] + k_part
            mixed.append(matmul(keys_t[h * HEAD_DIM : (h + 1) * HEAD_DIM, :], score_grad))
        back = jnp.transpose(jnp.concatenate(mixed, 0)) * HEAD_DIM**-0.5
        q_grad[start : start + width, :] = to_low(back)
    lane = lax.broadcasted_iota(jnp.int32, (KEYS, 2 * HEAD_DIM), 1) < HEAD_DIM
    k_grad[0:KEYS, :] = to_low(jnp.where(lane, k_sum[0], k_sum[1]))
    v_grad[0:KEYS, :] = to_low(jnp.where(lane, v_sum[0], v_sum[1]))


def attend_back(live, q, k, v, incoming, totals, first, count, earlier=()):
    spec = pl.BlockSpec((PADDED, 2 * HEAD_DIM), lambda i: (0, i + first))
    anywhere = pl.BlockSpec(memory_space=pl.ANY)

    def kernel(live, q, k, v, incoming, totals, *refs):
        attend_back_kernel(live, q, k, v, incoming, totals, *refs[-3:])

    return pl.pallas_call(
        kernel,
        grid=(count,),
        out_shape=(shape((PADDED, WIDTH)),) * 3,
        in_specs=[SCALARS]
        + [spec] * 4
        + [pl.BlockSpec((1, 8, PADDED), lambda i: (i + first, 0, 0))]
        + [anywhere] * len(earlier),
        out_specs=(spec,) * 3,
        input_output_aliases={6 + n: n for n in range(len(earlier))},
        compiler_params=pltpu.CompilerParams(vmem_limit_bytes=32 * 2**20),
        cost_estimate=cost(6.5 * count),
    )(live, q, k, v, incoming, totals, *earlier)


def middle_kernel(at, attended, embedded, vec, s8, r8, s8p, r8p, w_out, w_hid, middle, second):
    unpack(at, (s8, r8, s8p, r8p), ((0, 1, False, w_out), (48, 4, False, w_hid)))
    middle[...] = embedded[...] + matmul(attended[0:ROWS, :], square(w_out)) + vec[7:8, :]
    for rows in row_chunks(64):
        unit, unused_scale = standard(middle[rows, :])
        second[rows, :] = to_low(unit * vec[8:9, :] + vec[9:10, :])


def middle_of(place, attended, embedded, vec, pieces):
    outs = [
        shape((4, 2, 2, 48, WIDTH)),
        shape((4, 2, 2, 48, HIDDEN)),
        shape((ROWS, WIDTH), FULL),
        shape((ROWS, WIDTH)),
    ]
    return call(middle_kernel, 8, outs, place.scalars, attended, embedded, vec, *pieces)


def gelu_parts(u):
    cumulative = 0.5 * (1.0 + lax.erf(u * (2.0**-0.5)))
    slope = cumulative + u * (jnp.exp(-0.5 * u * u) * (2.0 * math.pi) ** -0.5)
    return u * cumulative, slope


def feed_kernel(
    at, second, cot, middle, vec, w_hid, hid, s8, r8, s8p, r8p,
    layer_out, second_grad, ret_keep, ret_send, hid_keep, hid_send, hid_sum, ret_sum,
    w_ret, act, inner, total,
):
    step = pl.program_id(0)
    core, x, y = at[0], at[1], at[2]

    def fill(zero_s, zero_r, one_s, one_r):
        for b in range(2):
            w_ret[y, x ^ b, :, 0:LANES] = zero_s[b, 0]
            w_ret[1 - y, x ^ b, :, 0:LANES] = zero_r[b, 0]
            w_ret[y ^ b, x, :, LANES:] = one_s[b, 0]
            w_ret[y ^ b, 1 - x, :, LANES:] = one_r[b, 0]

    @pl.when(core == 0)
    def _():
        fill(s8, r8, s8p, r8p)

    @pl.when(core == 1)
    def _():
        fill(s8p, r8p, s8, r8)

    ret = w_ret[...].reshape(WIDTH, WIDTH)
    inward = w_hid[...]
    for rows in row_chunks(432):
        pre = matmul(second[rows, :], inward) + hid[...]
        back = right_product(cot[rows, :], ret)
        value, slope = gelu_parts(pre)
        act[rows, :] = to_low(value)
        inner[rows, :] = to_low(back * slope)
        out = matmul(act[rows, :], ret)
        back = right_product(inner[rows, :], inward)

        @pl.when(step == 0)
        def _():
            total[rows, :] = out
            second_grad[rows, :] = back

        @pl.when(step > 0)
        def _():
            total[rows, :] += out
            second_grad[rows, :] += back

    hid_sum[...] = sum_rows(inner[...])
    ret_grad = to_low(left_product(act[...], cot[...])).reshape(4, 192, WIDTH)
    hid_grad = to_low(left_product(second[...], inner[...])).reshape(16, 48, WIDTH)

    @pl.when(core == 0)
    def _():
        ret_keep[...] = ret_grad[:, :, 0:LANES]
        ret_send[...] = ret_grad[:, :, LANES:]

    @pl.when(core == 1)
    def _():
        ret_keep[...] = ret_grad[:, :, LANES:]
        ret_send[...] = ret_grad[:, :, 0:LANES]

    @pl.when(step < 2)
    def _():
        hid_send[:, 0:48, :] = hid_grad[:, :, 0:LANES]
        hid_send[:, 48:96, :] = hid_grad[:, :, LANES:]

    @pl.when(step >= 2)
    def _():
        hid_keep[:, 0:48, :] = hid_grad[:, :, 0:LANES]
        hid_keep[:, 48:96, :] = hid_grad[:, :, LANES:]

    @pl.when(step == 3)
    def _():
        layer_out[...] = to_low(middle[...] + total[...] + vec[10:11, :])
        ret_sum[...] = sum_rows(cot[...])


def feed(place, second, cot, middle, vec, w_hid, hid, pieces):
    def column(i, at):
        half = jnp.where(i < 2, 1 - at[0], at[0])
        return 2 * half + lax.rem(i, 2)

    def whole(dims):
        return pl.BlockSpec(dims, lambda i, at: (0,) * len(dims))

    piece = pl.BlockSpec((2, 1, 192, LANES), lambda i, at: (0, column(i, at) ^ at[3], 0, 0))
    ret_spec = pl.BlockSpec((4, 192, LANES), lambda i, at: (column(i, at), 0, 0))
    outs = (
        shape((ROWS, WIDTH)),
        shape((ROWS, WIDTH), FULL),
        shape((16, 192, LANES)),
        shape((16, 192, LANES)),
        shape((16, 192, LANES)),
        shape((16, 192, LANES)),
        shape((1, HIDDEN), FULL),
        shape((1, WIDTH), FULL),
    )
    grid = pltpu.PrefetchScalarGridSpec(
        num_scalar_prefetch=1,
        grid=(4,),
        in_specs=[
            whole((ROWS, WIDTH)),
            whole((ROWS, WIDTH)),
            whole((ROWS, WIDTH)),
            whole((VEC_ROWS, WIDTH)),
            pl.BlockSpec((WIDTH, WIDTH), lambda i, at: (0, column(i, at))),
            pl.BlockSpec((1, WIDTH), lambda i, at: (0, column(i, at))),
            piece,
            piece,
            piece,
            piece,
        ],
        out_specs=(
            whole((ROWS, WIDTH)),
            whole((ROWS, WIDTH)),
            ret_spec,
            ret_spec,
            pl.BlockSpec((16, 96, LANES), lambda i, at: (0, jnp.maximum(i - 2, 0), 0)),
            pl.BlockSpec((16, 96, LANES), lambda i, at: (0, jnp.minimum(i, 1), 0)),
            pl.BlockSpec((1, WIDTH), lambda i, at: (0, column(i, at))),
            whole((1, WIDTH)),
        ),
        scratch_shapes=[
            pltpu.VMEM((2, 2, 192, WIDTH), LOW),
            pltpu.VMEM((ROWS, WIDTH), LOW),
            pltpu.VMEM((ROWS, WIDTH), LOW),
            pltpu.VMEM((ROWS, WIDTH), FULL),
        ],
    )
    return pl.pallas_call(
        feed_kernel,
        grid_spec=grid,
        out_shape=outs,
        compiler_params=pltpu.CompilerParams(vmem_limit_bytes=56 * 2**20),
        cost_estimate=cost(40),
    )(place.scalars, second, cot, middle, vec, w_hid, hid, *pieces)


def branch_kernel(middle, second_grad, cot, vec, w_out, middle_grad, branch, incoming, sums):
    parts = [jnp.zeros((1, WIDTH), FULL)] * 3
    for rows in row_chunks(64):
        e = second_grad[rows, :]
        back, unit = norm_back(middle[rows, :], vec[8:9, :], e)
        grad = cot[rows, :].astype(FULL) + back
        middle_grad[rows, :] = grad
        branch[rows, :] = to_low(grad)
        for n, term in enumerate((e * unit, e, to_low(grad))):
            parts[n] = parts[n] + sum_rows(term)
    for n in range(3):
        sums[n : n + 1, :] = parts[n]
    incoming[832:PADDED, :] = jnp.zeros((PADDED - 832, WIDTH), LOW)
    incoming[0:ROWS, :] = to_low(right_product(branch[...], square(w_out)))


def branch_of(middle, second_grad, cot, vec, w_out):
    outs = [
        shape((ROWS, WIDTH), FULL),
        shape((ROWS, WIDTH)),
        shape((PADDED, WIDTH)),
        shape((8, WIDTH), FULL),
    ]
    return call(branch_kernel, 8, outs, middle, second_grad, cot, vec, w_out)


def both_halves(core, left, right_ref, first, keep, send, offset, rows):
    for half, out in ((core, keep), (1 - core, send)):
        columns = pl.ds(pl.multiple_of(half * LANES, LANES), LANES)
        grad = left_product(left, right_ref[first, columns])
        out[:, offset : offset + 48, :] = to_low(grad).reshape(16, 48, LANES)


def square_grads_kernel(at, attended, branch, normed, dq, dk, dv, keep, send):
    rows = slice(0, ROWS)
    both_halves(at[0], attended[rows, :], branch, rows, keep, send, 0, 48)
    left = normed[...]
    for n, ref in enumerate((dq, dk, dv)):
        both_halves(at[0], left, ref, rows, keep, send, 48 * (n + 1), 48)


def square_grads(place, attended, branch, normed, grads):
    outs = [shape((16, 192, LANES))] * 2
    return call(
        square_grads_kernel, 11, outs, place.scalars, attended, branch, normed, *grads
    )


def norm_one_kernel(
    dq, dk, dv, wq, wk, wv, embedded, middle_grad, vec, image_low, text_low, late, grad
):
    rows = slice(0, ROWS)
    grad[...] = (
        right_product(dq[rows, :], square(wq))
        + right_product(dk[rows, :], square(wk))
        + right_product(dv[rows, :], square(wv))
    )
    parts = [jnp.zeros((1, WIDTH), FULL)] * 4
    for piece in row_chunks(64):
        e = grad[piece, :]
        back, unit = norm_back(embedded[piece, :], vec[3:4, :], e)
        for n, term in enumerate((e * unit, e, dq[piece, :], dv[piece, :])):
            parts[n] = parts[n] + sum_rows(term)
        grad[piece, :] = middle_grad[piece, :] + back
    image_low[...] = to_low(grad[1 : 1 + IMAGE, :])
    text_low[...] = to_low(grad[1 + IMAGE : ROWS, :])
    late[...] = jnp.zeros_like(late)
    late[0:1, :] = grad[0:1, :]
    for n in range(4):
        late[n + 1 : n + 2, :] = parts[n]


def norm_one(grads, projs, embedded, middle_grad, vec):
    outs = [shape((IMAGE, WIDTH)), shape((TEXTS, WIDTH)), shape((8, WIDTH), FULL)]
    scratch = (pltpu.VMEM((ROWS, WIDTH), FULL),)
    return call(
        norm_one_kernel, 11, outs, *grads, *projs, embedded, middle_grad, vec, scratch=scratch
    )


def last_kernel(
    at, image, text, image_low, text_low, sums, hid_sum, ret_sum, late,
    keep, send, rows16, packed,
):
    both_halves(at[0], image[...], image_low, slice(0, IMAGE), keep, send, 0, 48)
    both_halves(at[0], text[...], text_low, slice(0, TEXTS), keep, send, 48, 48)
    rows16[...] = jnp.zeros_like(rows16)
    found = (
        sum_rows(image_low[...]), sum_rows(text_low[...]), late[0:1, :], late[1:2, :], late[2:3, :],
        late[3:4, :], late[4:5, :], sums[2:3, :], sums[0:1, :], sums[1:2, :], ret_sum[...],
    )
    for n, value in enumerate(found):
        rows16[n : n + 1, :] = value
    packed[...] = jnp.zeros_like(packed)
    for f in range(16):
        packed[f, :, 0:48] = rows16[:, f * 48 : (f + 1) * 48]
        packed[f, 11:12, 0:192] = hid_sum[:, f * 192 : (f + 1) * 192]
    low = to_low(packed[...])
    keep[:, 96:112, :] = low
    send[:, 96:112, :] = low


def last(place, image, text, image_low, text_low, sums, hid_sum, ret_sum, late):
    outs = [shape((16, 112, LANES)), shape((16, 112, LANES))]
    scratch = (pltpu.VMEM((VEC_ROWS, WIDTH), FULL), pltpu.VMEM((16, VEC_ROWS, LANES), FULL))
    return call(
        last_kernel, 5.5, outs, place.scalars, image, text, image_low, text_low, sums, hid_sum, ret_sum,
        late, scratch=scratch,
    )


def inputs_kernel(image_low, text_low, w_image, w_text, image_grad, text_grad):
    image_grad[...] = right_product(image_low[...], square(w_image))
    text_grad[...] = right_product(text_low[...], square(w_text))


def input_grads(image_low, text_low, w_image, w_text):
    outs = [shape((IMAGE, WIDTH), FULL), shape((TEXTS, WIDTH), FULL)]
    return call(inputs_kernel, 4.4, outs, image_low, text_low, w_image, w_text)


def add_low(*values):
    total = values[0].astype(FULL)
    for value in values[1:]:
        total = total + value.astype(FULL)
    return to_low(total)


def pick(values, at, axis):
    return lax.dynamic_index_in_dim(values, at, axis, keepdims=False)


class Scatter:
    def __init__(self, place, pairs):
        self.place = place
        self.kept = [keep for keep, unused_send in pairs]
        self.sent = [send for unused_keep, send in pairs]
        self.got = None

    def state(self):
        return self.kept, self.got

    def first(self):
        zero, x, y = self.place.core == 0, self.place.x, self.place.y
        near = [jnp.where(zero, 2 * y + s, 2 * s + x) for s in (0, 1)]
        far = [jnp.where(zero, 2 * (1 - y) + s, 2 * s + (1 - x)) for s in (0, 1)]

        def summed(places):
            parts = []
            for keep, more in zip(self.kept, self.got):
                keep, more = (v.reshape(4, 4, v.shape[1], LANES) for v in (keep, more))
                added = [add_low(pick(keep, q, 1), pick(more, q, 1)) for q in places]
                parts.append(jnp.stack(added, 1))
            return jnp.concatenate(parts, 2) if len(parts) > 1 else parts[0]

        self.sent, self.kept = summed(far), summed(near)

    def second(self):
        mine = jnp.where(self.place.core == 0, self.place.x, self.place.y)
        kept, got = self.kept, self.got
        self.sent = add_low(pick(kept, 1 - mine, 1), pick(got, 1 - mine, 1))
        self.kept = add_low(pick(kept, mine, 1), pick(got, mine, 1))

    def third(self):
        z = self.place.z
        total = add_low(self.kept, self.got)
        self.kept = pick(total, z, 0)
        self.sent = [pick(total, z ^ s, 0) for s in (1, 2, 3)]

    def fourth(self):
        self.sent = self.kept = add_low(self.kept, *self.got)

    def swap(self):
        self.got = jax.tree.map(swap_cores, self.sent)

    def send_first(self):
        self.got = to_chip(self.sent, 2, 1)

    def send_second(self):
        self.got = to_chip(self.sent, 1, 2)

    def send_third(self):
        self.got = [to_chip(part, 4 * s, 4 * s) for s, part in zip((1, 2, 3), self.sent)]

    def sides(self):
        zero = self.place.core == 0
        mine, other = self.kept, self.got
        return jnp.where(zero, mine, other).astype(FULL), jnp.where(zero, other, mine).astype(FULL)


def owned_rows(chunk, left, right):
    result, at = {}, 0
    for index in chunk:
        rows = block_rows(index)
        if index == "vec":
            for n, vector in enumerate(VECTORS):
                result[vector] = left[at + n, : 192 if vector == 17 else 48]
        else:
            count = sub_blocks(index)
            step = rows // count
            sides = [
                side[at + s * step : at + (s + 1) * step] for side in (left, right) for s in range(count)
            ]
            result[index] = jnp.concatenate(sides, 1)
        at += rows
    return result


def by_kernels(shards, image, text, size_code, length, cot):
    place = Place()
    live = jnp.concatenate([size_code, length]).astype(jnp.int32)
    own_one = pack(place, shards, GATHER_CHUNKS[0])

    z_one = all_z(own_one)
    own_two, own_rest = (pack(place, shards, chunk) for chunk in GATHER_CHUNKS[1:])
    z_one, own_two, own_rest = settle(z_one, own_two, own_rest)

    z_one = jnp.stack(z_one)
    owns = [own_rest[n * 144 : (n + 1) * 144] for n in range(3)]
    b_one, z_two = to_chip(z_one, 1, 2), all_z(own_two)
    b_one, z_two, z_one, owns = settle(b_one, z_two, z_one, owns)

    s_one, z_two = jnp.stack([z_one, b_one]), jnp.stack(z_two)
    r_one, sp_one, z_a = to_chip(s_one, 2, 1), swap_cores(s_one), all_z(owns[0])
    r_one, sp_one, s_one, z_a, z_two = settle(r_one, sp_one, s_one, z_a, z_two)

    b_two, z_b, rp_one = to_chip(z_two, 1, 2), all_z(owns[1]), swap_cores(r_one)
    w_image, w_text, vec, hid, embedded, normed = embed(
        place, image, text, (s_one, r_one, sp_one, rp_one)
    )
    b_two, z_b, z_two, normed = settle(b_two, z_b, z_two, normed)

    s_two = jnp.stack([z_two, b_two])
    r_two, sp_two, z_c = to_chip(s_two, 2, 1), swap_cores(s_two), all_z(owns[2])
    z_ab = [jnp.concatenate(pair, 0) for pair in zip(z_a, z_b)]
    r_two, sp_two, z_c, s_two, z_ab = settle(r_two, sp_two, z_c, s_two, z_ab)

    z_rest = jnp.stack([jnp.concatenate(pair, 0) for pair in zip(z_ab, z_c)])
    b_rest, rp_two = to_chip(z_rest, 1, 2), swap_cores(r_two)
    wq, wk, wv, q, k, v = qkv(place, after(normed, z_rest), vec, (s_two, r_two, sp_two, rp_two))
    both = attend(live, q, k, v, 0, 2)
    b_rest, z_rest, both = settle(b_rest, z_rest, both)

    s_three = jnp.stack([z_rest[:, :240], b_rest[:, :240]])
    s_four = jnp.stack([z_rest[:, 240:], b_rest[:, 240:]])
    r_three, r_four = to_chip(s_three, 2, 1), to_chip(s_four, 2, 1)
    sp_three, sp_four = swap_cores(s_three), swap_cores(s_four)
    both = attend(live, after(q, s_three, s_four), k, v, 2, 2, both)
    attended, totals = attend(live, q, k, v, 4, 2, both)
    r_three, r_four, sp_three, sp_four, attended = settle(
        r_three, r_four, sp_three, sp_four, attended
    )

    rp_three, rp_four = swap_cores(r_three), swap_cores(r_four)
    w_out, w_hid, middle, second = middle_of(
        place, attended, embedded, vec, (s_three, r_three, sp_three, rp_three)
    )
    layer_out, second_grad, ret_keep, ret_send, hid_keep, hid_send, hid_sum, ret_sum = feed(
        place, second, cot, middle, vec, w_hid.reshape(WIDTH, HIDDEN), hid,
        (s_four, r_four, sp_four, rp_four),
    )

    feeding = Scatter(place, ((ret_keep, ret_send), (hid_keep, hid_send)))
    feeding.swap()
    middle_grad, branch, incoming, sums = branch_of(middle, second_grad, cot, vec, w_out)
    feeding.got, feeding.kept, incoming = settle(feeding.got, feeding.kept, incoming)

    feeding.first()
    feeding.send_first()
    ready = after(incoming, feeding.sent, feeding.kept)
    grads = attend_back(live, q, k, v, ready, totals, 0, 2)
    grads = attend_back(live, q, k, v, ready, totals, 2, 2, grads)
    feeding.got, feeding.kept, incoming, grads = settle(feeding.got, feeding.kept, ready, grads)

    feeding.second()
    feeding.send_second()
    ready = after(incoming, feeding.sent, feeding.kept)
    grads = attend_back(live, q, k, v, ready, totals, 4, 2, grads)
    feeding.got, feeding.kept, grads, normed = settle(feeding.got, feeding.kept, grads, normed)

    feeding.third()
    feeding.send_third()
    normed, grads = after((normed, grads), feeding.sent, feeding.kept)
    pair = square_grads(place, attended, branch, normed, grads)
    image_low, text_low, late = norm_one(grads, (wq, wk, wv), embedded, middle_grad, vec)
    feeding.got, feeding.kept, pair, image_low, text_low = settle(
        feeding.got, feeding.kept, pair, image_low, text_low
    )

    feeding.fourth()
    feeding.swap()
    squares = Scatter(place, (pair,))
    squares.swap()
    pair = last(
        place, image, text, after(image_low, feeding.sent), text_low, sums, hid_sum, ret_sum, late
    )
    feeding.got, squares.got, squares.kept, pair, image_low = settle(
        feeding.got, squares.got, squares.kept, pair, image_low
    )

    squares.first()
    squares.send_first()
    ending = Scatter(place, (pair,))
    ending.swap()
    ready = after(image_low, squares.sent, squares.kept)
    image_grad, text_grad = input_grads(ready, text_low, w_image, w_text)
    squares.got, squares.kept, ending.got, ending.kept, image_grad, text_grad = settle(
        squares.got, squares.kept, ending.got, ending.kept, image_grad, text_grad
    )

    squares.second()
    squares.send_second()
    ending.first()
    ending.send_first()
    owned = owned_rows(SCATTER_CHUNKS[0], *feeding.sides())
    squares.got, squares.kept, ending.got, ending.kept, owned = settle(
        squares.got, squares.kept, ending.got, ending.kept, owned
    )

    squares.third()
    squares.send_third()
    ending.second()
    ending.send_second()
    squares.got, squares.kept, ending.got, ending.kept = settle(
        squares.got, squares.kept, ending.got, ending.kept
    )

    ending.third()
    ending.send_third()
    squares.fourth()
    squares.swap()
    ending.got, ending.kept, squares.got = settle(ending.got, ending.kept, squares.got)

    ending.fourth()
    ending.swap()
    owned.update(owned_rows(SCATTER_CHUNKS[1], *squares.sides()))
    owned.update(owned_rows(SCATTER_CHUNKS[2], *ending.sides()))
    return (layer_out[None], image_grad[None], text_grad[None]) + tuple(owned[i] for i in range(20))


def gather_any(shards):
    return tuple(lax.all_gather(shard, "fsdp", axis=0, tiled=True) for shard in shards)


def scatter_any(grads):
    pieces = [lax.psum_scatter(g, "fsdp", scatter_dimension=0, tiled=True) for g in grads]
    return tuple(lax.psum(to_low(p), "dp").astype(jnp.float32) for p in pieces)


def on_device(
    chips,
    cores,
    image_states,
    text_states,
    size_group,
    caption_len,
    cotangent,
    image_proj,
    image_bias,
    text_proj,
    text_bias,
    cls_token,
    first_gain,
    first_shift,
    query_proj,
    query_bias,
    key_proj,
    value_proj,
    value_bias,
    output_proj,
    output_bias,
    second_gain,
    second_shift,
    hidden_proj,
    hidden_bias,
    return_proj,
    return_bias,
):
    shards = (
        image_proj,
        image_bias,
        text_proj,
        text_bias,
        cls_token,
        first_gain,
        first_shift,
        query_proj,
        query_bias,
        key_proj,
        value_proj,
        value_bias,
        output_proj,
        output_bias,
        second_gain,
        second_shift,
        hidden_proj,
        hidden_bias,
        return_proj,
        return_bias,
    )
    fits = chips == 16 and cores == 2 and image_states.shape == (1, IMAGE, WIDTH)
    if fits and text_states.shape == (1, TEXTS, WIDTH) and hidden_proj.shape == (48, HIDDEN):
        image, text, cot = image_states[0], text_states[0], cotangent[0]
        return by_kernels(shards, image, text, size_group, caption_len, cot)
    weights = gather_any(shards)
    results, summed = [], None
    for item in range(image_states.shape[0]):
        image_rows, text_rows = image_states[item], text_states[item]
        code, length = size_group[item], caption_len[item]
        result, kept_rows = item_forward(weights, image_rows, text_rows, code, length)
        image_grad, text_grad, grads = item_backward(
            weights, image_rows, text_rows, code, length, kept_rows, cotangent[item]
        )
        results.append((result, image_grad, text_grad))
        summed = grads if summed is None else jax.tree.map(jnp.add, summed, grads)
    owned = scatter_any(summed)
    return tuple(jnp.stack(parts) for parts in zip(*results)) + owned


def solution(mesh):
    placed = (
        P(("fsdp", "dp"), None, None),
        P(("fsdp", "dp"), None, None),
        P(("fsdp", "dp")),
        P(("fsdp", "dp")),
        P(("fsdp", "dp"), None, None),
        P("fsdp", None),
        P("fsdp"),
        P("fsdp", None),
        P("fsdp"),
        P("fsdp"),
        P("fsdp"),
        P("fsdp"),
        P("fsdp", None),
        P("fsdp"),
        P("fsdp", None),
        P("fsdp", None),
        P("fsdp"),
        P("fsdp", None),
        P("fsdp"),
        P("fsdp"),
        P("fsdp"),
        P("fsdp", None),
        P("fsdp"),
        P("fsdp", None),
        P("fsdp"),
    )
    chips, cores = mesh.shape["fsdp"], mesh.shape["dp"]
    return jax.shard_map(
        functools.partial(on_device, chips, cores),
        mesh=mesh,
        in_specs=placed,
        out_specs=(
            P(("fsdp", "dp"), None, None),
            P(("fsdp", "dp"), None, None),
            P(("fsdp", "dp"), None, None),
            P("fsdp", None),
            P("fsdp"),
            P("fsdp", None),
            P("fsdp"),
            P("fsdp"),
            P("fsdp"),
            P("fsdp"),
            P("fsdp", None),
            P("fsdp"),
            P("fsdp", None),
            P("fsdp", None),
            P("fsdp"),
            P("fsdp", None),
            P("fsdp"),
            P("fsdp"),
            P("fsdp"),
            P("fsdp", None),
            P("fsdp"),
            P("fsdp", None),
            P("fsdp"),
        ),
        check_vma=False,
    )
```

```python
import functools
import math

import jax
import jax.numpy as jnp
from jax import lax
from jax.experimental import pallas as pl
from jax.experimental.pallas import tpu as pltpu
from jax.sharding import PartitionSpec as P

HEADS = 12
HEAD_DIM = 64
PATCH_BIG = 325
PATCH_SMALL = 197


EPSILON = 1e-06
NEGATIVE = -1e30


def matmul(left, right):
    return jnp.dot(left, right, preferred_element_type=jnp.float32)


def left_product(left, right):
    return lax.dot_general(
        left, right, (((0,), (0,)), ((), ())), preferred_element_type=jnp.float32
    )


def right_product(left, right):
    return lax.dot_general(
        left, right, (((1,), (1,)), ((), ())), preferred_element_type=jnp.float32
    )


def to_low(values):
    return values.astype(jnp.bfloat16)


def column_sum(values):
    return jnp.sum(values.astype(jnp.float32), 0)


def gelu_exact(values):
    return jax.nn.gelu(values, approximate=False)


def layer_norm(values, gain, shift):
    centered = values - jnp.mean(values, -1, keepdims=True)
    scaled = centered * lax.rsqrt(jnp.mean(centered * centered, -1, keepdims=True) + EPSILON)
    return scaled * gain + shift


def key_mask(size_code, length, row_count):
    position = jnp.arange(row_count, dtype=jnp.int32)
    patches = jnp.where(size_code == 1, PATCH_BIG, PATCH_SMALL).astype(jnp.int32)
    image_live = (position >= 1) & (position <= patches)
    text_live = (position >= 1 + PATCH_BIG) & (position < 1 + PATCH_BIG + length)
    return (position == 0) | image_live | text_live


def head_slice(source, offset, span_width, per_group):
    part = lax.dynamic_slice_in_dim(source, offset, span_width, 1)
    return part.reshape(source.shape[0], per_group, HEAD_DIM)


def attend_forward(queries, keys_all, values_all, key_live):
    row_count = queries.shape[0]
    per_group = math.gcd(HEADS, 4)
    span_width = per_group * HEAD_DIM
    factor = HEAD_DIM ** (-0.5)

    def one_group(group_index, running):
        attended, totals = running
        offset = group_index * span_width
        query_part = head_slice(queries, offset, span_width, per_group)
        key_part = head_slice(keys_all, offset, span_width, per_group)
        value_part = head_slice(values_all, offset, span_width, per_group)
        scores = (
            jnp.einsum("qhd,khd->hqk", query_part, key_part, preferred_element_type=jnp.float32)
            * factor
        )
        scores = jnp.where(key_live, scores, NEGATIVE)
        row_top = jnp.max(scores, -1, keepdims=True)
        exps = jnp.exp(scores - row_top)
        row_total = jnp.sum(exps, -1, keepdims=True)
        prob_rows = to_low(exps / row_total)
        mixed_heads = jnp.einsum(
            "hqk,khd->qhd", prob_rows, value_part, preferred_element_type=jnp.float32
        )
        attended = lax.dynamic_update_slice_in_dim(
            attended, to_low(mixed_heads.reshape(row_count, span_width)), offset, 1
        )
        log_total = (row_top + jnp.log(row_total))[:, :, 0]
        totals = lax.dynamic_update_slice_in_dim(totals, log_total, group_index * per_group, 0)
        return (attended, totals)

    initial = (
        jnp.zeros((row_count, HEADS * HEAD_DIM), jnp.bfloat16),
        jnp.zeros((HEADS, row_count), jnp.float32),
    )
    return lax.fori_loop(0, HEADS // per_group, one_group, initial)


def attend_backward(queries, keys_all, values_all, key_live, totals, incoming):
    row_count = queries.shape[0]
    per_group = math.gcd(HEADS, 4)
    span_width = per_group * HEAD_DIM
    factor = HEAD_DIM ** (-0.5)

    def one_group(group_index, running):
        query_grad, key_grad, value_grad = running
        offset = group_index * span_width
        query_part = head_slice(queries, offset, span_width, per_group)
        key_part = head_slice(keys_all, offset, span_width, per_group)
        value_part = head_slice(values_all, offset, span_width, per_group)
        incoming_part = head_slice(incoming, offset, span_width, per_group)
        log_total = lax.dynamic_slice_in_dim(totals, group_index * per_group, per_group, 0)
        scores = (
            jnp.einsum("qhd,khd->hqk", query_part, key_part, preferred_element_type=jnp.float32)
            * factor
        )
        scores = jnp.where(key_live, scores, NEGATIVE)
        prob_rows = jnp.exp(scores - log_total[:, :, None])
        value_part_grad = jnp.einsum(
            "hqk,qhd->khd", to_low(prob_rows), incoming_part, preferred_element_type=jnp.float32
        )
        prob_grad = jnp.einsum(
            "qhd,khd->hqk", incoming_part, value_part, preferred_element_type=jnp.float32
        )
        score_grad = to_low(
            prob_rows * (prob_grad - jnp.sum(prob_rows * prob_grad, -1, keepdims=True))
        )
        query_part_grad = (
            jnp.einsum("hqk,khd->qhd", score_grad, key_part, preferred_element_type=jnp.float32)
            * factor
        )
        key_part_grad = (
            jnp.einsum("hqk,qhd->khd", score_grad, query_part, preferred_element_type=jnp.float32)
            * factor
        )
        query_grad = lax.dynamic_update_slice_in_dim(
            query_grad, to_low(query_part_grad.reshape(row_count, span_width)), offset, 1
        )
        key_grad = lax.dynamic_update_slice_in_dim(
            key_grad, to_low(key_part_grad.reshape(row_count, span_width)), offset, 1
        )
        value_grad = lax.dynamic_update_slice_in_dim(
            value_grad, to_low(value_part_grad.reshape(row_count, span_width)), offset, 1
        )
        return (query_grad, key_grad, value_grad)

    empty_grad = jnp.zeros((row_count, HEADS * HEAD_DIM), jnp.bfloat16)
    return lax.fori_loop(0, HEADS // per_group, one_group, (empty_grad, empty_grad, empty_grad))


def item_forward(weights, image_rows, text_rows, size_code, length):
    (
        image_proj,
        image_bias,
        text_proj,
        text_bias,
        cls_token,
        first_gain,
        first_shift,
        query_proj,
        query_bias,
        key_proj,
        value_proj,
        value_bias,
        output_proj,
        output_bias,
        second_gain,
        second_shift,
        hidden_proj,
        hidden_bias,
        return_proj,
        return_bias,
    ) = weights
    image_part = matmul(image_rows, image_proj) + image_bias.astype(jnp.float32)
    text_part = matmul(text_rows, text_proj) + text_bias.astype(jnp.float32)
    embedded = jnp.concatenate([cls_token.astype(jnp.float32)[None, :], image_part, text_part], 0)
    normed = to_low(
        layer_norm(embedded, first_gain.astype(jnp.float32), first_shift.astype(jnp.float32))
    )
    queries = to_low(matmul(normed, query_proj) + query_bias.astype(jnp.float32))
    keys_all = to_low(matmul(normed, key_proj))
    values_all = to_low(matmul(normed, value_proj) + value_bias.astype(jnp.float32))
    key_live = key_mask(size_code, length, embedded.shape[0])
    attended, totals = attend_forward(queries, keys_all, values_all, key_live)
    middle = embedded + matmul(attended, output_proj) + output_bias.astype(jnp.float32)
    second = to_low(
        layer_norm(middle, second_gain.astype(jnp.float32), second_shift.astype(jnp.float32))
    )
    inner_pre = matmul(second, hidden_proj) + hidden_bias.astype(jnp.float32)
    activated = to_low(gelu_exact(inner_pre))
    result = middle + matmul(activated, return_proj) + return_bias.astype(jnp.float32)
    kept_rows = (
        embedded,
        normed,
        queries,
        keys_all,
        values_all,
        attended,
        totals,
        middle,
        second,
        inner_pre,
        activated,
    )
    return (to_low(result), kept_rows)


def item_backward(weights, image_rows, text_rows, size_code, length, kept_rows, out_grad):
    (
        image_proj,
        image_bias,
        text_proj,
        text_bias,
        cls_token,
        first_gain,
        first_shift,
        query_proj,
        query_bias,
        key_proj,
        value_proj,
        value_bias,
        output_proj,
        output_bias,
        second_gain,
        second_shift,
        hidden_proj,
        hidden_bias,
        return_proj,
        return_bias,
    ) = weights
    (
        embedded,
        normed,
        queries,
        keys_all,
        values_all,
        attended,
        totals,
        middle,
        second,
        inner_pre,
        activated,
    ) = kept_rows
    grad_return_proj = left_product(activated, out_grad)
    grad_return_bias = column_sum(out_grad)
    activated_grad = right_product(out_grad, return_proj)
    unused_value, gelu_pull = jax.vjp(gelu_exact, inner_pre)
    inner_grad = to_low(gelu_pull(activated_grad)[0])
    grad_hidden_proj = left_product(second, inner_grad)
    grad_hidden_bias = column_sum(inner_grad)
    second_grad = right_product(inner_grad, hidden_proj)
    unused_norm, second_pull = jax.vjp(
        layer_norm, middle, second_gain.astype(jnp.float32), second_shift.astype(jnp.float32)
    )
    middle_part, grad_second_gain, grad_second_shift = second_pull(second_grad)
    middle_grad = out_grad.astype(jnp.float32) + middle_part
    branch_grad = to_low(middle_grad)
    grad_output_proj = left_product(attended, branch_grad)
    grad_output_bias = column_sum(branch_grad)
    attended_grad = to_low(right_product(branch_grad, output_proj))
    key_live = key_mask(size_code, length, embedded.shape[0])
    query_grad, key_grad, value_grad = attend_backward(
        queries, keys_all, values_all, key_live, totals, attended_grad
    )
    grad_query_proj = left_product(normed, query_grad)
    grad_query_bias = column_sum(query_grad)
    grad_key_proj = left_product(normed, key_grad)
    grad_value_proj = left_product(normed, value_grad)
    grad_value_bias = column_sum(value_grad)
    normed_grad = (
        right_product(query_grad, query_proj)
        + right_product(key_grad, key_proj)
        + right_product(value_grad, value_proj)
    )
    unused_first, first_pull = jax.vjp(
        layer_norm, embedded, first_gain.astype(jnp.float32), first_shift.astype(jnp.float32)
    )
    embedded_part, grad_first_gain, grad_first_shift = first_pull(normed_grad)
    embedded_grad = middle_grad + embedded_part
    grad_cls_token = embedded_grad[0]
    image_low = to_low(embedded_grad[1 : 1 + PATCH_BIG])
    text_low = to_low(embedded_grad[1 + PATCH_BIG :])
    image_grad = right_product(image_low, image_proj)
    text_grad = right_product(text_low, text_proj)
    grad_image_proj = left_product(image_rows, image_low)
    grad_image_bias = column_sum(image_low)
    grad_text_proj = left_product(text_rows, text_low)
    grad_text_bias = column_sum(text_low)
    grads = (
        grad_image_proj,
        grad_image_bias,
        grad_text_proj,
        grad_text_bias,
        grad_cls_token,
        grad_first_gain,
        grad_first_shift,
        grad_query_proj,
        grad_query_bias,
        grad_key_proj,
        grad_value_proj,
        grad_value_bias,
        grad_output_proj,
        grad_output_bias,
        grad_second_gain,
        grad_second_shift,
        grad_hidden_proj,
        grad_hidden_bias,
        grad_return_proj,
        grad_return_bias,
    )
    return (image_grad, text_grad, grads)


VECTORS = (1, 3, 4, 5, 6, 8, 11, 13, 14, 15, 19, 17)
LANES = 384
VEC_ROWS = 16
GATHER_CHUNKS = ((0, 2, "vec"), (7, 9, 10), (12, "low"), ("high",), (18,))
SCATTER_CHUNKS = ((18, 16), (12, 7, 9, 10), (0, 2, "vec"))
BOTH = ("fsdp", "dp")
WIDTH = 768
HIDDEN = 3072
IMAGE = 325
TEXTS = 513
ROWS = 839
KEYS = 848
PADDED = 896
LOW = jnp.bfloat16
FULL = jnp.float32
COST_SCALE = 0.3
FAST = pl.BlockSpec(memory_space=pltpu.VMEM)
SCALARS = pl.BlockSpec(memory_space=pltpu.SMEM)


def cost(micros):
    return pl.CostEstimate(
        flops=int(micros * COST_SCALE * 1e9), bytes_accessed=1024, transcendentals=0
    )


class Place:
    def __init__(self):
        self.core = lax.axis_index("dp")
        chip = lax.axis_index("fsdp")
        self.x, self.y, self.z = chip & 1, (chip >> 1) & 1, chip >> 2
        self.scalars = jnp.stack([self.core, self.x, self.y, self.z]).astype(jnp.int32)


def shape(dims, kind=LOW):
    return jax.ShapeDtypeStruct(dims, kind)


def call(kernel, micros, outs, *args, scratch=(), limit=60):
    specs = [SCALARS if a.dtype == jnp.int32 else FAST for a in args]
    return pl.pallas_call(
        kernel,
        out_shape=tuple(outs),
        in_specs=specs,
        out_specs=tuple(FAST for _ in outs),
        scratch_shapes=list(scratch),
        compiler_params=pltpu.CompilerParams(vmem_limit_bytes=limit * 2**20),
        cost_estimate=cost(micros),
    )(*args)


def after(values, *others):
    return lax.optimization_barrier((values, others))[0]


def settle(*values):
    return lax.optimization_barrier(values)


def swap_cores(values):
    with jax.named_scope("between_cores"):
        return lax.ppermute(values, "dp", [(0, 1), (1, 0)])


def to_chip(values, mask_zero, mask_one):
    pairs = []
    for chip in range(16):
        pairs.append((chip * 2, (chip ^ mask_zero) * 2))
        pairs.append((chip * 2 + 1, (chip ^ mask_one) * 2 + 1))
    with jax.named_scope(f"chips_{mask_zero}_{mask_one}"):
        return lax.ppermute(values, BOTH, pairs)


def sub_blocks(index):
    return 4 if index == 16 else 1


def block_rows(index):
    return {"vec": VEC_ROWS, 16: 192, 18: 192, "low": 96, "high": 96}.get(index, 48)


def pack_kernel(chunk, at_ref, *refs):
    core = at_ref[0]
    count = len(chunk) + (11 if "vec" in chunk else 0)
    ins, out = refs[:count], refs[count]
    offset = 0
    for place, index in enumerate(chunk):
        if index == "vec":
            rows = refs[-1]
            rows[...] = jnp.zeros_like(rows)
            for row in range(12):
                source = ins[place + row]
                rows[row : row + 1, 0 : source.shape[1]] = source[...].astype(FULL)
            out[offset : offset + VEC_ROWS, :] = rows[...].astype(LOW)
            continue
        parts = {"low": (4, (0, 1)), "high": (4, (2, 3))}.get(index, (1, (0,)))
        rows = ins[place].shape[0]
        for s in parts[1]:
            first = pl.multiple_of((core * parts[0] + s) * LANES, LANES)
            out[offset : offset + rows, :] = ins[place][:, pl.ds(first, LANES)]
            offset += rows


def pack(place, shards, chunk):
    rows = sum(block_rows(i) for i in chunk)
    ins = [shards[16 if i in ("low", "high") else i] for i in chunk if i != "vec"]
    scratch = ()
    if "vec" in chunk:
        ins += [shards[i].reshape(1, -1) for i in VECTORS]
        scratch = (pltpu.VMEM((VEC_ROWS, LANES), FULL),)
    kernel = functools.partial(pack_kernel, chunk)
    return call(kernel, 1, [shape((rows, LANES))], place.scalars, *ins, scratch=scratch)[0]


def all_z(own):
    return [own] + [to_chip(own, 4 * s, 4 * s) for s in (1, 2, 3)]


def unpack(at_ref, pieces, targets):
    core, x, y, z = at_ref[0], at_ref[1], at_ref[2], at_ref[3]

    def fill(zero_s, zero_r, one_s, one_r):
        for offset, blocks, count, out in targets:
            rows = out.shape[3]
            for n, s in enumerate(blocks):
                first = slice(offset + n * rows, offset + (n + 1) * rows)
                left = slice(s * LANES, (s + 1) * LANES)
                right = slice((count + s) * LANES, (count + s + 1) * LANES)
                for far in range(4):
                    plane = z ^ far
                    for b in range(2):
                        out[plane, y, x ^ b, :, left] = zero_s[b, far, first, :]
                        out[plane, 1 - y, x ^ b, :, left] = zero_r[b, far, first, :]
                        if count:
                            out[plane, y ^ b, x, :, right] = one_s[b, far, first, :]
                            out[plane, y ^ b, 1 - x, :, right] = one_r[b, far, first, :]

    s8, r8, s8p, r8p = pieces

    @pl.when(core == 0)
    def _():
        fill(s8, r8, s8p, r8p)

    @pl.when(core == 1)
    def _():
        fill(s8p, r8p, s8, r8)


def square(ref):
    return ref[...].reshape(16 * ref.shape[3], ref.shape[4])


def row_chunks(step, total=ROWS):
    return [slice(a, min(a + step, total)) for a in range(0, total, step)]


def standard(values):
    centered = values - jnp.mean(values, -1, keepdims=True)
    scale = lax.rsqrt(jnp.mean(centered * centered, -1, keepdims=True) + EPSILON)
    return centered * scale, scale


def norm_back(values, gain, incoming):
    unit, scale = standard(values)
    f = incoming * gain
    back = (f - jnp.mean(f, -1, keepdims=True) - unit * jnp.mean(f * unit, -1, keepdims=True)) * scale
    return back, unit


def sum_rows(values):
    return jnp.sum(values.astype(FULL), 0, keepdims=True)


def embed_kernel(at, image, text, s8, r8, s8p, r8p, w_image, w_text, vec, hid, embedded, normed, small):
    unpack(
        at,
        (s8, r8, s8p, r8p),
        ((0, (0,), 1, w_image), (48, (0,), 1, w_text), (96, (0,), 0, small)),
    )
    for f in range(16):
        piece = small[f >> 2, (f >> 1) & 1, f & 1].astype(FULL)
        vec[:, f * 48 : (f + 1) * 48] = piece[:, :48]
        hid[:, f * 192 : (f + 1) * 192] = piece[11:12, :192]
    embedded[0:1, :] = vec[2:3, :]
    embedded[1 : 1 + IMAGE, :] = matmul(image[...], square(w_image)) + vec[0:1, :]
    embedded[1 + IMAGE : ROWS, :] = matmul(text[...], square(w_text)) + vec[1:2, :]
    for rows in row_chunks(64):
        unit, unused_scale = standard(embedded[rows, :])
        normed[rows, :] = to_low(unit * vec[3:4, :] + vec[4:5, :])


def embed(place, image, text, pieces):
    block = (4, 2, 2, 48, WIDTH)
    outs = [
        shape(block),
        shape(block),
        shape((VEC_ROWS, WIDTH), FULL),
        shape((1, HIDDEN), FULL),
        shape((ROWS, WIDTH), FULL),
        shape((ROWS, WIDTH)),
    ]
    scratch = (pltpu.VMEM((4, 2, 2, VEC_ROWS, LANES), LOW),)
    return call(embed_kernel, 5.5, outs, place.scalars, image, text, *pieces, scratch=scratch)


def qkv_kernel(at, normed, vec, s8, r8, s8p, r8p, wq, wk, wv, q, k, v):
    unpack(
        at,
        (s8, r8, s8p, r8p),
        ((0, (0,), 1, wq), (48, (0,), 1, wk), (96, (0,), 1, wv)),
    )
    rows = normed[...]
    for out in (q, k, v):
        out[832:PADDED, :] = jnp.zeros((PADDED - 832, WIDTH), LOW)
    low = to_low(matmul(rows, square(wq)) + vec[5:6, :])
    q[0:ROWS, :] = to_low(low.astype(FULL) * HEAD_DIM**-0.5)
    k[0:ROWS, :] = to_low(matmul(rows, square(wk)))
    v[0:ROWS, :] = to_low(matmul(rows, square(wv)) + vec[6:7, :])


def qkv(place, normed, vec, pieces):
    outs = [shape((4, 2, 2, 48, WIDTH))] * 3 + [shape((PADDED, WIDTH))] * 3
    return call(qkv_kernel, 7, outs, place.scalars, normed, vec, *pieces)


def mask_column(live):
    position = lax.broadcasted_iota(jnp.int32, (KEYS, 1), 0)
    patches = jnp.where(live[0] == 1, PATCH_BIG, PATCH_SMALL).astype(jnp.int32)
    image_live = (position >= 1) & (position <= patches)
    text_live = (position >= 1 + PATCH_BIG) & (position < 1 + PATCH_BIG + live[1])
    return jnp.where((position == 0) | image_live | text_live, 0.0, NEGATIVE).astype(FULL)


def one_head(ref_value, head):
    lane = lax.broadcasted_iota(jnp.int32, ref_value.shape, 1)
    keep = (lane < HEAD_DIM) if head == 0 else (lane >= HEAD_DIM)
    return jnp.where(keep, ref_value, jnp.zeros_like(ref_value))


def across(values):
    return jnp.transpose(values.astype(FULL))


def fold_rows(values, op):
    return op(values.reshape(values.shape[0] // 8, 8, values.shape[1]), 0)


def attend_kernel(live, q, k, v, attended, totals, keys, scores, probs, mixed):
    bias = mask_column(live)
    for h in range(2):
        keys[h] = one_head(k[0:KEYS, :], h)
    values_t = to_low(across(v[0:KEYS, :]))
    totals[...] = jnp.zeros_like(totals)
    parts = [(piece, h) for piece in row_chunks(256, PADDED) for h in range(2)]
    tiles = row_chunks(128, KEYS)
    tops = {}

    def score(n, tile):
        piece, h = parts[n]
        made = right_product(keys[h, tile, :], q[piece, :]) + bias[tile, :]
        scores[n % 2, tile, 0 : made.shape[1]] = made
        top = fold_rows(made, jnp.max)
        tops[n] = jnp.maximum(tops[n], top) if n in tops else top

    for tile in tiles:
        score(0, tile)
    for n, (piece, h) in enumerate(parts):
        width = piece.stop - piece.start
        top = jnp.max(tops[n], 0, keepdims=True)
        total = jnp.zeros((8, width), FULL)
        for tile in tiles:
            if n + 1 < len(parts):
                score(n + 1, tile)
            exps = jnp.exp(scores[n % 2, tile, 0:width] - top)
            total = total + fold_rows(exps, jnp.sum)
            probs[n % 2, tile, 0:width] = to_low(exps)
        total = jnp.sum(total, 0, keepdims=True)
        rows = slice(h * HEAD_DIM, (h + 1) * HEAD_DIM)
        out = matmul(values_t[rows, :], probs[n % 2, :, 0:width])
        mixed[rows, piece] = out * (1.0 / total)
        totals[0, h : h + 1, piece] = top + jnp.log(total)
    attended[...] = to_low(jnp.transpose(mixed[...]))


def attend(live, q, k, v, first, count, earlier=()):
    spec = pl.BlockSpec((PADDED, 2 * HEAD_DIM), lambda i: (0, i + first))
    anywhere = pl.BlockSpec(memory_space=pl.ANY)

    def kernel(live, q, k, v, *refs):
        attend_kernel(live, q, k, v, *refs[len(earlier) :])

    return pl.pallas_call(
        kernel,
        grid=(count,),
        out_shape=(shape((PADDED, WIDTH)), shape((HEADS // 2, 8, PADDED), FULL)),
        in_specs=[SCALARS] + [spec] * 3 + [anywhere] * len(earlier),
        out_specs=(spec, pl.BlockSpec((1, 8, PADDED), lambda i: (i + first, 0, 0))),
        scratch_shapes=[
            pltpu.VMEM((2, KEYS, 2 * HEAD_DIM), LOW),
            pltpu.VMEM((2, KEYS, 256), FULL),
            pltpu.VMEM((2, KEYS, 256), LOW),
            pltpu.VMEM((2 * HEAD_DIM, PADDED), FULL),
        ],
        input_output_aliases={4 + n: n for n in range(len(earlier))},
        compiler_params=pltpu.CompilerParams(vmem_limit_bytes=60 * 2**20),
        cost_estimate=cost(3 * count),
    )(live, q, k, v, *earlier)


def attend_back_kernel(
    live, q, k, v, incoming, attended, totals, q_grad, k_grad, v_grad,
    keys, values, probs, score_grads, mixed,
):
    bias = mask_column(live)
    for h in range(2):
        keys[h] = one_head(k[0:KEYS, :], h)
        values[h] = one_head(v[0:KEYS, :], h)
    keys_t = to_low(across(k[0:KEYS, :]))
    product = jnp.transpose(incoming[...].astype(FULL) * attended[...].astype(FULL))
    for h in range(2):
        rows = slice(h * HEAD_DIM, (h + 1) * HEAD_DIM)
        along = jnp.sum(product[rows], 0, keepdims=True)
        for piece in row_chunks(256, PADDED):
            for tile in row_chunks(256, KEYS):
                made = right_product(keys[h, tile, :], q[piece, :]) + bias[tile, :]
                prob = jnp.exp(made - totals[0, h : h + 1, piece])
                prob_grad = right_product(values[h, tile, :], incoming[piece, :])
                probs[h, tile, piece] = to_low(prob)
                score_grads[h, tile, piece] = to_low(prob * (prob_grad - along[:, piece]))
        mixed[rows, :] = matmul(keys_t[rows, :], score_grads[h])
    lane = lax.broadcasted_iota(jnp.int32, (KEYS, 2 * HEAD_DIM), 1) < HEAD_DIM
    for out, left, right in ((k_grad, score_grads, q), (v_grad, probs, incoming)):
        right = right[...]
        out[0:KEYS, :] = to_low(jnp.where(lane, matmul(left[0], right), matmul(left[1], right)))
    q_grad[...] = to_low(jnp.transpose(mixed[...]) * HEAD_DIM**-0.5)


def attend_back(live, q, k, v, incoming, attended, totals):
    spec = pl.BlockSpec((PADDED, 2 * HEAD_DIM), lambda i: (0, i))
    return pl.pallas_call(
        attend_back_kernel,
        grid=(HEADS // 2,),
        out_shape=(shape((PADDED, WIDTH)),) * 3,
        in_specs=[SCALARS] + [spec] * 5 + [pl.BlockSpec((1, 8, PADDED), lambda i: (i, 0, 0))],
        out_specs=(spec,) * 3,
        scratch_shapes=[
            pltpu.VMEM((2, KEYS, 2 * HEAD_DIM), LOW),
            pltpu.VMEM((2, KEYS, 2 * HEAD_DIM), LOW),
            pltpu.VMEM((2, KEYS, PADDED), LOW),
            pltpu.VMEM((2, KEYS, PADDED), LOW),
            pltpu.VMEM((2 * HEAD_DIM, PADDED), FULL),
        ],
        compiler_params=pltpu.CompilerParams(vmem_limit_bytes=60 * 2**20),
        cost_estimate=cost(28),
    )(live, q, k, v, incoming, attended, totals)


def middle_kernel(
    at, attended, embedded, vec, s8, r8, s8p, r8p, s_hi, r_hi, sp_hi, rp_hi,
    w_out, w_hid, middle, second,
):
    unpack(at, (s8, r8, s8p, r8p), ((0, (0,), 1, w_out), (48, (0, 1), 4, w_hid)))
    unpack(at, (s_hi, r_hi, sp_hi, rp_hi), ((0, (2, 3), 4, w_hid),))
    middle[...] = embedded[...] + matmul(attended[0:ROWS, :], square(w_out)) + vec[7:8, :]
    for rows in row_chunks(64):
        unit, unused_scale = standard(middle[rows, :])
        second[rows, :] = to_low(unit * vec[8:9, :] + vec[9:10, :])


def middle_of(place, attended, embedded, vec, pieces):
    outs = [
        shape((4, 2, 2, 48, WIDTH)),
        shape((4, 2, 2, 48, HIDDEN)),
        shape((ROWS, WIDTH), FULL),
        shape((ROWS, WIDTH)),
    ]
    return call(middle_kernel, 8, outs, place.scalars, attended, embedded, vec, *pieces)


def gelu_parts(u):
    cumulative = 0.5 * (1.0 + lax.erf(u * (2.0**-0.5)))
    slope = cumulative + u * (jnp.exp(-0.5 * u * u) * (2.0 * math.pi) ** -0.5)
    return u * cumulative, slope


def feed_kernel(
    at, second, cot, middle, vec, w_hid, hid, s8, r8, s8p, r8p,
    layer_out, second_grad, ret_keep, ret_send, hid_keep, hid_send, hid_sum, ret_sum,
    w_ret, act, inner, total,
):
    step = pl.program_id(0)
    core, x, y = at[0], at[1], at[2]

    def fill(zero_s, zero_r, one_s, one_r):
        for b in range(2):
            w_ret[y, x ^ b, :, 0:LANES] = zero_s[b, 0]
            w_ret[1 - y, x ^ b, :, 0:LANES] = zero_r[b, 0]
            w_ret[y ^ b, x, :, LANES:] = one_s[b, 0]
            w_ret[y ^ b, 1 - x, :, LANES:] = one_r[b, 0]

    @pl.when(core == 0)
    def _():
        fill(s8, r8, s8p, r8p)

    @pl.when(core == 1)
    def _():
        fill(s8p, r8p, s8, r8)

    ret = w_ret[...].reshape(WIDTH, WIDTH)
    inward = w_hid[...]
    for rows in row_chunks(432):
        pre = matmul(second[rows, :], inward) + hid[...]
        back = right_product(cot[rows, :], ret)
        value, slope = gelu_parts(pre)
        act[rows, :] = to_low(value)
        inner[rows, :] = to_low(back * slope)
        out = matmul(act[rows, :], ret)
        back = right_product(inner[rows, :], inward)

        @pl.when(step == 0)
        def _():
            total[rows, :] = out
            second_grad[rows, :] = back

        @pl.when(step > 0)
        def _():
            total[rows, :] += out
            second_grad[rows, :] += back

    hid_sum[...] = sum_rows(inner[...])
    ret_grad = to_low(left_product(act[...], cot[...])).reshape(4, 192, WIDTH)
    hid_grad = to_low(left_product(second[...], inner[...])).reshape(16, 48, WIDTH)

    @pl.when(core == 0)
    def _():
        ret_keep[...] = ret_grad[:, :, 0:LANES]
        ret_send[...] = ret_grad[:, :, LANES:]

    @pl.when(core == 1)
    def _():
        ret_keep[...] = ret_grad[:, :, LANES:]
        ret_send[...] = ret_grad[:, :, 0:LANES]

    @pl.when(step < 2)
    def _():
        hid_send[:, 0:48, :] = hid_grad[:, :, 0:LANES]
        hid_send[:, 48:96, :] = hid_grad[:, :, LANES:]

    @pl.when(step >= 2)
    def _():
        hid_keep[:, 0:48, :] = hid_grad[:, :, 0:LANES]
        hid_keep[:, 48:96, :] = hid_grad[:, :, LANES:]

    @pl.when(step == 3)
    def _():
        layer_out[...] = to_low(middle[...] + total[...] + vec[10:11, :])
        ret_sum[...] = sum_rows(cot[...])


def feed(place, second, cot, middle, vec, w_hid, hid, pieces):
    def column(i, at):
        half = jnp.where(i < 2, 1 - at[0], at[0])
        return 2 * half + lax.rem(i, 2)

    def whole(dims):
        return pl.BlockSpec(dims, lambda i, at: (0,) * len(dims))

    piece = pl.BlockSpec((2, 1, 192, LANES), lambda i, at: (0, column(i, at) ^ at[3], 0, 0))
    ret_spec = pl.BlockSpec((4, 192, LANES), lambda i, at: (column(i, at), 0, 0))
    outs = (
        shape((ROWS, WIDTH)),
        shape((ROWS, WIDTH), FULL),
        shape((16, 192, LANES)),
        shape((16, 192, LANES)),
        shape((16, 192, LANES)),
        shape((16, 192, LANES)),
        shape((1, HIDDEN), FULL),
        shape((1, WIDTH), FULL),
    )
    grid = pltpu.PrefetchScalarGridSpec(
        num_scalar_prefetch=1,
        grid=(4,),
        in_specs=[
            whole((ROWS, WIDTH)),
            whole((ROWS, WIDTH)),
            whole((ROWS, WIDTH)),
            whole((VEC_ROWS, WIDTH)),
            pl.BlockSpec((WIDTH, WIDTH), lambda i, at: (0, column(i, at))),
            pl.BlockSpec((1, WIDTH), lambda i, at: (0, column(i, at))),
            piece,
            piece,
            piece,
            piece,
        ],
        out_specs=(
            whole((ROWS, WIDTH)),
            whole((ROWS, WIDTH)),
            ret_spec,
            ret_spec,
            pl.BlockSpec((16, 96, LANES), lambda i, at: (0, jnp.maximum(i - 2, 0), 0)),
            pl.BlockSpec((16, 96, LANES), lambda i, at: (0, jnp.minimum(i, 1), 0)),
            pl.BlockSpec((1, WIDTH), lambda i, at: (0, column(i, at))),
            whole((1, WIDTH)),
        ),
        scratch_shapes=[
            pltpu.VMEM((2, 2, 192, WIDTH), LOW),
            pltpu.VMEM((ROWS, WIDTH), LOW),
            pltpu.VMEM((ROWS, WIDTH), LOW),
            pltpu.VMEM((ROWS, WIDTH), FULL),
        ],
    )
    return pl.pallas_call(
        feed_kernel,
        grid_spec=grid,
        out_shape=outs,
        compiler_params=pltpu.CompilerParams(vmem_limit_bytes=60 * 2**20),
        cost_estimate=cost(40),
    )(place.scalars, second, cot, middle, vec, w_hid, hid, *pieces)


def branch_kernel(middle, second_grad, cot, vec, w_out, middle_grad, branch, incoming, sums):
    parts = [jnp.zeros((1, WIDTH), FULL)] * 3
    for rows in row_chunks(64):
        e = second_grad[rows, :]
        back, unit = norm_back(middle[rows, :], vec[8:9, :], e)
        grad = cot[rows, :].astype(FULL) + back
        middle_grad[rows, :] = grad
        branch[rows, :] = to_low(grad)
        for n, term in enumerate((e * unit, e, to_low(grad))):
            parts[n] = parts[n] + sum_rows(term)
    for n in range(3):
        sums[n : n + 1, :] = parts[n]
    incoming[832:PADDED, :] = jnp.zeros((PADDED - 832, WIDTH), LOW)
    incoming[0:ROWS, :] = to_low(right_product(branch[...], square(w_out)))


def branch_of(middle, second_grad, cot, vec, w_out):
    outs = [
        shape((ROWS, WIDTH), FULL),
        shape((ROWS, WIDTH)),
        shape((PADDED, WIDTH)),
        shape((8, WIDTH), FULL),
    ]
    return call(branch_kernel, 8, outs, middle, second_grad, cot, vec, w_out)


def both_halves(core, left, right_ref, first, keep, send, offset, rows):
    for half, out in ((core, keep), (1 - core, send)):
        columns = pl.ds(pl.multiple_of(half * LANES, LANES), LANES)
        grad = left_product(left, right_ref[first, columns])
        out[:, offset : offset + 48, :] = to_low(grad).reshape(16, 48, LANES)


def square_grads_kernel(at, attended, branch, normed, dq, dk, dv, keep, send):
    rows = slice(0, ROWS)
    both_halves(at[0], attended[rows, :], branch, rows, keep, send, 0, 48)
    left = normed[...]
    for n, ref in enumerate((dq, dk, dv)):
        both_halves(at[0], left, ref, rows, keep, send, 48 * (n + 1), 48)


def square_grads(place, attended, branch, normed, grads):
    outs = [shape((16, 192, LANES))] * 2
    return call(
        square_grads_kernel, 11, outs, place.scalars, attended, branch, normed, *grads
    )


def norm_one_kernel(
    dq, dk, dv, wq, wk, wv, embedded, middle_grad, vec, image_low, text_low, late, grad
):
    rows = slice(0, ROWS)
    grad[...] = (
        right_product(dq[rows, :], square(wq))
        + right_product(dk[rows, :], square(wk))
        + right_product(dv[rows, :], square(wv))
    )
    parts = [jnp.zeros((1, WIDTH), FULL)] * 4
    for piece in row_chunks(64):
        e = grad[piece, :]
        back, unit = norm_back(embedded[piece, :], vec[3:4, :], e)
        for n, term in enumerate((e * unit, e, dq[piece, :], dv[piece, :])):
            parts[n] = parts[n] + sum_rows(term)
        grad[piece, :] = middle_grad[piece, :] + back
    image_low[...] = to_low(grad[1 : 1 + IMAGE, :])
    text_low[...] = to_low(grad[1 + IMAGE : ROWS, :])
    late[...] = jnp.zeros_like(late)
    late[0:1, :] = grad[0:1, :]
    for n in range(4):
        late[n + 1 : n + 2, :] = parts[n]


def norm_one(grads, projs, embedded, middle_grad, vec):
    outs = [shape((IMAGE, WIDTH)), shape((TEXTS, WIDTH)), shape((8, WIDTH), FULL)]
    scratch = (pltpu.VMEM((ROWS, WIDTH), FULL),)
    return call(
        norm_one_kernel, 11, outs, *grads, *projs, embedded, middle_grad, vec, scratch=scratch
    )


def last_kernel(
    at, image, text, image_low, text_low, sums, hid_sum, ret_sum, late,
    keep, send, rows16, packed,
):
    both_halves(at[0], image[...], image_low, slice(0, IMAGE), keep, send, 0, 48)
    both_halves(at[0], text[...], text_low, slice(0, TEXTS), keep, send, 48, 48)
    rows16[...] = jnp.zeros_like(rows16)
    found = (
        sum_rows(image_low[...]), sum_rows(text_low[...]), late[0:1, :], late[1:2, :], late[2:3, :],
        late[3:4, :], late[4:5, :], sums[2:3, :], sums[0:1, :], sums[1:2, :], ret_sum[...],
    )
    for n, value in enumerate(found):
        rows16[n : n + 1, :] = value
    packed[...] = jnp.zeros_like(packed)
    for f in range(16):
        packed[f, :, 0:48] = rows16[:, f * 48 : (f + 1) * 48]
        packed[f, 11:12, 0:192] = hid_sum[:, f * 192 : (f + 1) * 192]
    low = to_low(packed[...])
    keep[:, 96:112, :] = low
    send[:, 96:112, :] = low


def last(place, image, text, image_low, text_low, sums, hid_sum, ret_sum, late):
    outs = [shape((16, 112, LANES)), shape((16, 112, LANES))]
    scratch = (pltpu.VMEM((VEC_ROWS, WIDTH), FULL), pltpu.VMEM((16, VEC_ROWS, LANES), FULL))
    return call(
        last_kernel, 5.5, outs, place.scalars, image, text, image_low, text_low, sums, hid_sum, ret_sum,
        late, scratch=scratch,
    )


def inputs_kernel(image_low, text_low, w_image, w_text, image_grad, text_grad):
    image_grad[...] = right_product(image_low[...], square(w_image))
    text_grad[...] = right_product(text_low[...], square(w_text))


def input_grads(image_low, text_low, w_image, w_text):
    outs = [shape((IMAGE, WIDTH), FULL), shape((TEXTS, WIDTH), FULL)]
    return call(inputs_kernel, 4.4, outs, image_low, text_low, w_image, w_text)


def add_low(*values):
    total = values[0].astype(FULL)
    for value in values[1:]:
        total = total + value.astype(FULL)
    return to_low(total)


def pick(values, at, axis):
    return lax.dynamic_index_in_dim(values, at, axis, keepdims=False)


class Scatter:
    def __init__(self, place, pairs):
        self.place = place
        self.kept = [keep for keep, unused_send in pairs]
        self.sent = [send for unused_keep, send in pairs]
        self.got = None

    def state(self):
        return self.kept, self.got

    def first(self):
        zero, x, y = self.place.core == 0, self.place.x, self.place.y
        near = [jnp.where(zero, 2 * y + s, 2 * s + x) for s in (0, 1)]
        far = [jnp.where(zero, 2 * (1 - y) + s, 2 * s + (1 - x)) for s in (0, 1)]

        def summed(places):
            parts = []
            for keep, more in zip(self.kept, self.got):
                keep, more = (v.reshape(4, 4, v.shape[1], LANES) for v in (keep, more))
                added = [add_low(pick(keep, q, 1), pick(more, q, 1)) for q in places]
                parts.append(jnp.stack(added, 1))
            return jnp.concatenate(parts, 2) if len(parts) > 1 else parts[0]

        self.sent, self.kept = summed(far), summed(near)

    def second(self):
        mine = jnp.where(self.place.core == 0, self.place.x, self.place.y)
        kept, got = self.kept, self.got
        self.sent = add_low(pick(kept, 1 - mine, 1), pick(got, 1 - mine, 1))
        self.kept = add_low(pick(kept, mine, 1), pick(got, mine, 1))

    def third(self):
        z = self.place.z
        total = add_low(self.kept, self.got)
        self.kept = pick(total, z, 0)
        self.sent = [pick(total, z ^ s, 0) for s in (1, 2, 3)]

    def fourth(self):
        self.sent = self.kept = add_low(self.kept, *self.got)

    def swap(self):
        self.got = jax.tree.map(swap_cores, self.sent)

    def send_first(self):
        self.got = to_chip(self.sent, 2, 1)

    def send_second(self):
        self.got = to_chip(self.sent, 1, 2)

    def send_third(self, steps=(1, 2, 3)):
        self.got = [to_chip(self.sent[s - 1], 4 * s, 4 * s) for s in steps]

    def sides(self):
        zero = self.place.core == 0
        mine, other = self.kept, self.got
        return jnp.where(zero, mine, other).astype(FULL), jnp.where(zero, other, mine).astype(FULL)


def owned_rows(chunk, left, right):
    result, at = {}, 0
    for index in chunk:
        rows = block_rows(index)
        if index == "vec":
            for n, vector in enumerate(VECTORS):
                result[vector] = left[at + n, : 192 if vector == 17 else 48]
        else:
            count = sub_blocks(index)
            step = rows // count
            sides = [
                side[at + s * step : at + (s + 1) * step] for side in (left, right) for s in range(count)
            ]
            result[index] = jnp.concatenate(sides, 1)
        at += rows
    return result


def by_kernels(shards, image, text, size_code, length, cot):
    place = Place()
    live = jnp.concatenate([size_code, length]).astype(jnp.int32)
    own_one = pack(place, shards, GATHER_CHUNKS[0])

    z_one = all_z(own_one)
    owns = [pack(place, shards, chunk) for chunk in GATHER_CHUNKS[1:]]
    z_one, owns = settle(z_one, owns)

    z_one = jnp.stack(z_one)
    b_one, z_two = to_chip(z_one, 1, 2), all_z(owns[0])
    b_one, z_two, z_one, owns = settle(b_one, z_two, z_one, owns)

    s_one, z_two = jnp.stack([z_one, b_one]), jnp.stack(z_two)
    r_one, sp_one, z_a = to_chip(s_one, 2, 1), swap_cores(s_one), all_z(owns[1])
    r_one, sp_one, s_one, z_a, z_two = settle(r_one, sp_one, s_one, z_a, z_two)

    z_a = jnp.stack(z_a)
    b_two, rp_one, b_a, z_b = to_chip(z_two, 1, 2), swap_cores(r_one), to_chip(z_a, 1, 2), all_z(owns[2])
    w_image, w_text, vec, hid, embedded, normed = embed(
        place, image, after(text, z_a), (s_one, r_one, sp_one, rp_one)
    )
    b_two, b_a, z_b, z_two, normed = settle(b_two, b_a, z_b, z_two, normed)

    s_two = jnp.stack([z_two, b_two])
    r_two, sp_two, z_c = to_chip(s_two, 2, 1), swap_cores(s_two), all_z(owns[3])
    s_a, z_b = jnp.stack([z_a, b_a]), jnp.stack(z_b)
    r_two, sp_two, z_c, s_two, s_a, z_b = settle(r_two, sp_two, z_c, s_two, s_a, z_b)

    rp_two, r_a, b_b = swap_cores(r_two), to_chip(s_a, 2, 1), to_chip(z_b, 1, 2)
    z_c, sp_a = jnp.stack(z_c), swap_cores(s_a)
    wq, wk, wv, q, k, v = qkv(place, after(normed, z_c), vec, (s_two, r_two, sp_two, rp_two))
    both = attend(live, q, k, v, 0, 2)
    r_a, b_b, z_c, sp_a, both = settle(r_a, b_b, z_c, sp_a, both)

    s_b = jnp.stack([z_b, b_b])
    r_b, b_c, sp_b, rp_a = to_chip(s_b, 2, 1), to_chip(z_c, 1, 2), swap_cores(s_b), swap_cores(r_a)
    both = attend(live, after(q, s_b), k, v, 2, 2, both)
    attended, totals = attend(live, q, k, v, 4, 2, both)
    r_b, b_c, sp_b, rp_a, attended = settle(r_b, b_c, sp_b, rp_a, attended)

    s_c = jnp.stack([z_c, b_c])
    r_c, sp_c, rp_b = to_chip(s_c, 2, 1), swap_cores(s_c), swap_cores(r_b)
    w_out, w_hid, middle, second = middle_of(
        place, after(attended, s_c), embedded, vec, (s_a, r_a, sp_a, rp_a, s_b, r_b, sp_b, rp_b)
    )
    r_c, sp_c, second = settle(r_c, sp_c, second)

    layer_out, second_grad, ret_keep, ret_send, hid_keep, hid_send, hid_sum, ret_sum = feed(
        place, second, cot, middle, vec, w_hid.reshape(WIDTH, HIDDEN), hid,
        (s_c, r_c, sp_c, swap_cores(r_c)),
    )

    feeding = Scatter(place, ((ret_keep, ret_send), (hid_keep, hid_send)))
    feeding.swap()
    middle_grad, branch, incoming, sums = branch_of(middle, second_grad, cot, vec, w_out)
    feeding.got, feeding.kept, incoming = settle(feeding.got, feeding.kept, incoming)

    feeding.first()
    feeding.send_first()
    incoming = after(incoming, feeding.sent, feeding.kept)
    grads = attend_back(live, q, k, v, incoming, attended, totals)
    feeding.got, feeding.kept, grads = settle(feeding.got, feeding.kept, grads)

    feeding.second()
    feeding.send_second()
    grads = after(grads, feeding.sent, feeding.kept)
    pair = square_grads(place, attended, branch, normed, grads)
    feeding.got, feeding.kept, grads, pair = settle(feeding.got, feeding.kept, grads, pair)

    feeding.third()
    feeding.send_third((1, 3))
    squares = Scatter(place, (pair,))
    squares.swap()
    grads = after(grads, feeding.sent, feeding.kept)
    image_low, text_low, late = norm_one(grads, (wq, wk, wv), embedded, middle_grad, vec)
    early, feeding.sent, squares.got, squares.kept, image_low, text_low = settle(
        feeding.got, feeding.sent, squares.got, squares.kept, image_low, text_low
    )

    feeding.send_third((2,))
    squares.first()
    squares.send_first()
    image_low, text_low = after((image_low, text_low), squares.sent, squares.kept)
    pair = last(place, image, text, image_low, text_low, sums, hid_sum, ret_sum, late)
    image_grad, text_grad = input_grads(image_low, text_low, w_image, w_text)
    feeding.got, squares.got, squares.kept, pair, image_grad, text_grad = settle(
        feeding.got + early, squares.got, squares.kept, pair, image_grad, text_grad
    )

    ending = Scatter(place, (pair,))
    ending.swap()
    squares.second()
    squares.send_second()
    feeding.fourth()
    ending.got, ending.kept, squares.got, squares.kept, feeding.sent = settle(
        ending.got, ending.kept, squares.got, squares.kept, feeding.sent
    )

    feeding.kept = feeding.sent
    feeding.swap()
    ending.first()
    ending.send_first()
    squares.third()
    squares.send_third()
    ending.got, ending.kept, squares.got, squares.kept, feeding.got, image_grad, text_grad = settle(
        ending.got, ending.kept, squares.got, squares.kept, feeding.got, image_grad, text_grad
    )

    ending.second()
    ending.send_second()
    squares.fourth()
    squares.swap()
    owned = owned_rows(SCATTER_CHUNKS[0], *feeding.sides())
    ending.got, ending.kept, squares.got, owned = settle(ending.got, ending.kept, squares.got, owned)

    ending.third()
    ending.send_third()
    owned.update(owned_rows(SCATTER_CHUNKS[1], *squares.sides()))
    ending.got, ending.kept, owned = settle(ending.got, ending.kept, owned)

    ending.fourth()
    ending.swap()
    owned.update(owned_rows(SCATTER_CHUNKS[2], *ending.sides()))
    return (layer_out[None], image_grad[None], text_grad[None]) + tuple(owned[i] for i in range(20))


def gather_any(shards):
    return tuple(lax.all_gather(shard, "fsdp", axis=0, tiled=True) for shard in shards)


def scatter_any(grads):
    pieces = [lax.psum_scatter(g, "fsdp", scatter_dimension=0, tiled=True) for g in grads]
    return tuple(lax.psum(to_low(p), "dp").astype(jnp.float32) for p in pieces)


def on_device(
    chips,
    cores,
    image_states,
    text_states,
    size_group,
    caption_len,
    cotangent,
    image_proj,
    image_bias,
    text_proj,
    text_bias,
    cls_token,
    first_gain,
    first_shift,
    query_proj,
    query_bias,
    key_proj,
    value_proj,
    value_bias,
    output_proj,
    output_bias,
    second_gain,
    second_shift,
    hidden_proj,
    hidden_bias,
    return_proj,
    return_bias,
):
    shards = (
        image_proj,
        image_bias,
        text_proj,
        text_bias,
        cls_token,
        first_gain,
        first_shift,
        query_proj,
        query_bias,
        key_proj,
        value_proj,
        value_bias,
        output_proj,
        output_bias,
        second_gain,
        second_shift,
        hidden_proj,
        hidden_bias,
        return_proj,
        return_bias,
    )
    fits = chips == 16 and cores == 2 and image_states.shape == (1, IMAGE, WIDTH)
    if fits and text_states.shape == (1, TEXTS, WIDTH) and hidden_proj.shape == (48, HIDDEN):
        image, text, cot = image_states[0], text_states[0], cotangent[0]
        return by_kernels(shards, image, text, size_group, caption_len, cot)
    weights = gather_any(shards)
    results, summed = [], None
    for item in range(image_states.shape[0]):
        image_rows, text_rows = image_states[item], text_states[item]
        code, length = size_group[item], caption_len[item]
        result, kept_rows = item_forward(weights, image_rows, text_rows, code, length)
        image_grad, text_grad, grads = item_backward(
            weights, image_rows, text_rows, code, length, kept_rows, cotangent[item]
        )
        results.append((result, image_grad, text_grad))
        summed = grads if summed is None else jax.tree.map(jnp.add, summed, grads)
    owned = scatter_any(summed)
    return tuple(jnp.stack(parts) for parts in zip(*results)) + owned


def solution(mesh):
    placed = (
        P(("fsdp", "dp"), None, None),
        P(("fsdp", "dp"), None, None),
        P(("fsdp", "dp")),
        P(("fsdp", "dp")),
        P(("fsdp", "dp"), None, None),
        P("fsdp", None),
        P("fsdp"),
        P("fsdp", None),
        P("fsdp"),
        P("fsdp"),
        P("fsdp"),
        P("fsdp"),
        P("fsdp", None),
        P("fsdp"),
        P("fsdp", None),
        P("fsdp", None),
        P("fsdp"),
        P("fsdp", None),
        P("fsdp"),
        P("fsdp"),
        P("fsdp"),
        P("fsdp", None),
        P("fsdp"),
        P("fsdp", None),
        P("fsdp"),
    )
    chips, cores = mesh.shape["fsdp"], mesh.shape["dp"]
    return jax.shard_map(
        functools.partial(on_device, chips, cores),
        mesh=mesh,
        in_specs=placed,
        out_specs=(
            P(("fsdp", "dp"), None, None),
            P(("fsdp", "dp"), None, None),
            P(("fsdp", "dp"), None, None),
            P("fsdp", None),
            P("fsdp"),
            P("fsdp", None),
            P("fsdp"),
            P("fsdp"),
            P("fsdp"),
            P("fsdp"),
            P("fsdp", None),
            P("fsdp"),
            P("fsdp", None),
            P("fsdp", None),
            P("fsdp"),
            P("fsdp", None),
            P("fsdp"),
            P("fsdp"),
            P("fsdp"),
            P("fsdp", None),
            P("fsdp"),
            P("fsdp", None),
            P("fsdp"),
        ),
        check_vma=False,
    )
```

```python
import functools
import math

import jax
import jax.numpy as jnp
from jax import lax
from jax.experimental import pallas as pl
from jax.experimental.pallas import tpu as pltpu
from jax.sharding import PartitionSpec as P

HEADS = 12
HEAD_DIM = 64
PATCH_BIG = 325
PATCH_SMALL = 197


EPSILON = 1e-06
NEGATIVE = -1e30


def matmul(left, right):
    return jnp.dot(left, right, preferred_element_type=jnp.float32)


def left_product(left, right):
    return lax.dot_general(
        left, right, (((0,), (0,)), ((), ())), preferred_element_type=jnp.float32
    )


def right_product(left, right):
    return lax.dot_general(
        left, right, (((1,), (1,)), ((), ())), preferred_element_type=jnp.float32
    )


def to_low(values):
    return values.astype(jnp.bfloat16)


def column_sum(values):
    return jnp.sum(values.astype(jnp.float32), 0)


def gelu_exact(values):
    return jax.nn.gelu(values, approximate=False)


def layer_norm(values, gain, shift):
    centered = values - jnp.mean(values, -1, keepdims=True)
    scaled = centered * lax.rsqrt(jnp.mean(centered * centered, -1, keepdims=True) + EPSILON)
    return scaled * gain + shift


def key_mask(size_code, length, row_count):
    position = jnp.arange(row_count, dtype=jnp.int32)
    patches = jnp.where(size_code == 1, PATCH_BIG, PATCH_SMALL).astype(jnp.int32)
    image_live = (position >= 1) & (position <= patches)
    text_live = (position >= 1 + PATCH_BIG) & (position < 1 + PATCH_BIG + length)
    return (position == 0) | image_live | text_live


def head_slice(source, offset, span_width, per_group):
    part = lax.dynamic_slice_in_dim(source, offset, span_width, 1)
    return part.reshape(source.shape[0], per_group, HEAD_DIM)


def attend_forward(queries, keys_all, values_all, key_live):
    row_count = queries.shape[0]
    per_group = math.gcd(HEADS, 4)
    span_width = per_group * HEAD_DIM
    factor = HEAD_DIM ** (-0.5)

    def one_group(group_index, running):
        attended, totals = running
        offset = group_index * span_width
        query_part = head_slice(queries, offset, span_width, per_group)
        key_part = head_slice(keys_all, offset, span_width, per_group)
        value_part = head_slice(values_all, offset, span_width, per_group)
        scores = (
            jnp.einsum("qhd,khd->hqk", query_part, key_part, preferred_element_type=jnp.float32)
            * factor
        )
        scores = jnp.where(key_live, scores, NEGATIVE)
        row_top = jnp.max(scores, -1, keepdims=True)
        exps = jnp.exp(scores - row_top)
        row_total = jnp.sum(exps, -1, keepdims=True)
        prob_rows = to_low(exps / row_total)
        mixed_heads = jnp.einsum(
            "hqk,khd->qhd", prob_rows, value_part, preferred_element_type=jnp.float32
        )
        attended = lax.dynamic_update_slice_in_dim(
            attended, to_low(mixed_heads.reshape(row_count, span_width)), offset, 1
        )
        log_total = (row_top + jnp.log(row_total))[:, :, 0]
        totals = lax.dynamic_update_slice_in_dim(totals, log_total, group_index * per_group, 0)
        return (attended, totals)

    initial = (
        jnp.zeros((row_count, HEADS * HEAD_DIM), jnp.bfloat16),
        jnp.zeros((HEADS, row_count), jnp.float32),
    )
    return lax.fori_loop(0, HEADS // per_group, one_group, initial)


def attend_backward(queries, keys_all, values_all, key_live, totals, incoming):
    row_count = queries.shape[0]
    per_group = math.gcd(HEADS, 4)
    span_width = per_group * HEAD_DIM
    factor = HEAD_DIM ** (-0.5)

    def one_group(group_index, running):
        query_grad, key_grad, value_grad = running
        offset = group_index * span_width
        query_part = head_slice(queries, offset, span_width, per_group)
        key_part = head_slice(keys_all, offset, span_width, per_group)
        value_part = head_slice(values_all, offset, span_width, per_group)
        incoming_part = head_slice(incoming, offset, span_width, per_group)
        log_total = lax.dynamic_slice_in_dim(totals, group_index * per_group, per_group, 0)
        scores = (
            jnp.einsum("qhd,khd->hqk", query_part, key_part, preferred_element_type=jnp.float32)
            * factor
        )
        scores = jnp.where(key_live, scores, NEGATIVE)
        prob_rows = jnp.exp(scores - log_total[:, :, None])
        value_part_grad = jnp.einsum(
            "hqk,qhd->khd", to_low(prob_rows), incoming_part, preferred_element_type=jnp.float32
        )
        prob_grad = jnp.einsum(
            "qhd,khd->hqk", incoming_part, value_part, preferred_element_type=jnp.float32
        )
        score_grad = to_low(
            prob_rows * (prob_grad - jnp.sum(prob_rows * prob_grad, -1, keepdims=True))
        )
        query_part_grad = (
            jnp.einsum("hqk,khd->qhd", score_grad, key_part, preferred_element_type=jnp.float32)
            * factor
        )
        key_part_grad = (
            jnp.einsum("hqk,qhd->khd", score_grad, query_part, preferred_element_type=jnp.float32)
            * factor
        )
        query_grad = lax.dynamic_update_slice_in_dim(
            query_grad, to_low(query_part_grad.reshape(row_count, span_width)), offset, 1
        )
        key_grad = lax.dynamic_update_slice_in_dim(
            key_grad, to_low(key_part_grad.reshape(row_count, span_width)), offset, 1
        )
        value_grad = lax.dynamic_update_slice_in_dim(
            value_grad, to_low(value_part_grad.reshape(row_count, span_width)), offset, 1
        )
        return (query_grad, key_grad, value_grad)

    empty_grad = jnp.zeros((row_count, HEADS * HEAD_DIM), jnp.bfloat16)
    return lax.fori_loop(0, HEADS // per_group, one_group, (empty_grad, empty_grad, empty_grad))


def item_forward(weights, image_rows, text_rows, size_code, length):
    (
        image_proj,
        image_bias,
        text_proj,
        text_bias,
        cls_token,
        first_gain,
        first_shift,
        query_proj,
        query_bias,
        key_proj,
        value_proj,
        value_bias,
        output_proj,
        output_bias,
        second_gain,
        second_shift,
        hidden_proj,
        hidden_bias,
        return_proj,
        return_bias,
    ) = weights
    image_part = matmul(image_rows, image_proj) + image_bias.astype(jnp.float32)
    text_part = matmul(text_rows, text_proj) + text_bias.astype(jnp.float32)
    embedded = jnp.concatenate([cls_token.astype(jnp.float32)[None, :], image_part, text_part], 0)
    normed = to_low(
        layer_norm(embedded, first_gain.astype(jnp.float32), first_shift.astype(jnp.float32))
    )
    queries = to_low(matmul(normed, query_proj) + query_bias.astype(jnp.float32))
    keys_all = to_low(matmul(normed, key_proj))
    values_all = to_low(matmul(normed, value_proj) + value_bias.astype(jnp.float32))
    key_live = key_mask(size_code, length, embedded.shape[0])
    attended, totals = attend_forward(queries, keys_all, values_all, key_live)
    middle = embedded + matmul(attended, output_proj) + output_bias.astype(jnp.float32)
    second = to_low(
        layer_norm(middle, second_gain.astype(jnp.float32), second_shift.astype(jnp.float32))
    )
    inner_pre = matmul(second, hidden_proj) + hidden_bias.astype(jnp.float32)
    activated = to_low(gelu_exact(inner_pre))
    result = middle + matmul(activated, return_proj) + return_bias.astype(jnp.float32)
    kept_rows = (
        embedded,
        normed,
        queries,
        keys_all,
        values_all,
        attended,
        totals,
        middle,
        second,
        inner_pre,
        activated,
    )
    return (to_low(result), kept_rows)


def item_backward(weights, image_rows, text_rows, size_code, length, kept_rows, out_grad):
    (
        image_proj,
        image_bias,
        text_proj,
        text_bias,
        cls_token,
        first_gain,
        first_shift,
        query_proj,
        query_bias,
        key_proj,
        value_proj,
        value_bias,
        output_proj,
        output_bias,
        second_gain,
        second_shift,
        hidden_proj,
        hidden_bias,
        return_proj,
        return_bias,
    ) = weights
    (
        embedded,
        normed,
        queries,
        keys_all,
        values_all,
        attended,
        totals,
        middle,
        second,
        inner_pre,
        activated,
    ) = kept_rows
    grad_return_proj = left_product(activated, out_grad)
    grad_return_bias = column_sum(out_grad)
    activated_grad = right_product(out_grad, return_proj)
    unused_value, gelu_pull = jax.vjp(gelu_exact, inner_pre)
    inner_grad = to_low(gelu_pull(activated_grad)[0])
    grad_hidden_proj = left_product(second, inner_grad)
    grad_hidden_bias = column_sum(inner_grad)
    second_grad = right_product(inner_grad, hidden_proj)
    unused_norm, second_pull = jax.vjp(
        layer_norm, middle, second_gain.astype(jnp.float32), second_shift.astype(jnp.float32)
    )
    middle_part, grad_second_gain, grad_second_shift = second_pull(second_grad)
    middle_grad = out_grad.astype(jnp.float32) + middle_part
    branch_grad = to_low(middle_grad)
    grad_output_proj = left_product(attended, branch_grad)
    grad_output_bias = column_sum(branch_grad)
    attended_grad = to_low(right_product(branch_grad, output_proj))
    key_live = key_mask(size_code, length, embedded.shape[0])
    query_grad, key_grad, value_grad = attend_backward(
        queries, keys_all, values_all, key_live, totals, attended_grad
    )
    grad_query_proj = left_product(normed, query_grad)
    grad_query_bias = column_sum(query_grad)
    grad_key_proj = left_product(normed, key_grad)
    grad_value_proj = left_product(normed, value_grad)
    grad_value_bias = column_sum(value_grad)
    normed_grad = (
        right_product(query_grad, query_proj)
        + right_product(key_grad, key_proj)
        + right_product(value_grad, value_proj)
    )
    unused_first, first_pull = jax.vjp(
        layer_norm, embedded, first_gain.astype(jnp.float32), first_shift.astype(jnp.float32)
    )
    embedded_part, grad_first_gain, grad_first_shift = first_pull(normed_grad)
    embedded_grad = middle_grad + embedded_part
    grad_cls_token = embedded_grad[0]
    image_low = to_low(embedded_grad[1 : 1 + PATCH_BIG])
    text_low = to_low(embedded_grad[1 + PATCH_BIG :])
    image_grad = right_product(image_low, image_proj)
    text_grad = right_product(text_low, text_proj)
    grad_image_proj = left_product(image_rows, image_low)
    grad_image_bias = column_sum(image_low)
    grad_text_proj = left_product(text_rows, text_low)
    grad_text_bias = column_sum(text_low)
    grads = (
        grad_image_proj,
        grad_image_bias,
        grad_text_proj,
        grad_text_bias,
        grad_cls_token,
        grad_first_gain,
        grad_first_shift,
        grad_query_proj,
        grad_query_bias,
        grad_key_proj,
        grad_value_proj,
        grad_value_bias,
        grad_output_proj,
        grad_output_bias,
        grad_second_gain,
        grad_second_shift,
        grad_hidden_proj,
        grad_hidden_bias,
        grad_return_proj,
        grad_return_bias,
    )
    return (image_grad, text_grad, grads)


VECTORS = (1, 3, 4, 5, 6, 8, 11, 13, 14, 15, 19, 17)
LANES = 384
VEC_ROWS = 16
GATHER_CHUNKS = ((0, 2, "vec", 7, 9, 10), (12, "low"), ("high", 18))
SCATTER_CHUNKS = ((18, 16), (12, 7, 9, 10), (0, 2, "vec"))
BOTH = ("fsdp", "dp")
WIDTH = 768
HIDDEN = 3072
IMAGE = 325
TEXTS = 513
ROWS = 839
KEYS = 848
PADDED = 896
LOW = jnp.bfloat16
FULL = jnp.float32
COST_SCALE = 0.3
FAST = pl.BlockSpec(memory_space=pltpu.VMEM)
SCALARS = pl.BlockSpec(memory_space=pltpu.SMEM)


def cost(micros):
    return pl.CostEstimate(
        flops=int(micros * COST_SCALE * 1e9), bytes_accessed=1024, transcendentals=0
    )


class Place:
    def __init__(self):
        self.core = lax.axis_index("dp")
        chip = lax.axis_index("fsdp")
        self.x, self.y, self.z = chip & 1, (chip >> 1) & 1, chip >> 2
        self.scalars = jnp.stack([self.core, self.x, self.y, self.z]).astype(jnp.int32)


def shape(dims, kind=LOW):
    return jax.ShapeDtypeStruct(dims, kind)


def call(kernel, micros, outs, *args, scratch=(), limit=60):
    specs = [SCALARS if a.dtype == jnp.int32 else FAST for a in args]
    return pl.pallas_call(
        kernel,
        out_shape=tuple(outs),
        in_specs=specs,
        out_specs=tuple(FAST for _ in outs),
        scratch_shapes=list(scratch),
        compiler_params=pltpu.CompilerParams(vmem_limit_bytes=limit * 2**20),
        cost_estimate=cost(micros),
    )(*args)


def after(values, *others):
    return lax.optimization_barrier((values, others))[0]


def settle(*values):
    return lax.optimization_barrier(values)


def swap_cores(values):
    with jax.named_scope("between_cores"):
        return lax.ppermute(values, "dp", [(0, 1), (1, 0)])


def to_chip(values, mask_zero, mask_one):
    pairs = []
    for chip in range(16):
        pairs.append((chip * 2, (chip ^ mask_zero) * 2))
        pairs.append((chip * 2 + 1, (chip ^ mask_one) * 2 + 1))
    with jax.named_scope(f"chips_{mask_zero}_{mask_one}"):
        return lax.ppermute(values, BOTH, pairs)


def sub_blocks(index):
    return 4 if index == 16 else 1


def block_rows(index):
    return {"vec": VEC_ROWS, 16: 192, 18: 192, "low": 96, "high": 96}.get(index, 48)


def pack_kernel(chunk, at_ref, *refs):
    core = at_ref[0]
    count = len(chunk) + (11 if "vec" in chunk else 0)
    ins, out = refs[:count], refs[count]
    offset = 0
    order = [i for i in chunk if i != "vec"]
    for index in chunk:
        if index == "vec":
            rows = refs[-1]
            rows[...] = jnp.zeros_like(rows)
            for row in range(12):
                source = ins[len(order) + row]
                rows[row : row + 1, 0 : source.shape[1]] = source[...].astype(FULL)
            out[offset : offset + VEC_ROWS, :] = rows[...].astype(LOW)
            offset += VEC_ROWS
            continue
        parts = {"low": (4, (0, 1)), "high": (4, (2, 3))}.get(index, (1, (0,)))
        source = ins[order.index(index)]
        rows = source.shape[0]
        for s in parts[1]:
            first = pl.multiple_of((core * parts[0] + s) * LANES, LANES)
            out[offset : offset + rows, :] = source[:, pl.ds(first, LANES)]
            offset += rows


def pack(place, shards, chunk):
    rows = sum(block_rows(i) for i in chunk)
    ins = [shards[16 if i in ("low", "high") else i] for i in chunk if i != "vec"]
    scratch = ()
    if "vec" in chunk:
        ins += [shards[i].reshape(1, -1) for i in VECTORS]
        scratch = (pltpu.VMEM((VEC_ROWS, LANES), FULL),)
    kernel = functools.partial(pack_kernel, chunk)
    return call(kernel, 1, [shape((rows, LANES))], place.scalars, *ins, scratch=scratch)[0]


def all_z(own):
    return [own] + [to_chip(own, 4 * s, 4 * s) for s in (1, 2, 3)]


def unpack(at_ref, pieces, targets):
    core, x, y, z = at_ref[0], at_ref[1], at_ref[2], at_ref[3]

    def fill(zero_s, zero_r, one_s, one_r):
        for offset, blocks, count, out in targets:
            rows = out.shape[3]
            for n, s in enumerate(blocks):
                first = slice(offset + n * rows, offset + (n + 1) * rows)
                left = slice(s * LANES, (s + 1) * LANES)
                right = slice((count + s) * LANES, (count + s + 1) * LANES)
                for far in range(4):
                    plane = z ^ far
                    for b in range(2):
                        out[plane, y, x ^ b, :, left] = zero_s[b, far, first, :]
                        out[plane, 1 - y, x ^ b, :, left] = zero_r[b, far, first, :]
                        if count:
                            out[plane, y ^ b, x, :, right] = one_s[b, far, first, :]
                            out[plane, y ^ b, 1 - x, :, right] = one_r[b, far, first, :]

    s8, r8, s8p, r8p = pieces

    @pl.when(core == 0)
    def _():
        fill(s8, r8, s8p, r8p)

    @pl.when(core == 1)
    def _():
        fill(s8p, r8p, s8, r8)


def square(ref):
    return ref[...].reshape(16 * ref.shape[3], ref.shape[4])


def row_chunks(step, total=ROWS):
    return [slice(a, min(a + step, total)) for a in range(0, total, step)]


def standard(values):
    centered = values - jnp.mean(values, -1, keepdims=True)
    scale = lax.rsqrt(jnp.mean(centered * centered, -1, keepdims=True) + EPSILON)
    return centered * scale, scale


def norm_back(values, gain, incoming):
    unit, scale = standard(values)
    f = incoming * gain
    back = (f - jnp.mean(f, -1, keepdims=True) - unit * jnp.mean(f * unit, -1, keepdims=True)) * scale
    return back, unit


def sum_rows(values):
    return jnp.sum(values.astype(FULL), 0, keepdims=True)


def embed_kernel(
    at, image, text, s8, r8, s8p, r8p,
    w_image, w_text, wq, wk, wv, vec, hid, embedded, normed, q, k, v, small,
):
    unpack(
        at,
        (s8, r8, s8p, r8p),
        (
            (0, (0,), 1, w_image),
            (48, (0,), 1, w_text),
            (96, (0,), 0, small),
            (112, (0,), 1, wq),
            (160, (0,), 1, wk),
            (208, (0,), 1, wv),
        ),
    )
    for f in range(16):
        piece = small[f >> 2, (f >> 1) & 1, f & 1].astype(FULL)
        vec[:, f * 48 : (f + 1) * 48] = piece[:, :48]
        hid[:, f * 192 : (f + 1) * 192] = piece[11:12, :192]
    embedded[0:1, :] = vec[2:3, :]
    embedded[1 : 1 + IMAGE, :] = matmul(image[...], square(w_image)) + vec[0:1, :]
    embedded[1 + IMAGE : ROWS, :] = matmul(text[...], square(w_text)) + vec[1:2, :]
    for rows in row_chunks(64):
        unit, unused_scale = standard(embedded[rows, :])
        normed[rows, :] = to_low(unit * vec[3:4, :] + vec[4:5, :])
    for out in (q, k, v):
        out[832:PADDED, :] = jnp.zeros((PADDED - 832, WIDTH), LOW)
    rows = normed[...]
    low = to_low(matmul(rows, square(wq)) + vec[5:6, :])
    q[0:ROWS, :] = to_low(low.astype(FULL) * HEAD_DIM**-0.5)
    k[0:ROWS, :] = to_low(matmul(rows, square(wk)))
    v[0:ROWS, :] = to_low(matmul(rows, square(wv)) + vec[6:7, :])


def embed(place, image, text, pieces):
    outs = [shape((4, 2, 2, 48, WIDTH))] * 5
    outs += [shape((VEC_ROWS, WIDTH), FULL), shape((1, HIDDEN), FULL)]
    outs += [shape((ROWS, WIDTH), FULL), shape((ROWS, WIDTH))] + [shape((PADDED, WIDTH))] * 3
    scratch = (pltpu.VMEM((4, 2, 2, VEC_ROWS, LANES), LOW),)
    return call(embed_kernel, 12, outs, place.scalars, image, text, *pieces, scratch=scratch)


def mask_column(live):
    position = lax.broadcasted_iota(jnp.int32, (KEYS, 1), 0)
    patches = jnp.where(live[0] == 1, PATCH_BIG, PATCH_SMALL).astype(jnp.int32)
    image_live = (position >= 1) & (position <= patches)
    text_live = (position >= 1 + PATCH_BIG) & (position < 1 + PATCH_BIG + live[1])
    return jnp.where((position == 0) | image_live | text_live, 0.0, NEGATIVE).astype(FULL)


def one_head(ref_value, head):
    lane = lax.broadcasted_iota(jnp.int32, ref_value.shape, 1)
    keep = (lane < HEAD_DIM) if head == 0 else (lane >= HEAD_DIM)
    return jnp.where(keep, ref_value, jnp.zeros_like(ref_value))


def across(values):
    return jnp.transpose(values.astype(FULL))


def fold_rows(values, op):
    return op(values.reshape(values.shape[0] // 8, 8, values.shape[1]), 0)


def attend_kernel(live, q, k, v, attended, totals, keys, scores, probs, mixed):
    bias = mask_column(live)
    for h in range(2):
        keys[h] = one_head(k[0:KEYS, :], h)
    values_t = to_low(across(v[0:KEYS, :]))
    totals[...] = jnp.zeros_like(totals)
    parts = [(piece, h) for piece in row_chunks(256, PADDED) for h in range(2)]
    tiles = row_chunks(128, KEYS)
    tops = {}

    def score(n, tile):
        piece, h = parts[n]
        made = right_product(keys[h, tile, :], q[piece, :]) + bias[tile, :]
        scores[n % 2, tile, 0 : made.shape[1]] = made
        top = fold_rows(made, jnp.max)
        tops[n] = jnp.maximum(tops[n], top) if n in tops else top

    for tile in tiles:
        score(0, tile)
    for n, (piece, h) in enumerate(parts):
        width = piece.stop - piece.start
        top = jnp.max(tops[n], 0, keepdims=True)
        total = jnp.zeros((8, width), FULL)
        for tile in tiles:
            if n + 1 < len(parts):
                score(n + 1, tile)
            exps = jnp.exp(scores[n % 2, tile, 0:width] - top)
            total = total + fold_rows(exps, jnp.sum)
            probs[n % 2, tile, 0:width] = to_low(exps)
        total = jnp.sum(total, 0, keepdims=True)
        rows = slice(h * HEAD_DIM, (h + 1) * HEAD_DIM)
        out = matmul(values_t[rows, :], probs[n % 2, :, 0:width])
        mixed[rows, piece] = out * (1.0 / total)
        totals[0, h : h + 1, piece] = top + jnp.log(total)
    attended[...] = to_low(jnp.transpose(mixed[...]))


def attend(live, q, k, v, first, count, earlier=()):
    spec = pl.BlockSpec((PADDED, 2 * HEAD_DIM), lambda i: (0, i + first))
    anywhere = pl.BlockSpec(memory_space=pl.ANY)

    def kernel(live, q, k, v, *refs):
        attend_kernel(live, q, k, v, *refs[len(earlier) :])

    return pl.pallas_call(
        kernel,
        grid=(count,),
        out_shape=(shape((PADDED, WIDTH)), shape((HEADS // 2, 8, PADDED), FULL)),
        in_specs=[SCALARS] + [spec] * 3 + [anywhere] * len(earlier),
        out_specs=(spec, pl.BlockSpec((1, 8, PADDED), lambda i: (i + first, 0, 0))),
        scratch_shapes=[
            pltpu.VMEM((2, KEYS, 2 * HEAD_DIM), LOW),
            pltpu.VMEM((2, KEYS, 256), FULL),
            pltpu.VMEM((2, KEYS, 256), LOW),
            pltpu.VMEM((2 * HEAD_DIM, PADDED), FULL),
        ],
        input_output_aliases={4 + n: n for n in range(len(earlier))},
        compiler_params=pltpu.CompilerParams(vmem_limit_bytes=60 * 2**20),
        cost_estimate=cost(3 * count),
    )(live, q, k, v, *earlier)


def attend_back_kernel(
    live, q, k, v, incoming, attended, totals, q_grad, k_grad, v_grad,
    keys, values, probs, score_grads, mixed,
):
    bias = mask_column(live)
    for h in range(2):
        keys[h] = one_head(k[0:KEYS, :], h)
        values[h] = one_head(v[0:KEYS, :], h)
    keys_t = to_low(across(k[0:KEYS, :]))
    product = jnp.transpose(incoming[...].astype(FULL) * attended[...].astype(FULL))
    for h in range(2):
        rows = slice(h * HEAD_DIM, (h + 1) * HEAD_DIM)
        along = jnp.sum(product[rows], 0, keepdims=True)
        for piece in row_chunks(256, PADDED):
            for tile in row_chunks(256, KEYS):
                made = right_product(keys[h, tile, :], q[piece, :]) + bias[tile, :]
                prob = jnp.exp(made - totals[0, h : h + 1, piece])
                prob_grad = right_product(values[h, tile, :], incoming[piece, :])
                probs[h, tile, piece] = to_low(prob)
                score_grads[h, tile, piece] = to_low(prob * (prob_grad - along[:, piece]))
        mixed[rows, :] = matmul(keys_t[rows, :], score_grads[h])
    lane = lax.broadcasted_iota(jnp.int32, (KEYS, 2 * HEAD_DIM), 1) < HEAD_DIM
    for out, left, right in ((k_grad, score_grads, q), (v_grad, probs, incoming)):
        right = right[...]
        out[0:KEYS, :] = to_low(jnp.where(lane, matmul(left[0], right), matmul(left[1], right)))
    q_grad[...] = to_low(jnp.transpose(mixed[...]) * HEAD_DIM**-0.5)


def attend_back(live, q, k, v, incoming, attended, totals):
    spec = pl.BlockSpec((PADDED, 2 * HEAD_DIM), lambda i: (0, i))
    return pl.pallas_call(
        attend_back_kernel,
        grid=(HEADS // 2,),
        out_shape=(shape((PADDED, WIDTH)),) * 3,
        in_specs=[SCALARS] + [spec] * 5 + [pl.BlockSpec((1, 8, PADDED), lambda i: (i, 0, 0))],
        out_specs=(spec,) * 3,
        scratch_shapes=[
            pltpu.VMEM((2, KEYS, 2 * HEAD_DIM), LOW),
            pltpu.VMEM((2, KEYS, 2 * HEAD_DIM), LOW),
            pltpu.VMEM((2, KEYS, PADDED), LOW),
            pltpu.VMEM((2, KEYS, PADDED), LOW),
            pltpu.VMEM((2 * HEAD_DIM, PADDED), FULL),
        ],
        compiler_params=pltpu.CompilerParams(vmem_limit_bytes=60 * 2**20),
        cost_estimate=cost(28),
    )(live, q, k, v, incoming, attended, totals)


def middle_kernel(
    at, attended, embedded, vec, s8, r8, s8p, r8p, s_hi, r_hi, sp_hi, rp_hi,
    w_out, w_hid, middle, second,
):
    unpack(at, (s8, r8, s8p, r8p), ((0, (0,), 1, w_out), (48, (0, 1), 4, w_hid)))
    unpack(at, (s_hi, r_hi, sp_hi, rp_hi), ((0, (2, 3), 4, w_hid),))
    middle[...] = embedded[...] + matmul(attended[0:ROWS, :], square(w_out)) + vec[7:8, :]
    for rows in row_chunks(64):
        unit, unused_scale = standard(middle[rows, :])
        second[rows, :] = to_low(unit * vec[8:9, :] + vec[9:10, :])


def middle_of(place, attended, embedded, vec, pieces):
    outs = [
        shape((4, 2, 2, 48, WIDTH)),
        shape((4, 2, 2, 48, HIDDEN)),
        shape((ROWS, WIDTH), FULL),
        shape((ROWS, WIDTH)),
    ]
    return call(middle_kernel, 8, outs, place.scalars, attended, embedded, vec, *pieces)


def gelu_parts(u):
    cumulative = 0.5 * (1.0 + lax.erf(u * (2.0**-0.5)))
    slope = cumulative + u * (jnp.exp(-0.5 * u * u) * (2.0 * math.pi) ** -0.5)
    return u * cumulative, slope


def feed_kernel(
    at, second, cot, middle, vec, w_hid, hid, s8, r8, s8p, r8p,
    layer_out, second_grad, ret_keep, ret_send, hid_keep, hid_send, hid_sum, ret_sum,
    w_ret, act, inner, total,
):
    step = pl.program_id(0)
    core, x, y = at[0], at[1], at[2]

    def fill(zero_s, zero_r, one_s, one_r):
        for b in range(2):
            w_ret[y, x ^ b, :, 0:LANES] = zero_s[b, 0]
            w_ret[1 - y, x ^ b, :, 0:LANES] = zero_r[b, 0]
            w_ret[y ^ b, x, :, LANES:] = one_s[b, 0]
            w_ret[y ^ b, 1 - x, :, LANES:] = one_r[b, 0]

    @pl.when(core == 0)
    def _():
        fill(s8, r8, s8p, r8p)

    @pl.when(core == 1)
    def _():
        fill(s8p, r8p, s8, r8)

    ret = w_ret[...].reshape(WIDTH, WIDTH)
    inward = w_hid[...]
    for rows in row_chunks(432):
        pre = matmul(second[rows, :], inward) + hid[...]
        back = right_product(cot[rows, :], ret)
        value, slope = gelu_parts(pre)
        act[rows, :] = to_low(value)
        inner[rows, :] = to_low(back * slope)
        out = matmul(act[rows, :], ret)
        back = right_product(inner[rows, :], inward)

        @pl.when(step == 0)
        def _():
            total[rows, :] = out
            second_grad[rows, :] = back

        @pl.when(step > 0)
        def _():
            total[rows, :] += out
            second_grad[rows, :] += back

    hid_sum[...] = sum_rows(inner[...])
    ret_grad = to_low(left_product(act[...], cot[...])).reshape(4, 192, WIDTH)
    hid_grad = to_low(left_product(second[...], inner[...])).reshape(16, 48, WIDTH)

    @pl.when(core == 0)
    def _():
        ret_keep[...] = ret_grad[:, :, 0:LANES]
        ret_send[...] = ret_grad[:, :, LANES:]

    @pl.when(core == 1)
    def _():
        ret_keep[...] = ret_grad[:, :, LANES:]
        ret_send[...] = ret_grad[:, :, 0:LANES]

    @pl.when(step < 2)
    def _():
        hid_send[:, 0:48, :] = hid_grad[:, :, 0:LANES]
        hid_send[:, 48:96, :] = hid_grad[:, :, LANES:]

    @pl.when(step >= 2)
    def _():
        hid_keep[:, 0:48, :] = hid_grad[:, :, 0:LANES]
        hid_keep[:, 48:96, :] = hid_grad[:, :, LANES:]

    @pl.when(step == 3)
    def _():
        layer_out[...] = to_low(middle[...] + total[...] + vec[10:11, :])
        ret_sum[...] = sum_rows(cot[...])


def feed(place, second, cot, middle, vec, w_hid, hid, pieces):
    def column(i, at):
        half = jnp.where(i < 2, 1 - at[0], at[0])
        return 2 * half + lax.rem(i, 2)

    def whole(dims):
        return pl.BlockSpec(dims, lambda i, at: (0,) * len(dims))

    piece = pl.BlockSpec((2, 1, 192, LANES), lambda i, at: (0, column(i, at) ^ at[3], 0, 0))
    ret_spec = pl.BlockSpec((4, 192, LANES), lambda i, at: (column(i, at), 0, 0))
    outs = (
        shape((ROWS, WIDTH)),
        shape((ROWS, WIDTH), FULL),
        shape((16, 192, LANES)),
        shape((16, 192, LANES)),
        shape((16, 192, LANES)),
        shape((16, 192, LANES)),
        shape((1, HIDDEN), FULL),
        shape((1, WIDTH), FULL),
    )
    grid = pltpu.PrefetchScalarGridSpec(
        num_scalar_prefetch=1,
        grid=(4,),
        in_specs=[
            whole((ROWS, WIDTH)),
            whole((ROWS, WIDTH)),
            whole((ROWS, WIDTH)),
            whole((VEC_ROWS, WIDTH)),
            pl.BlockSpec((WIDTH, WIDTH), lambda i, at: (0, column(i, at))),
            pl.BlockSpec((1, WIDTH), lambda i, at: (0, column(i, at))),
            piece,
            piece,
            piece,
            piece,
        ],
        out_specs=(
            whole((ROWS, WIDTH)),
            whole((ROWS, WIDTH)),
            ret_spec,
            ret_spec,
            pl.BlockSpec((16, 96, LANES), lambda i, at: (0, jnp.maximum(i - 2, 0), 0)),
            pl.BlockSpec((16, 96, LANES), lambda i, at: (0, jnp.minimum(i, 1), 0)),
            pl.BlockSpec((1, WIDTH), lambda i, at: (0, column(i, at))),
            whole((1, WIDTH)),
        ),
        scratch_shapes=[
            pltpu.VMEM((2, 2, 192, WIDTH), LOW),
            pltpu.VMEM((ROWS, WIDTH), LOW),
            pltpu.VMEM((ROWS, WIDTH), LOW),
            pltpu.VMEM((ROWS, WIDTH), FULL),
        ],
    )
    return pl.pallas_call(
        feed_kernel,
        grid_spec=grid,
        out_shape=outs,
        compiler_params=pltpu.CompilerParams(vmem_limit_bytes=60 * 2**20),
        cost_estimate=cost(40),
    )(place.scalars, second, cot, middle, vec, w_hid, hid, *pieces)


def branch_kernel(middle, second_grad, cot, vec, w_out, middle_grad, branch, incoming, sums):
    parts = [jnp.zeros((1, WIDTH), FULL)] * 3
    for rows in row_chunks(64):
        e = second_grad[rows, :]
        back, unit = norm_back(middle[rows, :], vec[8:9, :], e)
        grad = cot[rows, :].astype(FULL) + back
        middle_grad[rows, :] = grad
        branch[rows, :] = to_low(grad)
        for n, term in enumerate((e * unit, e, to_low(grad))):
            parts[n] = parts[n] + sum_rows(term)
    for n in range(3):
        sums[n : n + 1, :] = parts[n]
    incoming[832:PADDED, :] = jnp.zeros((PADDED - 832, WIDTH), LOW)
    incoming[0:ROWS, :] = to_low(right_product(branch[...], square(w_out)))


def branch_of(middle, second_grad, cot, vec, w_out):
    outs = [
        shape((ROWS, WIDTH), FULL),
        shape((ROWS, WIDTH)),
        shape((PADDED, WIDTH)),
        shape((8, WIDTH), FULL),
    ]
    return call(branch_kernel, 8, outs, middle, second_grad, cot, vec, w_out)


def both_halves(core, left_t, right_ref, first, keep, send, offset):
    for half, out in ((core, keep), (1 - core, send)):
        columns = pl.ds(pl.multiple_of(half * LANES, LANES), LANES)
        grad = matmul(left_t, right_ref[first, columns])
        out[:, offset : offset + 48, :] = to_low(grad).reshape(16, 48, LANES)


def square_grads_kernel(at, attended, branch, normed, dq, dk, dv, keep, send):
    rows = slice(0, ROWS)
    both_halves(at[0], jnp.transpose(attended[rows, :]), branch, rows, keep, send, 0)
    left_t = jnp.transpose(normed[...])
    for n, ref in enumerate((dq, dk, dv)):
        both_halves(at[0], left_t, ref, rows, keep, send, 48 * (n + 1))


def square_grads(place, attended, branch, normed, grads):
    outs = [shape((16, 192, LANES))] * 2
    return call(
        square_grads_kernel, 11, outs, place.scalars, attended, branch, normed, *grads
    )


def norm_one_kernel(
    dq, dk, dv, wq, wk, wv, embedded, middle_grad, vec, image_low, text_low, late, grad
):
    rows = slice(0, ROWS)
    grad[...] = (
        right_product(dq[rows, :], square(wq))
        + right_product(dk[rows, :], square(wk))
        + right_product(dv[rows, :], square(wv))
    )
    parts = [jnp.zeros((1, WIDTH), FULL)] * 4
    for piece in row_chunks(64):
        e = grad[piece, :]
        back, unit = norm_back(embedded[piece, :], vec[3:4, :], e)
        for n, term in enumerate((e * unit, e, dq[piece, :], dv[piece, :])):
            parts[n] = parts[n] + sum_rows(term)
        grad[piece, :] = middle_grad[piece, :] + back
    image_low[...] = to_low(grad[1 : 1 + IMAGE, :])
    text_low[...] = to_low(grad[1 + IMAGE : ROWS, :])
    late[...] = jnp.zeros_like(late)
    late[0:1, :] = grad[0:1, :]
    for n in range(4):
        late[n + 1 : n + 2, :] = parts[n]


def norm_one(grads, projs, embedded, middle_grad, vec):
    outs = [shape((IMAGE, WIDTH)), shape((TEXTS, WIDTH)), shape((8, WIDTH), FULL)]
    scratch = (pltpu.VMEM((ROWS, WIDTH), FULL),)
    return call(
        norm_one_kernel, 11, outs, *grads, *projs, embedded, middle_grad, vec, scratch=scratch
    )


def last_kernel(
    at, image, text, image_low, text_low, sums, hid_sum, ret_sum, late,
    keep, send, rows16, packed,
):
    both_halves(at[0], jnp.transpose(image[...]), image_low, slice(0, IMAGE), keep, send, 0)
    both_halves(at[0], jnp.transpose(text[...]), text_low, slice(0, TEXTS), keep, send, 48)
    rows16[...] = jnp.zeros_like(rows16)
    found = (
        sum_rows(image_low[...]), sum_rows(text_low[...]), late[0:1, :], late[1:2, :], late[2:3, :],
        late[3:4, :], late[4:5, :], sums[2:3, :], sums[0:1, :], sums[1:2, :], ret_sum[...],
    )
    for n, value in enumerate(found):
        rows16[n : n + 1, :] = value
    packed[...] = jnp.zeros_like(packed)
    for f in range(16):
        packed[f, :, 0:48] = rows16[:, f * 48 : (f + 1) * 48]
        packed[f, 11:12, 0:192] = hid_sum[:, f * 192 : (f + 1) * 192]
    low = to_low(packed[...])
    keep[:, 96:112, :] = low
    send[:, 96:112, :] = low


def last(place, image, text, image_low, text_low, sums, hid_sum, ret_sum, late):
    outs = [shape((16, 112, LANES)), shape((16, 112, LANES))]
    scratch = (pltpu.VMEM((VEC_ROWS, WIDTH), FULL), pltpu.VMEM((16, VEC_ROWS, LANES), FULL))
    return call(
        last_kernel, 5.5, outs, place.scalars, image, text, image_low, text_low, sums, hid_sum, ret_sum,
        late, scratch=scratch,
    )


def inputs_kernel(image_low, text_low, w_image, w_text, image_grad, text_grad):
    image_grad[:, 0, :] = right_product(image_low[...], square(w_image))
    text_grad[:, 0, :] = right_product(text_low[...], square(w_text))


def input_grads(image_low, text_low, w_image, w_text):
    outs = [shape((IMAGE, 1, WIDTH), FULL), shape((TEXTS, 1, WIDTH), FULL)]
    return call(inputs_kernel, 4.4, outs, image_low, text_low, w_image, w_text)


def add_low(*values):
    total = values[0].astype(FULL)
    for value in values[1:]:
        total = total + value.astype(FULL)
    return to_low(total)


def pick(values, at, axis):
    return lax.dynamic_index_in_dim(values, at, axis, keepdims=False)


class Scatter:
    def __init__(self, place, pairs):
        self.place = place
        self.kept = [keep for keep, unused_send in pairs]
        self.sent = [send for unused_keep, send in pairs]
        self.got = None

    def state(self):
        return self.kept, self.got

    def summed(self, q):
        parts = []
        for keep, more in zip(self.kept, self.swapped):
            keep, more = (pick(v.reshape(4, 4, v.shape[1], LANES), q, 1) for v in (keep, more))
            parts.append(keep.astype(FULL) + more.astype(FULL))
        return jnp.concatenate(parts, 1) if len(parts) > 1 else parts[0]

    def first(self):
        zero, x, y = self.place.core == 0, self.place.x, self.place.y
        self.swapped = self.got
        far = [jnp.where(zero, 2 * (1 - y) + s, 2 * s + (1 - x)) for s in (0, 1)]
        self.sent = jnp.stack([to_low(self.summed(q)) for q in far], 1)

    def second(self):
        zero, x, y = self.place.core == 0, self.place.x, self.place.y
        mine = jnp.where(zero, x, y)

        def added(s):
            near = self.summed(jnp.where(zero, 2 * y + s, 2 * s + x))
            return to_low(near + pick(self.got, s, 1).astype(FULL))

        self.sent, self.kept = added(1 - mine), added(mine)

    def third(self):
        z = self.place.z
        total = add_low(self.kept, self.got)
        self.kept = pick(total, z, 0)
        self.sent = [pick(total, z ^ s, 0) for s in (1, 2, 3)]

    def fourth(self):
        self.sent = self.kept = add_low(self.kept, *self.got)

    def swap(self):
        self.got = jax.tree.map(swap_cores, self.sent)

    def send_first(self):
        self.got = to_chip(self.sent, 2, 1)

    def send_second(self):
        self.got = to_chip(self.sent, 1, 2)

    def send_third(self, steps=(1, 2, 3)):
        self.got = [to_chip(self.sent[s - 1], 4 * s, 4 * s) for s in steps]

    def sides(self):
        zero = self.place.core == 0
        mine, other = self.kept, self.got
        return jnp.where(zero, mine, other).astype(FULL), jnp.where(zero, other, mine).astype(FULL)


def owned_rows(chunk, left, right):
    result, at = {}, 0
    for index in chunk:
        rows = block_rows(index)
        if index == "vec":
            for n, vector in enumerate(VECTORS):
                result[vector] = left[at + n, : 192 if vector == 17 else 48]
        else:
            count = sub_blocks(index)
            step = rows // count
            sides = [
                side[at + s * step : at + (s + 1) * step] for side in (left, right) for s in range(count)
            ]
            result[index] = jnp.concatenate(sides, 1)
        at += rows
    return result


def by_kernels(shards, image, text, size_code, length, cot):
    place = Place()
    live = jnp.concatenate([size_code, length]).astype(jnp.int32)
    own_one = pack(place, shards, GATHER_CHUNKS[0])

    z_one = all_z(own_one)
    owns = [pack(place, shards, chunk) for chunk in GATHER_CHUNKS[1:]]
    z_one, owns = settle(z_one, owns)

    z_one = jnp.stack(z_one)
    b_one, z_a, z_one, owns = settle(to_chip(z_one, 1, 2), all_z(owns[0]), z_one, owns)

    s_one, z_a = jnp.stack([z_one, b_one]), jnp.stack(z_a)
    r_one, sp_one, z_b, s_one, z_a = settle(
        to_chip(s_one, 2, 1), swap_cores(s_one), all_z(owns[1]), s_one, z_a
    )

    rp_one, b_a = swap_cores(r_one), to_chip(z_a, 1, 2)
    z_b = jnp.stack(z_b)
    b_b = to_chip(z_b, 1, 2)
    w_image, w_text, wq, wk, wv, vec, hid, embedded, normed, q, k, v = embed(
        place, image, after(text, z_a, z_b), (s_one, r_one, sp_one, rp_one)
    )
    b_a, b_b, z_a, z_b, q = settle(b_a, b_b, z_a, z_b, q)

    s_a, s_b = jnp.stack([z_a, b_a]), jnp.stack([z_b[:, :96], b_b[:, :96]])
    s_c = jnp.stack([z_b[:, 96:], b_b[:, 96:]])
    r_a, r_b, sp_a = to_chip(s_a, 2, 1), to_chip(s_b, 2, 1), swap_cores(s_a)
    both = attend(live, after(q, s_a, s_b, s_c), k, v, 0, 3)
    r_a, r_b, sp_a, both, s_b, s_c = settle(r_a, r_b, sp_a, both, s_b, s_c)

    r_c, sp_b, sp_c = to_chip(s_c, 2, 1), swap_cores(s_b), swap_cores(s_c)
    rp_a, rp_b = swap_cores(r_a), swap_cores(r_b)
    attended, totals = attend(live, q, k, v, 3, 3, both)
    r_c, sp_b, sp_c, rp_a, rp_b, attended = settle(r_c, sp_b, sp_c, rp_a, rp_b, attended)

    rp_c = swap_cores(r_c)
    w_out, w_hid, middle, second = middle_of(
        place, attended, embedded, vec, (s_a, r_a, sp_a, rp_a, s_b, r_b, sp_b, rp_b)
    )
    rp_c, second = settle(rp_c, second)

    layer_out, second_grad, ret_keep, ret_send, hid_keep, hid_send, hid_sum, ret_sum = feed(
        place, second, cot, middle, vec, w_hid.reshape(WIDTH, HIDDEN), hid,
        (s_c, r_c, sp_c, rp_c),
    )

    feeding = Scatter(place, ((ret_keep, ret_send), (hid_keep, hid_send)))
    feeding.swap()
    middle_grad, branch, incoming, sums = branch_of(middle, second_grad, cot, vec, w_out)
    feeding.got, feeding.kept, incoming = settle(feeding.got, feeding.kept, incoming)

    feeding.first()
    feeding.send_first()
    incoming = after(incoming, feeding.sent, feeding.kept)
    grads = attend_back(live, q, k, v, incoming, attended, totals)
    feeding.got, feeding.kept, grads = settle(feeding.got, feeding.kept, grads)

    feeding.second()
    feeding.send_second()
    grads = after(grads, feeding.sent, feeding.kept)
    pair = square_grads(place, attended, branch, normed, grads)
    feeding.got, feeding.kept, grads, pair = settle(feeding.got, feeding.kept, grads, pair)

    feeding.third()
    feeding.send_third((1, 3))
    squares = Scatter(place, (pair,))
    squares.swap()
    grads = after(grads, feeding.sent, feeding.kept)
    image_low, text_low, late = norm_one(grads, (wq, wk, wv), embedded, middle_grad, vec)
    early, feeding.sent, squares.got, squares.kept, image_low, text_low = settle(
        feeding.got, feeding.sent, squares.got, squares.kept, image_low, text_low
    )

    feeding.send_third((2,))
    squares.first()
    squares.send_first()
    image_low, text_low = after((image_low, text_low), squares.sent, squares.kept)
    pair = last(place, image, text, image_low, text_low, sums, hid_sum, ret_sum, late)
    image_grad, text_grad = input_grads(image_low, text_low, w_image, w_text)
    feeding.got, squares.got, squares.kept, pair, image_grad, text_grad = settle(
        feeding.got + early, squares.got, squares.kept, pair, image_grad, text_grad
    )

    ending = Scatter(place, (pair,))
    ending.swap()
    squares.second()
    squares.send_second()
    feeding.fourth()
    ending.got, ending.kept, squares.got, squares.kept, feeding.sent = settle(
        ending.got, ending.kept, squares.got, squares.kept, feeding.sent
    )

    feeding.kept = feeding.sent
    feeding.swap()
    ending.first()
    ending.send_first()
    squares.third()
    squares.send_third()
    ending.got, ending.kept, squares.got, squares.kept, feeding.got, image_grad, text_grad = settle(
        ending.got, ending.kept, squares.got, squares.kept, feeding.got, image_grad, text_grad
    )

    ending.second()
    ending.send_second()
    squares.fourth()
    squares.swap()
    owned = owned_rows(SCATTER_CHUNKS[0], *feeding.sides())
    ending.got, ending.kept, squares.got, owned = settle(ending.got, ending.kept, squares.got, owned)

    ending.third()
    ending.send_third()
    owned.update(owned_rows(SCATTER_CHUNKS[1], *squares.sides()))
    ending.got, ending.kept, owned = settle(ending.got, ending.kept, owned)

    ending.fourth()
    ending.swap()
    owned.update(owned_rows(SCATTER_CHUNKS[2], *ending.sides()))
    image_grad, text_grad = (jnp.transpose(grad, (1, 0, 2)) for grad in (image_grad, text_grad))
    return (layer_out[None], image_grad, text_grad) + tuple(owned[i] for i in range(20))


def gather_any(shards):
    return tuple(lax.all_gather(shard, "fsdp", axis=0, tiled=True) for shard in shards)


def scatter_any(grads):
    pieces = [lax.psum_scatter(g, "fsdp", scatter_dimension=0, tiled=True) for g in grads]
    return tuple(lax.psum(to_low(p), "dp").astype(jnp.float32) for p in pieces)


def on_device(
    chips,
    cores,
    image_states,
    text_states,
    size_group,
    caption_len,
    cotangent,
    image_proj,
    image_bias,
    text_proj,
    text_bias,
    cls_token,
    first_gain,
    first_shift,
    query_proj,
    query_bias,
    key_proj,
    value_proj,
    value_bias,
    output_proj,
    output_bias,
    second_gain,
    second_shift,
    hidden_proj,
    hidden_bias,
    return_proj,
    return_bias,
):
    shards = (
        image_proj,
        image_bias,
        text_proj,
        text_bias,
        cls_token,
        first_gain,
        first_shift,
        query_proj,
        query_bias,
        key_proj,
        value_proj,
        value_bias,
        output_proj,
        output_bias,
        second_gain,
        second_shift,
        hidden_proj,
        hidden_bias,
        return_proj,
        return_bias,
    )
    fits = chips == 16 and cores == 2 and image_states.shape == (1, IMAGE, WIDTH)
    if fits and text_states.shape == (1, TEXTS, WIDTH) and hidden_proj.shape == (48, HIDDEN):
        image, text, cot = image_states[0], text_states[0], cotangent[0]
        return by_kernels(shards, image, text, size_group, caption_len, cot)
    weights = gather_any(shards)
    results, summed = [], None
    for item in range(image_states.shape[0]):
        image_rows, text_rows = image_states[item], text_states[item]
        code, length = size_group[item], caption_len[item]
        result, kept_rows = item_forward(weights, image_rows, text_rows, code, length)
        image_grad, text_grad, grads = item_backward(
            weights, image_rows, text_rows, code, length, kept_rows, cotangent[item]
        )
        results.append((result, image_grad, text_grad))
        summed = grads if summed is None else jax.tree.map(jnp.add, summed, grads)
    owned = scatter_any(summed)
    return tuple(jnp.stack(parts) for parts in zip(*results)) + owned


def solution(mesh):
    placed = (
        P(("fsdp", "dp"), None, None),
        P(("fsdp", "dp"), None, None),
        P(("fsdp", "dp")),
        P(("fsdp", "dp")),
        P(("fsdp", "dp"), None, None),
        P("fsdp", None),
        P("fsdp"),
        P("fsdp", None),
        P("fsdp"),
        P("fsdp"),
        P("fsdp"),
        P("fsdp"),
        P("fsdp", None),
        P("fsdp"),
        P("fsdp", None),
        P("fsdp", None),
        P("fsdp"),
        P("fsdp", None),
        P("fsdp"),
        P("fsdp"),
        P("fsdp"),
        P("fsdp", None),
        P("fsdp"),
        P("fsdp", None),
        P("fsdp"),
    )
    chips, cores = mesh.shape["fsdp"], mesh.shape["dp"]
    return jax.shard_map(
        functools.partial(on_device, chips, cores),
        mesh=mesh,
        in_specs=placed,
        out_specs=(
            P(("fsdp", "dp"), None, None),
            P(("fsdp", "dp"), None, None),
            P(("fsdp", "dp"), None, None),
            P("fsdp", None),
            P("fsdp"),
            P("fsdp", None),
            P("fsdp"),
            P("fsdp"),
            P("fsdp"),
            P("fsdp"),
            P("fsdp", None),
            P("fsdp"),
            P("fsdp", None),
            P("fsdp", None),
            P("fsdp"),
            P("fsdp", None),
            P("fsdp"),
            P("fsdp"),
            P("fsdp"),
            P("fsdp", None),
            P("fsdp"),
            P("fsdp", None),
            P("fsdp"),
        ),
        check_vma=False,
    )
```

```python
import functools
import math

import jax
import jax.numpy as jnp
from jax import lax
from jax.experimental import pallas as pl
from jax.experimental.pallas import tpu as pltpu
from jax.sharding import PartitionSpec as P

HEADS = 12
HEAD_DIM = 64
PATCH_BIG = 325
PATCH_SMALL = 197


EPSILON = 1e-06
NEGATIVE = -1e30


def matmul(left, right):
    return jnp.dot(left, right, preferred_element_type=jnp.float32)


def left_product(left, right):
    return lax.dot_general(
        left, right, (((0,), (0,)), ((), ())), preferred_element_type=jnp.float32
    )


def right_product(left, right):
    return lax.dot_general(
        left, right, (((1,), (1,)), ((), ())), preferred_element_type=jnp.float32
    )


def to_low(values):
    return values.astype(jnp.bfloat16)


def column_sum(values):
    return jnp.sum(values.astype(jnp.float32), 0)


def gelu_exact(values):
    return jax.nn.gelu(values, approximate=False)


def layer_norm(values, gain, shift):
    centered = values - jnp.mean(values, -1, keepdims=True)
    scaled = centered * lax.rsqrt(jnp.mean(centered * centered, -1, keepdims=True) + EPSILON)
    return scaled * gain + shift


def key_mask(size_code, length, row_count):
    position = jnp.arange(row_count, dtype=jnp.int32)
    patches = jnp.where(size_code == 1, PATCH_BIG, PATCH_SMALL).astype(jnp.int32)
    image_live = (position >= 1) & (position <= patches)
    text_live = (position >= 1 + PATCH_BIG) & (position < 1 + PATCH_BIG + length)
    return (position == 0) | image_live | text_live


def head_slice(source, offset, span_width, per_group):
    part = lax.dynamic_slice_in_dim(source, offset, span_width, 1)
    return part.reshape(source.shape[0], per_group, HEAD_DIM)


def attend_forward(queries, keys_all, values_all, key_live):
    row_count = queries.shape[0]
    per_group = math.gcd(HEADS, 4)
    span_width = per_group * HEAD_DIM
    factor = HEAD_DIM ** (-0.5)

    def one_group(group_index, running):
        attended, totals = running
        offset = group_index * span_width
        query_part = head_slice(queries, offset, span_width, per_group)
        key_part = head_slice(keys_all, offset, span_width, per_group)
        value_part = head_slice(values_all, offset, span_width, per_group)
        scores = (
            jnp.einsum("qhd,khd->hqk", query_part, key_part, preferred_element_type=jnp.float32)
            * factor
        )
        scores = jnp.where(key_live, scores, NEGATIVE)
        row_top = jnp.max(scores, -1, keepdims=True)
        exps = jnp.exp(scores - row_top)
        row_total = jnp.sum(exps, -1, keepdims=True)
        prob_rows = to_low(exps / row_total)
        mixed_heads = jnp.einsum(
            "hqk,khd->qhd", prob_rows, value_part, preferred_element_type=jnp.float32
        )
        attended = lax.dynamic_update_slice_in_dim(
            attended, to_low(mixed_heads.reshape(row_count, span_width)), offset, 1
        )
        log_total = (row_top + jnp.log(row_total))[:, :, 0]
        totals = lax.dynamic_update_slice_in_dim(totals, log_total, group_index * per_group, 0)
        return (attended, totals)

    initial = (
        jnp.zeros((row_count, HEADS * HEAD_DIM), jnp.bfloat16),
        jnp.zeros((HEADS, row_count), jnp.float32),
    )
    return lax.fori_loop(0, HEADS // per_group, one_group, initial)


def attend_backward(queries, keys_all, values_all, key_live, totals, incoming):
    row_count = queries.shape[0]
    per_group = math.gcd(HEADS, 4)
    span_width = per_group * HEAD_DIM
    factor = HEAD_DIM ** (-0.5)

    def one_group(group_index, running):
        query_grad, key_grad, value_grad = running
        offset = group_index * span_width
        query_part = head_slice(queries, offset, span_width, per_group)
        key_part = head_slice(keys_all, offset, span_width, per_group)
        value_part = head_slice(values_all, offset, span_width, per_group)
        incoming_part = head_slice(incoming, offset, span_width, per_group)
        log_total = lax.dynamic_slice_in_dim(totals, group_index * per_group, per_group, 0)
        scores = (
            jnp.einsum("qhd,khd->hqk", query_part, key_part, preferred_element_type=jnp.float32)
            * factor
        )
        scores = jnp.where(key_live, scores, NEGATIVE)
        prob_rows = jnp.exp(scores - log_total[:, :, None])
        value_part_grad = jnp.einsum(
            "hqk,qhd->khd", to_low(prob_rows), incoming_part, preferred_element_type=jnp.float32
        )
        prob_grad = jnp.einsum(
            "qhd,khd->hqk", incoming_part, value_part, preferred_element_type=jnp.float32
        )
        score_grad = to_low(
            prob_rows * (prob_grad - jnp.sum(prob_rows * prob_grad, -1, keepdims=True))
        )
        query_part_grad = (
            jnp.einsum("hqk,khd->qhd", score_grad, key_part, preferred_element_type=jnp.float32)
            * factor
        )
        key_part_grad = (
            jnp.einsum("hqk,qhd->khd", score_grad, query_part, preferred_element_type=jnp.float32)
            * factor
        )
        query_grad = lax.dynamic_update_slice_in_dim(
            query_grad, to_low(query_part_grad.reshape(row_count, span_width)), offset, 1
        )
        key_grad = lax.dynamic_update_slice_in_dim(
            key_grad, to_low(key_part_grad.reshape(row_count, span_width)), offset, 1
        )
        value_grad = lax.dynamic_update_slice_in_dim(
            value_grad, to_low(value_part_grad.reshape(row_count, span_width)), offset, 1
        )
        return (query_grad, key_grad, value_grad)

    empty_grad = jnp.zeros((row_count, HEADS * HEAD_DIM), jnp.bfloat16)
    return lax.fori_loop(0, HEADS // per_group, one_group, (empty_grad, empty_grad, empty_grad))


def item_forward(weights, image_rows, text_rows, size_code, length):
    (
        image_proj,
        image_bias,
        text_proj,
        text_bias,
        cls_token,
        first_gain,
        first_shift,
        query_proj,
        query_bias,
        key_proj,
        value_proj,
        value_bias,
        output_proj,
        output_bias,
        second_gain,
        second_shift,
        hidden_proj,
        hidden_bias,
        return_proj,
        return_bias,
    ) = weights
    image_part = matmul(image_rows, image_proj) + image_bias.astype(jnp.float32)
    text_part = matmul(text_rows, text_proj) + text_bias.astype(jnp.float32)
    embedded = jnp.concatenate([cls_token.astype(jnp.float32)[None, :], image_part, text_part], 0)
    normed = to_low(
        layer_norm(embedded, first_gain.astype(jnp.float32), first_shift.astype(jnp.float32))
    )
    queries = to_low(matmul(normed, query_proj) + query_bias.astype(jnp.float32))
    keys_all = to_low(matmul(normed, key_proj))
    values_all = to_low(matmul(normed, value_proj) + value_bias.astype(jnp.float32))
    key_live = key_mask(size_code, length, embedded.shape[0])
    attended, totals = attend_forward(queries, keys_all, values_all, key_live)
    middle = embedded + matmul(attended, output_proj) + output_bias.astype(jnp.float32)
    second = to_low(
        layer_norm(middle, second_gain.astype(jnp.float32), second_shift.astype(jnp.float32))
    )
    inner_pre = matmul(second, hidden_proj) + hidden_bias.astype(jnp.float32)
    activated = to_low(gelu_exact(inner_pre))
    result = middle + matmul(activated, return_proj) + return_bias.astype(jnp.float32)
    kept_rows = (
        embedded,
        normed,
        queries,
        keys_all,
        values_all,
        attended,
        totals,
        middle,
        second,
        inner_pre,
        activated,
    )
    return (to_low(result), kept_rows)


def item_backward(weights, image_rows, text_rows, size_code, length, kept_rows, out_grad):
    (
        image_proj,
        image_bias,
        text_proj,
        text_bias,
        cls_token,
        first_gain,
        first_shift,
        query_proj,
        query_bias,
        key_proj,
        value_proj,
        value_bias,
        output_proj,
        output_bias,
        second_gain,
        second_shift,
        hidden_proj,
        hidden_bias,
        return_proj,
        return_bias,
    ) = weights
    (
        embedded,
        normed,
        queries,
        keys_all,
        values_all,
        attended,
        totals,
        middle,
        second,
        inner_pre,
        activated,
    ) = kept_rows
    grad_return_proj = left_product(activated, out_grad)
    grad_return_bias = column_sum(out_grad)
    activated_grad = right_product(out_grad, return_proj)
    unused_value, gelu_pull = jax.vjp(gelu_exact, inner_pre)
    inner_grad = to_low(gelu_pull(activated_grad)[0])
    grad_hidden_proj = left_product(second, inner_grad)
    grad_hidden_bias = column_sum(inner_grad)
    second_grad = right_product(inner_grad, hidden_proj)
    unused_norm, second_pull = jax.vjp(
        layer_norm, middle, second_gain.astype(jnp.float32), second_shift.astype(jnp.float32)
    )
    middle_part, grad_second_gain, grad_second_shift = second_pull(second_grad)
    middle_grad = out_grad.astype(jnp.float32) + middle_part
    branch_grad = to_low(middle_grad)
    grad_output_proj = left_product(attended, branch_grad)
    grad_output_bias = column_sum(branch_grad)
    attended_grad = to_low(right_product(branch_grad, output_proj))
    key_live = key_mask(size_code, length, embedded.shape[0])
    query_grad, key_grad, value_grad = attend_backward(
        queries, keys_all, values_all, key_live, totals, attended_grad
    )
    grad_query_proj = left_product(normed, query_grad)
    grad_query_bias = column_sum(query_grad)
    grad_key_proj = left_product(normed, key_grad)
    grad_value_proj = left_product(normed, value_grad)
    grad_value_bias = column_sum(value_grad)
    normed_grad = (
        right_product(query_grad, query_proj)
        + right_product(key_grad, key_proj)
        + right_product(value_grad, value_proj)
    )
    unused_first, first_pull = jax.vjp(
        layer_norm, embedded, first_gain.astype(jnp.float32), first_shift.astype(jnp.float32)
    )
    embedded_part, grad_first_gain, grad_first_shift = first_pull(normed_grad)
    embedded_grad = middle_grad + embedded_part
    grad_cls_token = embedded_grad[0]
    image_low = to_low(embedded_grad[1 : 1 + PATCH_BIG])
    text_low = to_low(embedded_grad[1 + PATCH_BIG :])
    image_grad = right_product(image_low, image_proj)
    text_grad = right_product(text_low, text_proj)
    grad_image_proj = left_product(image_rows, image_low)
    grad_image_bias = column_sum(image_low)
    grad_text_proj = left_product(text_rows, text_low)
    grad_text_bias = column_sum(text_low)
    grads = (
        grad_image_proj,
        grad_image_bias,
        grad_text_proj,
        grad_text_bias,
        grad_cls_token,
        grad_first_gain,
        grad_first_shift,
        grad_query_proj,
        grad_query_bias,
        grad_key_proj,
        grad_value_proj,
        grad_value_bias,
        grad_output_proj,
        grad_output_bias,
        grad_second_gain,
        grad_second_shift,
        grad_hidden_proj,
        grad_hidden_bias,
        grad_return_proj,
        grad_return_bias,
    )
    return (image_grad, text_grad, grads)


VECTORS = (1, 3, 4, 5, 6, 8, 11, 13, 14, 15, 19, 17)
LANES = 384
VEC_ROWS = 16
GATHER_CHUNKS = ((0, 2, "vec", 7, 9, 10), (12, "low"), ("high", 18))
SCATTER_CHUNKS = ((18, 16), (12, 7, 9, 10), (0, 2, "vec"))
BOTH = ("fsdp", "dp")
WIDTH = 768
HIDDEN = 3072
IMAGE = 325
TEXTS = 513
ROWS = 839
KEYS = 848
PADDED = 896
LOW = jnp.bfloat16
FULL = jnp.float32
COST_SCALE = 0.3
FAST = pl.BlockSpec(memory_space=pltpu.VMEM)
SCALARS = pl.BlockSpec(memory_space=pltpu.SMEM)


def cost(micros):
    return pl.CostEstimate(
        flops=int(micros * COST_SCALE * 1e9), bytes_accessed=1024, transcendentals=0
    )


class Place:
    def __init__(self):
        self.core = lax.axis_index("dp")
        chip = lax.axis_index("fsdp")
        self.x, self.y, self.z = chip & 1, (chip >> 1) & 1, chip >> 2
        self.scalars = jnp.stack([self.core, self.x, self.y, self.z]).astype(jnp.int32)


def shape(dims, kind=LOW):
    return jax.ShapeDtypeStruct(dims, kind)


def call(kernel, micros, outs, *args, scratch=(), limit=60):
    specs = [SCALARS if a.dtype == jnp.int32 else FAST for a in args]
    return pl.pallas_call(
        kernel,
        out_shape=tuple(outs),
        in_specs=specs,
        out_specs=tuple(FAST for _ in outs),
        scratch_shapes=list(scratch),
        compiler_params=pltpu.CompilerParams(vmem_limit_bytes=limit * 2**20),
        cost_estimate=cost(micros),
    )(*args)


def after(values, *others):
    return lax.optimization_barrier((values, others))[0]


def settle(*values):
    return lax.optimization_barrier(values)


def swap_cores(values):
    with jax.named_scope("between_cores"):
        return lax.ppermute(values, "dp", [(0, 1), (1, 0)])


def to_chip(values, mask_zero, mask_one):
    pairs = []
    for chip in range(16):
        pairs.append((chip * 2, (chip ^ mask_zero) * 2))
        pairs.append((chip * 2 + 1, (chip ^ mask_one) * 2 + 1))
    with jax.named_scope(f"chips_{mask_zero}_{mask_one}"):
        return lax.ppermute(values, BOTH, pairs)


def sub_blocks(index):
    return 4 if index == 16 else 1


def block_rows(index):
    return {"vec": VEC_ROWS, 16: 192, 18: 192, "low": 96, "high": 96}.get(index, 48)


def pack_kernel(chunk, at_ref, *refs):
    core = at_ref[0]
    count = len(chunk) + (11 if "vec" in chunk else 0)
    ins, out = refs[:count], refs[count]
    offset = 0
    order = [i for i in chunk if i != "vec"]
    for index in chunk:
        if index == "vec":
            rows = refs[-1]
            rows[...] = jnp.zeros_like(rows)
            for row in range(12):
                source = ins[len(order) + row]
                width = source.shape[0]
                rows[row : row + 1, 0:width] = source[...].astype(FULL).reshape(1, width)
            out[offset : offset + VEC_ROWS, :] = rows[...].astype(LOW)
            offset += VEC_ROWS
            continue
        parts = {"low": (4, (0, 1)), "high": (4, (2, 3))}.get(index, (1, (0,)))
        source = ins[order.index(index)]
        rows = source.shape[0]
        for s in parts[1]:
            first = pl.multiple_of((core * parts[0] + s) * LANES, LANES)
            out[offset : offset + rows, :] = source[:, pl.ds(first, LANES)]
            offset += rows


def pack(place, shards, chunk):
    rows = sum(block_rows(i) for i in chunk)
    ins = [shards[16 if i in ("low", "high") else i] for i in chunk if i != "vec"]
    scratch = ()
    if "vec" in chunk:
        ins += [shards[i] for i in VECTORS]
        scratch = (pltpu.VMEM((VEC_ROWS, LANES), FULL),)
    kernel = functools.partial(pack_kernel, chunk)
    return call(kernel, 1, [shape((rows, LANES))], place.scalars, *ins, scratch=scratch)[0]


def all_z(own):
    return [own] + [to_chip(own, 4 * s, 4 * s) for s in (1, 2, 3)]


def unpack(at_ref, pieces, targets):
    core, x, y, z = at_ref[0], at_ref[1], at_ref[2], at_ref[3]

    def fill(zero_s, zero_r, one_s, one_r):
        for offset, blocks, count, out in targets:
            rows = out.shape[3]
            for n, s in enumerate(blocks):
                first = slice(offset + n * rows, offset + (n + 1) * rows)
                left = slice(s * LANES, (s + 1) * LANES)
                right = slice((count + s) * LANES, (count + s + 1) * LANES)
                for far in range(4):
                    plane = z ^ far
                    for b in range(2):
                        out[plane, y, x ^ b, :, left] = zero_s[b, far, first, :]
                        out[plane, 1 - y, x ^ b, :, left] = zero_r[b, far, first, :]
                        if count:
                            out[plane, y ^ b, x, :, right] = one_s[b, far, first, :]
                            out[plane, y ^ b, 1 - x, :, right] = one_r[b, far, first, :]

    s8, r8, s8p, r8p = pieces

    @pl.when(core == 0)
    def _():
        fill(s8, r8, s8p, r8p)

    @pl.when(core == 1)
    def _():
        fill(s8p, r8p, s8, r8)


def square(ref):
    return ref[...].reshape(16 * ref.shape[3], ref.shape[4])


def row_chunks(step, total=ROWS):
    return [slice(a, min(a + step, total)) for a in range(0, total, step)]


def standard(values):
    centered = values - jnp.mean(values, -1, keepdims=True)
    scale = lax.rsqrt(jnp.mean(centered * centered, -1, keepdims=True) + EPSILON)
    return centered * scale, scale


def norm_back(values, gain, incoming):
    unit, scale = standard(values)
    f = incoming * gain
    back = (f - jnp.mean(f, -1, keepdims=True) - unit * jnp.mean(f * unit, -1, keepdims=True)) * scale
    return back, unit


def sum_rows(values):
    return jnp.sum(values.astype(FULL), 0, keepdims=True)


def embed_kernel(
    at, image, text, s8, r8, s8p, r8p,
    w_image, w_text, wq, wk, wv, vec, hid, embedded, normed, q, k, v, small,
):
    unpack(
        at,
        (s8, r8, s8p, r8p),
        (
            (0, (0,), 1, w_image),
            (48, (0,), 1, w_text),
            (96, (0,), 0, small),
            (112, (0,), 1, wq),
            (160, (0,), 1, wk),
            (208, (0,), 1, wv),
        ),
    )
    for f in range(16):
        piece = small[f >> 2, (f >> 1) & 1, f & 1].astype(FULL)
        vec[:, f * 48 : (f + 1) * 48] = piece[:, :48]
        hid[:, f * 192 : (f + 1) * 192] = piece[11:12, :192]
    embedded[0:1, :] = vec[2:3, :]
    embedded[1 : 1 + IMAGE, :] = matmul(image[...], square(w_image)) + vec[0:1, :]
    embedded[1 + IMAGE : ROWS, :] = matmul(text[...], square(w_text)) + vec[1:2, :]
    for rows in row_chunks(64):
        unit, unused_scale = standard(embedded[rows, :])
        normed[rows, :] = to_low(unit * vec[3:4, :] + vec[4:5, :])
    for out in (q, k, v):
        out[832:PADDED, :] = jnp.zeros((PADDED - 832, WIDTH), LOW)
    rows = normed[...]
    low = to_low(matmul(rows, square(wq)) + vec[5:6, :])
    q[0:ROWS, :] = to_low(low.astype(FULL) * HEAD_DIM**-0.5)
    k[0:ROWS, :] = to_low(matmul(rows, square(wk)))
    v[0:ROWS, :] = to_low(matmul(rows, square(wv)) + vec[6:7, :])


def embed(place, image, text, pieces):
    outs = [shape((4, 2, 2, 48, WIDTH))] * 5
    outs += [shape((VEC_ROWS, WIDTH), FULL), shape((1, HIDDEN), FULL)]
    outs += [shape((ROWS, WIDTH), FULL), shape((ROWS, WIDTH))] + [shape((PADDED, WIDTH))] * 3
    scratch = (pltpu.VMEM((4, 2, 2, VEC_ROWS, LANES), LOW),)
    return call(embed_kernel, 12, outs, place.scalars, image, text, *pieces, scratch=scratch)


def mask_column(live):
    position = lax.broadcasted_iota(jnp.int32, (KEYS, 1), 0)
    patches = jnp.where(live[0] == 1, PATCH_BIG, PATCH_SMALL).astype(jnp.int32)
    image_live = (position >= 1) & (position <= patches)
    text_live = (position >= 1 + PATCH_BIG) & (position < 1 + PATCH_BIG + live[1])
    return jnp.where((position == 0) | image_live | text_live, 0.0, NEGATIVE).astype(FULL)


def one_head(ref_value, head):
    lane = lax.broadcasted_iota(jnp.int32, ref_value.shape, 1)
    keep = (lane < HEAD_DIM) if head == 0 else (lane >= HEAD_DIM)
    return jnp.where(keep, ref_value, jnp.zeros_like(ref_value))


def across(values):
    return jnp.transpose(values.astype(FULL))


def fold_rows(values, op):
    return op(values.reshape(values.shape[0] // 8, 8, values.shape[1]), 0)


def attend_kernel(live, q, k, v, attended, totals, keys, scores, probs, mixed):
    bias = mask_column(live)
    for h in range(2):
        keys[h] = one_head(k[0:KEYS, :], h)
    values_t = to_low(across(v[0:KEYS, :]))
    totals[...] = jnp.zeros_like(totals)
    parts = [(piece, h) for piece in row_chunks(256, PADDED) for h in range(2)]
    tiles = row_chunks(128, KEYS)
    tops = {}

    def score(n, tile):
        piece, h = parts[n]
        made = right_product(keys[h, tile, :], q[piece, :]) + bias[tile, :]
        scores[n % 2, tile, 0 : made.shape[1]] = made
        top = fold_rows(made, jnp.max)
        tops[n] = jnp.maximum(tops[n], top) if n in tops else top

    for tile in tiles:
        score(0, tile)
    for n, (piece, h) in enumerate(parts):
        width = piece.stop - piece.start
        top = jnp.max(tops[n], 0, keepdims=True)
        total = jnp.zeros((8, width), FULL)
        for tile in tiles:
            if n + 1 < len(parts):
                score(n + 1, tile)
            exps = jnp.exp(scores[n % 2, tile, 0:width] - top)
            total = total + fold_rows(exps, jnp.sum)
            probs[n % 2, tile, 0:width] = to_low(exps)
        total = jnp.sum(total, 0, keepdims=True)
        rows = slice(h * HEAD_DIM, (h + 1) * HEAD_DIM)
        out = matmul(values_t[rows, :], probs[n % 2, :, 0:width])
        mixed[rows, piece] = out * (1.0 / total)
        totals[0, h : h + 1, piece] = top + jnp.log(total)
    attended[...] = to_low(jnp.transpose(mixed[...]))


def attend(live, q, k, v, first, count, earlier=()):
    spec = pl.BlockSpec((PADDED, 2 * HEAD_DIM), lambda i: (0, i + first))
    anywhere = pl.BlockSpec(memory_space=pl.ANY)

    def kernel(live, q, k, v, *refs):
        attend_kernel(live, q, k, v, *refs[len(earlier) :])

    return pl.pallas_call(
        kernel,
        grid=(count,),
        out_shape=(shape((PADDED, WIDTH)), shape((HEADS // 2, 8, PADDED), FULL)),
        in_specs=[SCALARS] + [spec] * 3 + [anywhere] * len(earlier),
        out_specs=(spec, pl.BlockSpec((1, 8, PADDED), lambda i: (i + first, 0, 0))),
        scratch_shapes=[
            pltpu.VMEM((2, KEYS, 2 * HEAD_DIM), LOW),
            pltpu.VMEM((2, KEYS, 256), FULL),
            pltpu.VMEM((2, KEYS, 256), LOW),
            pltpu.VMEM((2 * HEAD_DIM, PADDED), FULL),
        ],
        input_output_aliases={4 + n: n for n in range(len(earlier))},
        compiler_params=pltpu.CompilerParams(vmem_limit_bytes=60 * 2**20),
        cost_estimate=cost(3 * count),
    )(live, q, k, v, *earlier)


def attend_back_kernel(
    live, q, k, v, incoming, attended, totals, q_grad, k_grad, v_grad,
    keys, values, probs, score_grads, mixed,
):
    bias = mask_column(live)
    for h in range(2):
        keys[h] = one_head(k[0:KEYS, :], h)
        values[h] = one_head(v[0:KEYS, :], h)
    keys_t = to_low(across(k[0:KEYS, :]))
    product = jnp.transpose(incoming[...].astype(FULL) * attended[...].astype(FULL))
    for h in range(2):
        rows = slice(h * HEAD_DIM, (h + 1) * HEAD_DIM)
        along = jnp.sum(product[rows], 0, keepdims=True)
        for piece in row_chunks(256, PADDED):
            for tile in row_chunks(256, KEYS):
                made = right_product(keys[h, tile, :], q[piece, :]) + bias[tile, :]
                prob = jnp.exp(made - totals[0, h : h + 1, piece])
                prob_grad = right_product(values[h, tile, :], incoming[piece, :])
                probs[h, tile, piece] = to_low(prob)
                score_grads[h, tile, piece] = to_low(prob * (prob_grad - along[:, piece]))
        mixed[rows, :] = matmul(keys_t[rows, :], score_grads[h])
    lane = lax.broadcasted_iota(jnp.int32, (KEYS, 2 * HEAD_DIM), 1) < HEAD_DIM
    for out, left, right in ((k_grad, score_grads, q), (v_grad, probs, incoming)):
        right = right[...]
        out[0:KEYS, :] = to_low(jnp.where(lane, matmul(left[0], right), matmul(left[1], right)))
    q_grad[...] = to_low(jnp.transpose(mixed[...]) * HEAD_DIM**-0.5)


def attend_back(live, q, k, v, incoming, attended, totals):
    spec = pl.BlockSpec((PADDED, 2 * HEAD_DIM), lambda i: (0, i))
    return pl.pallas_call(
        attend_back_kernel,
        grid=(HEADS // 2,),
        out_shape=(shape((PADDED, WIDTH)),) * 3,
        in_specs=[SCALARS] + [spec] * 5 + [pl.BlockSpec((1, 8, PADDED), lambda i: (i, 0, 0))],
        out_specs=(spec,) * 3,
        scratch_shapes=[
            pltpu.VMEM((2, KEYS, 2 * HEAD_DIM), LOW),
            pltpu.VMEM((2, KEYS, 2 * HEAD_DIM), LOW),
            pltpu.VMEM((2, KEYS, PADDED), LOW),
            pltpu.VMEM((2, KEYS, PADDED), LOW),
            pltpu.VMEM((2 * HEAD_DIM, PADDED), FULL),
        ],
        compiler_params=pltpu.CompilerParams(vmem_limit_bytes=60 * 2**20),
        cost_estimate=cost(28),
    )(live, q, k, v, incoming, attended, totals)


def middle_kernel(
    at, attended, embedded, vec, s8, r8, s8p, r8p, s_hi, r_hi, sp_hi, rp_hi,
    w_out, w_hid, middle, second,
):
    unpack(at, (s8, r8, s8p, r8p), ((0, (0,), 1, w_out), (48, (0, 1), 4, w_hid)))
    unpack(at, (s_hi, r_hi, sp_hi, rp_hi), ((0, (2, 3), 4, w_hid),))
    middle[...] = embedded[...] + matmul(attended[0:ROWS, :], square(w_out)) + vec[7:8, :]
    for rows in row_chunks(64):
        unit, unused_scale = standard(middle[rows, :])
        second[rows, :] = to_low(unit * vec[8:9, :] + vec[9:10, :])


def middle_of(place, attended, embedded, vec, pieces):
    outs = [
        shape((4, 2, 2, 48, WIDTH)),
        shape((4, 2, 2, 48, HIDDEN)),
        shape((ROWS, WIDTH), FULL),
        shape((ROWS, WIDTH)),
    ]
    return call(middle_kernel, 8, outs, place.scalars, attended, embedded, vec, *pieces)


def gelu_parts(u):
    cumulative = 0.5 * (1.0 + lax.erf(u * (2.0**-0.5)))
    slope = cumulative + u * (jnp.exp(-0.5 * u * u) * (2.0 * math.pi) ** -0.5)
    return u * cumulative, slope


def feed_kernel(
    at, second, cot, middle, vec, w_hid, hid, s8, r8, s8p, r8p,
    layer_out, second_grad, ret_keep, ret_send, hid_keep, hid_send, hid_sum, ret_sum,
    w_ret, act, inner, total,
):
    step = pl.program_id(0)
    core, x, y = at[0], at[1], at[2]

    def fill(zero_s, zero_r, one_s, one_r):
        for b in range(2):
            w_ret[y, x ^ b, :, 0:LANES] = zero_s[b, 0]
            w_ret[1 - y, x ^ b, :, 0:LANES] = zero_r[b, 0]
            w_ret[y ^ b, x, :, LANES:] = one_s[b, 0]
            w_ret[y ^ b, 1 - x, :, LANES:] = one_r[b, 0]

    @pl.when(core == 0)
    def _():
        fill(s8, r8, s8p, r8p)

    @pl.when(core == 1)
    def _():
        fill(s8p, r8p, s8, r8)

    ret = w_ret[...].reshape(WIDTH, WIDTH)
    inward = w_hid[...]
    for rows in row_chunks(432):
        pre = matmul(second[rows, :], inward) + hid[...]
        back = right_product(cot[rows, :], ret)
        value, slope = gelu_parts(pre)
        act[rows, :] = to_low(value)
        inner[rows, :] = to_low(back * slope)
        out = matmul(act[rows, :], ret)
        back = right_product(inner[rows, :], inward)

        @pl.when(step == 0)
        def _():
            total[rows, :] = out
            second_grad[rows, :] = back

        @pl.when(step > 0)
        def _():
            total[rows, :] += out
            second_grad[rows, :] += back

    hid_sum[...] = sum_rows(inner[...])
    ret_grad = to_low(left_product(act[...], cot[...])).reshape(4, 192, WIDTH)
    hid_grad = to_low(left_product(second[...], inner[...])).reshape(16, 48, WIDTH)

    @pl.when(core == 0)
    def _():
        ret_keep[...] = ret_grad[:, :, 0:LANES]
        ret_send[...] = ret_grad[:, :, LANES:]

    @pl.when(core == 1)
    def _():
        ret_keep[...] = ret_grad[:, :, LANES:]
        ret_send[...] = ret_grad[:, :, 0:LANES]

    @pl.when(step < 2)
    def _():
        hid_send[:, 0:48, :] = hid_grad[:, :, 0:LANES]
        hid_send[:, 48:96, :] = hid_grad[:, :, LANES:]

    @pl.when(step >= 2)
    def _():
        hid_keep[:, 0:48, :] = hid_grad[:, :, 0:LANES]
        hid_keep[:, 48:96, :] = hid_grad[:, :, LANES:]

    @pl.when(step == 3)
    def _():
        layer_out[...] = to_low(middle[...] + total[...] + vec[10:11, :])
        ret_sum[...] = sum_rows(cot[...])


def feed(place, second, cot, middle, vec, w_hid, hid, pieces):
    def column(i, at):
        half = jnp.where(i < 2, 1 - at[0], at[0])
        return 2 * half + lax.rem(i, 2)

    def whole(dims):
        return pl.BlockSpec(dims, lambda i, at: (0,) * len(dims))

    piece = pl.BlockSpec((2, 1, 192, LANES), lambda i, at: (0, column(i, at) ^ at[3], 0, 0))
    ret_spec = pl.BlockSpec((4, 192, LANES), lambda i, at: (column(i, at), 0, 0))
    outs = (
        shape((ROWS, WIDTH)),
        shape((ROWS, WIDTH), FULL),
        shape((16, 192, LANES)),
        shape((16, 192, LANES)),
        shape((16, 192, LANES)),
        shape((16, 192, LANES)),
        shape((1, HIDDEN), FULL),
        shape((1, WIDTH), FULL),
    )
    grid = pltpu.PrefetchScalarGridSpec(
        num_scalar_prefetch=1,
        grid=(4,),
        in_specs=[
            whole((ROWS, WIDTH)),
            whole((ROWS, WIDTH)),
            whole((ROWS, WIDTH)),
            whole((VEC_ROWS, WIDTH)),
            pl.BlockSpec((WIDTH, WIDTH), lambda i, at: (0, column(i, at))),
            pl.BlockSpec((1, WIDTH), lambda i, at: (0, column(i, at))),
            piece,
            piece,
            piece,
            piece,
        ],
        out_specs=(
            whole((ROWS, WIDTH)),
            whole((ROWS, WIDTH)),
            ret_spec,
            ret_spec,
            pl.BlockSpec((16, 96, LANES), lambda i, at: (0, jnp.maximum(i - 2, 0), 0)),
            pl.BlockSpec((16, 96, LANES), lambda i, at: (0, jnp.minimum(i, 1), 0)),
            pl.BlockSpec((1, WIDTH), lambda i, at: (0, column(i, at))),
            whole((1, WIDTH)),
        ),
        scratch_shapes=[
            pltpu.VMEM((2, 2, 192, WIDTH), LOW),
            pltpu.VMEM((ROWS, WIDTH), LOW),
            pltpu.VMEM((ROWS, WIDTH), LOW),
            pltpu.VMEM((ROWS, WIDTH), FULL),
        ],
    )
    return pl.pallas_call(
        feed_kernel,
        grid_spec=grid,
        out_shape=outs,
        compiler_params=pltpu.CompilerParams(vmem_limit_bytes=63 * 2**20),
        cost_estimate=cost(40),
    )(place.scalars, second, cot, middle, vec, w_hid, hid, *pieces)


def branch_kernel(middle, second_grad, cot, vec, w_out, middle_grad, branch, incoming, sums):
    parts = [jnp.zeros((1, WIDTH), FULL)] * 3
    for rows in row_chunks(64):
        e = second_grad[rows, :]
        back, unit = norm_back(middle[rows, :], vec[8:9, :], e)
        grad = cot[rows, :].astype(FULL) + back
        middle_grad[rows, :] = grad
        branch[rows, :] = to_low(grad)
        for n, term in enumerate((e * unit, e, to_low(grad))):
            parts[n] = parts[n] + sum_rows(term)
    for n in range(3):
        sums[n : n + 1, :] = parts[n]
    incoming[832:PADDED, :] = jnp.zeros((PADDED - 832, WIDTH), LOW)
    incoming[0:ROWS, :] = to_low(right_product(branch[...], square(w_out)))


def branch_of(middle, second_grad, cot, vec, w_out):
    outs = [
        shape((ROWS, WIDTH), FULL),
        shape((ROWS, WIDTH)),
        shape((PADDED, WIDTH)),
        shape((8, WIDTH), FULL),
    ]
    return call(branch_kernel, 8, outs, middle, second_grad, cot, vec, w_out)


def both_halves(core, left_t, right_ref, first, keep, send, offset):
    for half, out in ((core, keep), (1 - core, send)):
        columns = pl.ds(pl.multiple_of(half * LANES, LANES), LANES)
        grad = matmul(left_t, right_ref[first, columns])
        out[:, offset : offset + 48, :] = to_low(grad).reshape(16, 48, LANES)


def square_grads_kernel(at, attended, branch, normed, dq, dk, dv, keep, send):
    rows = slice(0, ROWS)
    both_halves(at[0], jnp.transpose(attended[rows, :]), branch, rows, keep, send, 0)
    left_t = jnp.transpose(normed[...])
    for n, ref in enumerate((dq, dk, dv)):
        both_halves(at[0], left_t, ref, rows, keep, send, 48 * (n + 1))


def square_grads(place, attended, branch, normed, grads):
    outs = [shape((16, 192, LANES))] * 2
    return call(
        square_grads_kernel, 11, outs, place.scalars, attended, branch, normed, *grads
    )


def norm_one_kernel(
    dq, dk, dv, wq, wk, wv, embedded, middle_grad, vec, image_low, text_low, late, grad
):
    rows = slice(0, ROWS)
    grad[...] = (
        right_product(dq[rows, :], square(wq))
        + right_product(dk[rows, :], square(wk))
        + right_product(dv[rows, :], square(wv))
    )
    parts = [jnp.zeros((1, WIDTH), FULL)] * 4
    for piece in row_chunks(64):
        e = grad[piece, :]
        back, unit = norm_back(embedded[piece, :], vec[3:4, :], e)
        for n, term in enumerate((e * unit, e, dq[piece, :], dv[piece, :])):
            parts[n] = parts[n] + sum_rows(term)
        grad[piece, :] = middle_grad[piece, :] + back
    image_low[...] = to_low(grad[1 : 1 + IMAGE, :])
    text_low[...] = to_low(grad[1 + IMAGE : ROWS, :])
    late[...] = jnp.zeros_like(late)
    late[0:1, :] = grad[0:1, :]
    for n in range(4):
        late[n + 1 : n + 2, :] = parts[n]


def norm_one(grads, projs, embedded, middle_grad, vec):
    outs = [shape((IMAGE, WIDTH)), shape((TEXTS, WIDTH)), shape((8, WIDTH), FULL)]
    scratch = (pltpu.VMEM((ROWS, WIDTH), FULL),)
    return call(
        norm_one_kernel, 11, outs, *grads, *projs, embedded, middle_grad, vec, scratch=scratch
    )


def last_kernel(
    at, image, text, image_low, text_low, sums, hid_sum, ret_sum, late,
    keep, send, rows16, packed,
):
    both_halves(at[0], jnp.transpose(image[...]), image_low, slice(0, IMAGE), keep, send, 0)
    both_halves(at[0], jnp.transpose(text[...]), text_low, slice(0, TEXTS), keep, send, 48)
    rows16[...] = jnp.zeros_like(rows16)
    found = (
        sum_rows(image_low[...]), sum_rows(text_low[...]), late[0:1, :], late[1:2, :], late[2:3, :],
        late[3:4, :], late[4:5, :], sums[2:3, :], sums[0:1, :], sums[1:2, :], ret_sum[...],
    )
    for n, value in enumerate(found):
        rows16[n : n + 1, :] = value
    packed[...] = jnp.zeros_like(packed)
    for f in range(16):
        packed[f, :, 0:48] = rows16[:, f * 48 : (f + 1) * 48]
        packed[f, 11:12, 0:192] = hid_sum[:, f * 192 : (f + 1) * 192]
    low = to_low(packed[...])
    keep[:, 96:112, :] = low
    send[:, 96:112, :] = low


def last(place, image, text, image_low, text_low, sums, hid_sum, ret_sum, late):
    outs = [shape((16, 112, LANES)), shape((16, 112, LANES))]
    scratch = (pltpu.VMEM((VEC_ROWS, WIDTH), FULL), pltpu.VMEM((16, VEC_ROWS, LANES), FULL))
    return call(
        last_kernel, 5.5, outs, place.scalars, image, text, image_low, text_low, sums, hid_sum, ret_sum,
        late, scratch=scratch,
    )


def inputs_kernel(image_low, text_low, w_image, w_text, image_grad, text_grad):
    image_grad[:, 0, :] = right_product(image_low[...], square(w_image))
    text_grad[:, 0, :] = right_product(text_low[...], square(w_text))


def input_grads(image_low, text_low, w_image, w_text):
    outs = [shape((IMAGE, 1, WIDTH), FULL), shape((TEXTS, 1, WIDTH), FULL)]
    return call(inputs_kernel, 4.4, outs, image_low, text_low, w_image, w_text)


def add_low(*values):
    total = values[0].astype(FULL)
    for value in values[1:]:
        total = total + value.astype(FULL)
    return to_low(total)


def pick(values, at, axis):
    return lax.dynamic_index_in_dim(values, at, axis, keepdims=False)


class Scatter:
    def __init__(self, place, pairs):
        self.place = place
        self.kept = [keep for keep, unused_send in pairs]
        self.sent = [send for unused_keep, send in pairs]
        self.got = None

    def state(self):
        return self.kept, self.got

    def summed(self, q):
        parts = []
        for keep, more in zip(self.kept, self.swapped):
            keep, more = (pick(v.reshape(4, 4, v.shape[1], LANES), q, 1) for v in (keep, more))
            parts.append(keep.astype(FULL) + more.astype(FULL))
        return jnp.concatenate(parts, 1) if len(parts) > 1 else parts[0]

    def first(self):
        zero, x, y = self.place.core == 0, self.place.x, self.place.y
        self.swapped = self.got
        far = [jnp.where(zero, 2 * (1 - y) + s, 2 * s + (1 - x)) for s in (0, 1)]
        self.sent = jnp.stack([to_low(self.summed(q)) for q in far], 1)

    def second(self):
        zero, x, y = self.place.core == 0, self.place.x, self.place.y
        mine = jnp.where(zero, x, y)

        def added(s):
            near = self.summed(jnp.where(zero, 2 * y + s, 2 * s + x))
            return to_low(near + pick(self.got, s, 1).astype(FULL))

        self.sent, self.kept = added(1 - mine), added(mine)

    def third(self):
        z = self.place.z
        total = add_low(self.kept, self.got)
        self.kept = pick(total, z, 0)
        self.sent = [pick(total, z ^ s, 0) for s in (1, 2, 3)]

    def fourth(self):
        self.sent = self.kept = add_low(self.kept, *self.got)

    def swap(self):
        self.got = jax.tree.map(swap_cores, self.sent)

    def send_first(self):
        self.got = to_chip(self.sent, 2, 1)

    def send_second(self):
        self.got = to_chip(self.sent, 1, 2)

    def send_third(self, steps=(1, 2, 3)):
        self.got = [to_chip(self.sent[s - 1], 4 * s, 4 * s) for s in steps]

    def sides(self):
        zero = self.place.core == 0
        mine, other = self.kept, self.got
        return jnp.where(zero, mine, other).astype(FULL), jnp.where(zero, other, mine).astype(FULL)


def owned_rows(chunk, left, right):
    result, at = {}, 0
    for index in chunk:
        rows = block_rows(index)
        if index == "vec":
            for n, vector in enumerate(VECTORS):
                result[vector] = left[at + n, : 192 if vector == 17 else 48]
        else:
            count = sub_blocks(index)
            step = rows // count
            sides = [
                side[at + s * step : at + (s + 1) * step] for side in (left, right) for s in range(count)
            ]
            result[index] = jnp.concatenate(sides, 1)
        at += rows
    return result


def by_kernels(shards, image, text, size_code, length, cot):
    place = Place()
    live = jnp.concatenate([size_code, length]).astype(jnp.int32)
    own_one = pack(place, shards, GATHER_CHUNKS[0])

    z_one = all_z(own_one)
    owns = [pack(place, shards, chunk) for chunk in GATHER_CHUNKS[1:]]
    z_one, owns = settle(z_one, owns)

    z_one = jnp.stack(z_one)
    b_one, z_a, z_one, owns = settle(to_chip(z_one, 1, 2), all_z(owns[0]), z_one, owns)

    s_one, z_a = jnp.stack([z_one, b_one]), jnp.stack(z_a)
    r_one, sp_one, z_b, s_one, z_a = settle(
        to_chip(s_one, 2, 1), swap_cores(s_one), all_z(owns[1]), s_one, z_a
    )

    rp_one, b_a = swap_cores(r_one), to_chip(z_a, 1, 2)
    z_b = jnp.stack(z_b)
    b_b = to_chip(z_b, 1, 2)
    w_image, w_text, wq, wk, wv, vec, hid, embedded, normed, q, k, v = embed(
        place, image, after(text, z_a, z_b), (s_one, r_one, sp_one, rp_one)
    )
    b_a, b_b, z_a, z_b, q = settle(b_a, b_b, z_a, z_b, q)

    s_a, s_b = jnp.stack([z_a, b_a]), jnp.stack([z_b[:, :96], b_b[:, :96]])
    s_c = jnp.stack([z_b[:, 96:], b_b[:, 96:]])
    r_a, r_b, sp_a = to_chip(s_a, 2, 1), to_chip(s_b, 2, 1), swap_cores(s_a)
    both = attend(live, after(q, s_a, s_b, s_c), k, v, 0, 3)
    r_a, r_b, sp_a, both, s_b, s_c = settle(r_a, r_b, sp_a, both, s_b, s_c)

    r_c, sp_b, sp_c = to_chip(s_c, 2, 1), swap_cores(s_b), swap_cores(s_c)
    rp_a, rp_b = swap_cores(r_a), swap_cores(r_b)
    attended, totals = attend(live, q, k, v, 3, 3, both)
    r_c, sp_b, sp_c, rp_a, rp_b, attended = settle(r_c, sp_b, sp_c, rp_a, rp_b, attended)

    rp_c = swap_cores(r_c)
    w_out, w_hid, middle, second = middle_of(
        place, attended, embedded, vec, (s_a, r_a, sp_a, rp_a, s_b, r_b, sp_b, rp_b)
    )
    rp_c, second = settle(rp_c, second)

    layer_out, second_grad, ret_keep, ret_send, hid_keep, hid_send, hid_sum, ret_sum = feed(
        place, second, cot, middle, vec, w_hid.reshape(WIDTH, HIDDEN), hid,
        (s_c, r_c, sp_c, rp_c),
    )

    feeding = Scatter(place, ((ret_keep, ret_send), (hid_keep, hid_send)))
    feeding.swap()
    middle_grad, branch, incoming, sums = branch_of(middle, second_grad, cot, vec, w_out)
    feeding.got, feeding.kept, incoming = settle(feeding.got, feeding.kept, incoming)

    feeding.first()
    feeding.send_first()
    incoming = after(incoming, feeding.sent, feeding.kept)
    grads = attend_back(live, q, k, v, incoming, attended, totals)
    feeding.got, feeding.kept, grads = settle(feeding.got, feeding.kept, grads)

    feeding.second()
    feeding.send_second()
    grads = after(grads, feeding.sent, feeding.kept)
    pair = square_grads(place, attended, branch, normed, grads)
    feeding.got, feeding.kept, grads, pair = settle(feeding.got, feeding.kept, grads, pair)

    feeding.third()
    feeding.send_third((1, 3))
    squares = Scatter(place, (pair,))
    squares.swap()
    grads = after(grads, feeding.sent, feeding.kept)
    image_low, text_low, late = norm_one(grads, (wq, wk, wv), embedded, middle_grad, vec)
    early, feeding.sent, squares.got, squares.kept, image_low, text_low = settle(
        feeding.got, feeding.sent, squares.got, squares.kept, image_low, text_low
    )

    feeding.send_third((2,))
    squares.first()
    squares.send_first()
    image_low, text_low = after((image_low, text_low), squares.sent, squares.kept)
    pair = last(place, image, text, image_low, text_low, sums, hid_sum, ret_sum, late)
    image_grad, text_grad = input_grads(image_low, text_low, w_image, w_text)
    feeding.got, squares.got, squares.kept, pair, image_grad, text_grad = settle(
        feeding.got + early, squares.got, squares.kept, pair, image_grad, text_grad
    )

    ending = Scatter(place, (pair,))
    ending.swap()
    squares.second()
    squares.send_second()
    feeding.fourth()
    ending.got, ending.kept, squares.got, squares.kept, feeding.sent = settle(
        ending.got, ending.kept, squares.got, squares.kept, feeding.sent
    )

    feeding.kept = feeding.sent
    feeding.swap()
    ending.first()
    ending.send_first()
    squares.third()
    squares.send_third()
    ending.got, ending.kept, squares.got, squares.kept, feeding.got, image_grad, text_grad = settle(
        ending.got, ending.kept, squares.got, squares.kept, feeding.got, image_grad, text_grad
    )

    ending.second()
    ending.send_second()
    squares.fourth()
    squares.swap()
    owned = owned_rows(SCATTER_CHUNKS[0], *feeding.sides())
    ending.got, ending.kept, squares.got, owned = settle(ending.got, ending.kept, squares.got, owned)

    ending.third()
    ending.send_third()
    owned.update(owned_rows(SCATTER_CHUNKS[1], *squares.sides()))
    ending.got, ending.kept, owned = settle(ending.got, ending.kept, owned)

    ending.fourth()
    ending.swap()
    owned.update(owned_rows(SCATTER_CHUNKS[2], *ending.sides()))
    image_grad, text_grad = (jnp.transpose(grad, (1, 0, 2)) for grad in (image_grad, text_grad))
    return (layer_out[None], image_grad, text_grad) + tuple(owned[i] for i in range(20))


def gather_any(shards):
    return tuple(lax.all_gather(shard, "fsdp", axis=0, tiled=True) for shard in shards)


def scatter_any(grads):
    pieces = [lax.psum_scatter(g, "fsdp", scatter_dimension=0, tiled=True) for g in grads]
    return tuple(lax.psum(to_low(p), "dp").astype(jnp.float32) for p in pieces)


def on_device(
    chips,
    cores,
    image_states,
    text_states,
    size_group,
    caption_len,
    cotangent,
    image_proj,
    image_bias,
    text_proj,
    text_bias,
    cls_token,
    first_gain,
    first_shift,
    query_proj,
    query_bias,
    key_proj,
    value_proj,
    value_bias,
    output_proj,
    output_bias,
    second_gain,
    second_shift,
    hidden_proj,
    hidden_bias,
    return_proj,
    return_bias,
):
    shards = (
        image_proj,
        image_bias,
        text_proj,
        text_bias,
        cls_token,
        first_gain,
        first_shift,
        query_proj,
        query_bias,
        key_proj,
        value_proj,
        value_bias,
        output_proj,
        output_bias,
        second_gain,
        second_shift,
        hidden_proj,
        hidden_bias,
        return_proj,
        return_bias,
    )
    fits = chips == 16 and cores == 2 and image_states.shape == (1, IMAGE, WIDTH)
    if fits and text_states.shape == (1, TEXTS, WIDTH) and hidden_proj.shape == (48, HIDDEN):
        image, text, cot = image_states[0], text_states[0], cotangent[0]
        return by_kernels(shards, image, text, size_group, caption_len, cot)
    weights = gather_any(shards)
    results, summed = [], None
    for item in range(image_states.shape[0]):
        image_rows, text_rows = image_states[item], text_states[item]
        code, length = size_group[item], caption_len[item]
        result, kept_rows = item_forward(weights, image_rows, text_rows, code, length)
        image_grad, text_grad, grads = item_backward(
            weights, image_rows, text_rows, code, length, kept_rows, cotangent[item]
        )
        results.append((result, image_grad, text_grad))
        summed = grads if summed is None else jax.tree.map(jnp.add, summed, grads)
    owned = scatter_any(summed)
    return tuple(jnp.stack(parts) for parts in zip(*results)) + owned


def solution(mesh):
    placed = (
        P(("fsdp", "dp"), None, None),
        P(("fsdp", "dp"), None, None),
        P(("fsdp", "dp")),
        P(("fsdp", "dp")),
        P(("fsdp", "dp"), None, None),
        P("fsdp", None),
        P("fsdp"),
        P("fsdp", None),
        P("fsdp"),
        P("fsdp"),
        P("fsdp"),
        P("fsdp"),
        P("fsdp", None),
        P("fsdp"),
        P("fsdp", None),
        P("fsdp", None),
        P("fsdp"),
        P("fsdp", None),
        P("fsdp"),
        P("fsdp"),
        P("fsdp"),
        P("fsdp", None),
        P("fsdp"),
        P("fsdp", None),
        P("fsdp"),
    )
    chips, cores = mesh.shape["fsdp"], mesh.shape["dp"]
    return jax.shard_map(
        functools.partial(on_device, chips, cores),
        mesh=mesh,
        in_specs=placed,
        out_specs=(
            P(("fsdp", "dp"), None, None),
            P(("fsdp", "dp"), None, None),
            P(("fsdp", "dp"), None, None),
            P("fsdp", None),
            P("fsdp"),
            P("fsdp", None),
            P("fsdp"),
            P("fsdp"),
            P("fsdp"),
            P("fsdp"),
            P("fsdp", None),
            P("fsdp"),
            P("fsdp", None),
            P("fsdp", None),
            P("fsdp"),
            P("fsdp", None),
            P("fsdp"),
            P("fsdp"),
            P("fsdp"),
            P("fsdp", None),
            P("fsdp"),
            P("fsdp", None),
            P("fsdp"),
        ),
        check_vma=False,
    )
```

```python
import functools
import math

import jax
import jax.numpy as jnp
from jax import lax
from jax.experimental import pallas as pl
from jax.experimental.pallas import tpu as pltpu
from jax.sharding import PartitionSpec as P

HEADS = 12
HEAD_DIM = 64
PATCH_BIG = 325
PATCH_SMALL = 197


EPSILON = 1e-06
NEGATIVE = -1e30


def matmul(left, right):
    return jnp.dot(left, right, preferred_element_type=jnp.float32)


def left_product(left, right):
    return lax.dot_general(
        left, right, (((0,), (0,)), ((), ())), preferred_element_type=jnp.float32
    )


def right_product(left, right):
    return lax.dot_general(
        left, right, (((1,), (1,)), ((), ())), preferred_element_type=jnp.float32
    )


def to_low(values):
    return values.astype(jnp.bfloat16)


def column_sum(values):
    return jnp.sum(values.astype(jnp.float32), 0)


def gelu_exact(values):
    return jax.nn.gelu(values, approximate=False)


def layer_norm(values, gain, shift):
    centered = values - jnp.mean(values, -1, keepdims=True)
    scaled = centered * lax.rsqrt(jnp.mean(centered * centered, -1, keepdims=True) + EPSILON)
    return scaled * gain + shift


def key_mask(size_code, length, row_count):
    position = jnp.arange(row_count, dtype=jnp.int32)
    patches = jnp.where(size_code == 1, PATCH_BIG, PATCH_SMALL).astype(jnp.int32)
    image_live = (position >= 1) & (position <= patches)
    text_live = (position >= 1 + PATCH_BIG) & (position < 1 + PATCH_BIG + length)
    return (position == 0) | image_live | text_live


def head_slice(source, offset, span_width, per_group):
    part = lax.dynamic_slice_in_dim(source, offset, span_width, 1)
    return part.reshape(source.shape[0], per_group, HEAD_DIM)


def attend_forward(queries, keys_all, values_all, key_live):
    row_count = queries.shape[0]
    per_group = math.gcd(HEADS, 4)
    span_width = per_group * HEAD_DIM
    factor = HEAD_DIM ** (-0.5)

    def one_group(group_index, running):
        attended, totals = running
        offset = group_index * span_width
        query_part = head_slice(queries, offset, span_width, per_group)
        key_part = head_slice(keys_all, offset, span_width, per_group)
        value_part = head_slice(values_all, offset, span_width, per_group)
        scores = (
            jnp.einsum("qhd,khd->hqk", query_part, key_part, preferred_element_type=jnp.float32)
            * factor
        )
        scores = jnp.where(key_live, scores, NEGATIVE)
        row_top = jnp.max(scores, -1, keepdims=True)
        exps = jnp.exp(scores - row_top)
        row_total = jnp.sum(exps, -1, keepdims=True)
        prob_rows = to_low(exps / row_total)
        mixed_heads = jnp.einsum(
            "hqk,khd->qhd", prob_rows, value_part, preferred_element_type=jnp.float32
        )
        attended = lax.dynamic_update_slice_in_dim(
            attended, to_low(mixed_heads.reshape(row_count, span_width)), offset, 1
        )
        log_total = (row_top + jnp.log(row_total))[:, :, 0]
        totals = lax.dynamic_update_slice_in_dim(totals, log_total, group_index * per_group, 0)
        return (attended, totals)

    initial = (
        jnp.zeros((row_count, HEADS * HEAD_DIM), jnp.bfloat16),
        jnp.zeros((HEADS, row_count), jnp.float32),
    )
    return lax.fori_loop(0, HEADS // per_group, one_group, initial)


def attend_backward(queries, keys_all, values_all, key_live, totals, incoming):
    row_count = queries.shape[0]
    per_group = math.gcd(HEADS, 4)
    span_width = per_group * HEAD_DIM
    factor = HEAD_DIM ** (-0.5)

    def one_group(group_index, running):
        query_grad, key_grad, value_grad = running
        offset = group_index * span_width
        query_part = head_slice(queries, offset, span_width, per_group)
        key_part = head_slice(keys_all, offset, span_width, per_group)
        value_part = head_slice(values_all, offset, span_width, per_group)
        incoming_part = head_slice(incoming, offset, span_width, per_group)
        log_total = lax.dynamic_slice_in_dim(totals, group_index * per_group, per_group, 0)
        scores = (
            jnp.einsum("qhd,khd->hqk", query_part, key_part, preferred_element_type=jnp.float32)
            * factor
        )
        scores = jnp.where(key_live, scores, NEGATIVE)
        prob_rows = jnp.exp(scores - log_total[:, :, None])
        value_part_grad = jnp.einsum(
            "hqk,qhd->khd", to_low(prob_rows), incoming_part, preferred_element_type=jnp.float32
        )
        prob_grad = jnp.einsum(
            "qhd,khd->hqk", incoming_part, value_part, preferred_element_type=jnp.float32
        )
        score_grad = to_low(
            prob_rows * (prob_grad - jnp.sum(prob_rows * prob_grad, -1, keepdims=True))
        )
        query_part_grad = (
            jnp.einsum("hqk,khd->qhd", score_grad, key_part, preferred_element_type=jnp.float32)
            * factor
        )
        key_part_grad = (
            jnp.einsum("hqk,qhd->khd", score_grad, query_part, preferred_element_type=jnp.float32)
            * factor
        )
        query_grad = lax.dynamic_update_slice_in_dim(
            query_grad, to_low(query_part_grad.reshape(row_count, span_width)), offset, 1
        )
        key_grad = lax.dynamic_update_slice_in_dim(
            key_grad, to_low(key_part_grad.reshape(row_count, span_width)), offset, 1
        )
        value_grad = lax.dynamic_update_slice_in_dim(
            value_grad, to_low(value_part_grad.reshape(row_count, span_width)), offset, 1
        )
        return (query_grad, key_grad, value_grad)

    empty_grad = jnp.zeros((row_count, HEADS * HEAD_DIM), jnp.bfloat16)
    return lax.fori_loop(0, HEADS // per_group, one_group, (empty_grad, empty_grad, empty_grad))


def item_forward(weights, image_rows, text_rows, size_code, length):
    (
        image_proj,
        image_bias,
        text_proj,
        text_bias,
        cls_token,
        first_gain,
        first_shift,
        query_proj,
        query_bias,
        key_proj,
        value_proj,
        value_bias,
        output_proj,
        output_bias,
        second_gain,
        second_shift,
        hidden_proj,
        hidden_bias,
        return_proj,
        return_bias,
    ) = weights
    image_part = matmul(image_rows, image_proj) + image_bias.astype(jnp.float32)
    text_part = matmul(text_rows, text_proj) + text_bias.astype(jnp.float32)
    embedded = jnp.concatenate([cls_token.astype(jnp.float32)[None, :], image_part, text_part], 0)
    normed = to_low(
        layer_norm(embedded, first_gain.astype(jnp.float32), first_shift.astype(jnp.float32))
    )
    queries = to_low(matmul(normed, query_proj) + query_bias.astype(jnp.float32))
    keys_all = to_low(matmul(normed, key_proj))
    values_all = to_low(matmul(normed, value_proj) + value_bias.astype(jnp.float32))
    key_live = key_mask(size_code, length, embedded.shape[0])
    attended, totals = attend_forward(queries, keys_all, values_all, key_live)
    middle = embedded + matmul(attended, output_proj) + output_bias.astype(jnp.float32)
    second = to_low(
        layer_norm(middle, second_gain.astype(jnp.float32), second_shift.astype(jnp.float32))
    )
    inner_pre = matmul(second, hidden_proj) + hidden_bias.astype(jnp.float32)
    activated = to_low(gelu_exact(inner_pre))
    result = middle + matmul(activated, return_proj) + return_bias.astype(jnp.float32)
    kept_rows = (
        embedded,
        normed,
        queries,
        keys_all,
        values_all,
        attended,
        totals,
        middle,
        second,
        inner_pre,
        activated,
    )
    return (to_low(result), kept_rows)


def item_backward(weights, image_rows, text_rows, size_code, length, kept_rows, out_grad):
    (
        image_proj,
        image_bias,
        text_proj,
        text_bias,
        cls_token,
        first_gain,
        first_shift,
        query_proj,
        query_bias,
        key_proj,
        value_proj,
        value_bias,
        output_proj,
        output_bias,
        second_gain,
        second_shift,
        hidden_proj,
        hidden_bias,
        return_proj,
        return_bias,
    ) = weights
    (
        embedded,
        normed,
        queries,
        keys_all,
        values_all,
        attended,
        totals,
        middle,
        second,
        inner_pre,
        activated,
    ) = kept_rows
    grad_return_proj = left_product(activated, out_grad)
    grad_return_bias = column_sum(out_grad)
    activated_grad = right_product(out_grad, return_proj)
    unused_value, gelu_pull = jax.vjp(gelu_exact, inner_pre)
    inner_grad = to_low(gelu_pull(activated_grad)[0])
    grad_hidden_proj = left_product(second, inner_grad)
    grad_hidden_bias = column_sum(inner_grad)
    second_grad = right_product(inner_grad, hidden_proj)
    unused_norm, second_pull = jax.vjp(
        layer_norm, middle, second_gain.astype(jnp.float32), second_shift.astype(jnp.float32)
    )
    middle_part, grad_second_gain, grad_second_shift = second_pull(second_grad)
    middle_grad = out_grad.astype(jnp.float32) + middle_part
    branch_grad = to_low(middle_grad)
    grad_output_proj = left_product(attended, branch_grad)
    grad_output_bias = column_sum(branch_grad)
    attended_grad = to_low(right_product(branch_grad, output_proj))
    key_live = key_mask(size_code, length, embedded.shape[0])
    query_grad, key_grad, value_grad = attend_backward(
        queries, keys_all, values_all, key_live, totals, attended_grad
    )
    grad_query_proj = left_product(normed, query_grad)
    grad_query_bias = column_sum(query_grad)
    grad_key_proj = left_product(normed, key_grad)
    grad_value_proj = left_product(normed, value_grad)
    grad_value_bias = column_sum(value_grad)
    normed_grad = (
        right_product(query_grad, query_proj)
        + right_product(key_grad, key_proj)
        + right_product(value_grad, value_proj)
    )
    unused_first, first_pull = jax.vjp(
        layer_norm, embedded, first_gain.astype(jnp.float32), first_shift.astype(jnp.float32)
    )
    embedded_part, grad_first_gain, grad_first_shift = first_pull(normed_grad)
    embedded_grad = middle_grad + embedded_part
    grad_cls_token = embedded_grad[0]
    image_low = to_low(embedded_grad[1 : 1 + PATCH_BIG])
    text_low = to_low(embedded_grad[1 + PATCH_BIG :])
    image_grad = right_product(image_low, image_proj)
    text_grad = right_product(text_low, text_proj)
    grad_image_proj = left_product(image_rows, image_low)
    grad_image_bias = column_sum(image_low)
    grad_text_proj = left_product(text_rows, text_low)
    grad_text_bias = column_sum(text_low)
    grads = (
        grad_image_proj,
        grad_image_bias,
        grad_text_proj,
        grad_text_bias,
        grad_cls_token,
        grad_first_gain,
        grad_first_shift,
        grad_query_proj,
        grad_query_bias,
        grad_key_proj,
        grad_value_proj,
        grad_value_bias,
        grad_output_proj,
        grad_output_bias,
        grad_second_gain,
        grad_second_shift,
        grad_hidden_proj,
        grad_hidden_bias,
        grad_return_proj,
        grad_return_bias,
    )
    return (image_grad, text_grad, grads)


VECTORS = (1, 3, 4, 5, 6, 8, 11, 13, 14, 15, 19, 17)
LANES = 384
VEC_ROWS = 16
GATHER_CHUNKS = ((0, 2, "vec", 7, 9, 10), (12, "low"), ("high", 18))
SCATTER_CHUNKS = ((18, 16), (12, 7, 9, 10), (0, 2, "vec"))
BOTH = ("fsdp", "dp")
WIDTH = 768
HIDDEN = 3072
IMAGE = 325
TEXTS = 513
ROWS = 839
KEYS = 848
PADDED = 896
LOW = jnp.bfloat16
FULL = jnp.float32
COST_SCALE = 0.3
FAST = pl.BlockSpec(memory_space=pltpu.VMEM)
SCALARS = pl.BlockSpec(memory_space=pltpu.SMEM)


def cost(micros):
    return pl.CostEstimate(
        flops=int(micros * COST_SCALE * 1e9), bytes_accessed=1024, transcendentals=0
    )


class Place:
    def __init__(self):
        self.core = lax.axis_index("dp")
        chip = lax.axis_index("fsdp")
        self.x, self.y, self.z = chip & 1, (chip >> 1) & 1, chip >> 2
        self.scalars = jnp.stack([self.core, self.x, self.y, self.z]).astype(jnp.int32)


def shape(dims, kind=LOW):
    return jax.ShapeDtypeStruct(dims, kind)


def call(kernel, micros, outs, *args, scratch=(), limit=60):
    specs = [SCALARS if a.dtype == jnp.int32 else FAST for a in args]
    return pl.pallas_call(
        kernel,
        out_shape=tuple(outs),
        in_specs=specs,
        out_specs=tuple(FAST for _ in outs),
        scratch_shapes=list(scratch),
        compiler_params=pltpu.CompilerParams(vmem_limit_bytes=limit * 2**20),
        cost_estimate=cost(micros),
    )(*args)


def after(values, *others):
    return lax.optimization_barrier((values, others))[0]


def settle(*values):
    return lax.optimization_barrier(values)


def swap_cores(values):
    with jax.named_scope("between_cores"):
        return lax.ppermute(values, "dp", [(0, 1), (1, 0)])


def to_chip(values, mask_zero, mask_one):
    pairs = []
    for chip in range(16):
        pairs.append((chip * 2, (chip ^ mask_zero) * 2))
        pairs.append((chip * 2 + 1, (chip ^ mask_one) * 2 + 1))
    with jax.named_scope(f"chips_{mask_zero}_{mask_one}"):
        return lax.ppermute(values, BOTH, pairs)


def sub_blocks(index):
    return 4 if index == 16 else 1


def block_rows(index):
    return {"vec": VEC_ROWS, 16: 192, 18: 192, "low": 96, "high": 96}.get(index, 48)


def pack_kernel(chunk, at_ref, *refs):
    core = at_ref[0]
    count = len(chunk) + (11 if "vec" in chunk else 0)
    ins, out = refs[:count], refs[count]
    offset = 0
    order = [i for i in chunk if i != "vec"]
    for index in chunk:
        if index == "vec":
            rows = refs[-1]
            rows[...] = jnp.zeros_like(rows)
            for row in range(12):
                source = ins[len(order) + row]
                width = source.shape[0]
                rows[row : row + 1, 0:width] = source[...].astype(FULL).reshape(1, width)
            out[offset : offset + VEC_ROWS, :] = rows[...].astype(LOW)
            offset += VEC_ROWS
            continue
        parts = {"low": (4, (0, 1)), "high": (4, (2, 3))}.get(index, (1, (0,)))
        source = ins[order.index(index)]
        rows = source.shape[0]
        for s in parts[1]:
            first = pl.multiple_of((core * parts[0] + s) * LANES, LANES)
            out[offset : offset + rows, :] = source[:, pl.ds(first, LANES)]
            offset += rows


def pack(place, shards, chunk):
    rows = sum(block_rows(i) for i in chunk)
    ins = [shards[16 if i in ("low", "high") else i] for i in chunk if i != "vec"]
    scratch = ()
    if "vec" in chunk:
        ins += [shards[i] for i in VECTORS]
        scratch = (pltpu.VMEM((VEC_ROWS, LANES), FULL),)
    kernel = functools.partial(pack_kernel, chunk)
    return call(kernel, 1, [shape((rows, LANES))], place.scalars, *ins, scratch=scratch)[0]


def all_z(own):
    return [own] + [to_chip(own, 4 * s, 4 * s) for s in (1, 2, 3)]


def unpack(at_ref, pieces, targets):
    core, x, y, z = at_ref[0], at_ref[1], at_ref[2], at_ref[3]

    def fill(zero_s, zero_r, one_s, one_r):
        for offset, blocks, count, out in targets:
            rows = out.shape[3]
            for n, s in enumerate(blocks):
                first = slice(offset + n * rows, offset + (n + 1) * rows)
                left = slice(s * LANES, (s + 1) * LANES)
                right = slice((count + s) * LANES, (count + s + 1) * LANES)
                for far in range(4):
                    plane = z ^ far
                    for b in range(2):
                        out[plane, y, x ^ b, :, left] = zero_s[b, far, first, :]
                        out[plane, 1 - y, x ^ b, :, left] = zero_r[b, far, first, :]
                        if count:
                            out[plane, y ^ b, x, :, right] = one_s[b, far, first, :]
                            out[plane, y ^ b, 1 - x, :, right] = one_r[b, far, first, :]

    s8, r8, s8p, r8p = pieces

    @pl.when(core == 0)
    def _():
        fill(s8, r8, s8p, r8p)

    @pl.when(core == 1)
    def _():
        fill(s8p, r8p, s8, r8)


def square(ref):
    return ref[...].reshape(16 * ref.shape[3], ref.shape[4])


def row_chunks(step, total=ROWS):
    return [slice(a, min(a + step, total)) for a in range(0, total, step)]


def standard(values):
    centered = values - jnp.mean(values, -1, keepdims=True)
    scale = lax.rsqrt(jnp.mean(centered * centered, -1, keepdims=True) + EPSILON)
    return centered * scale, scale


def norm_back(values, gain, incoming):
    unit, scale = standard(values)
    f = incoming * gain
    back = (f - jnp.mean(f, -1, keepdims=True) - unit * jnp.mean(f * unit, -1, keepdims=True)) * scale
    return back, unit


def sum_rows(values):
    return jnp.sum(values.astype(FULL), 0, keepdims=True)


def embed_kernel(
    at, image, text, s8, r8, s8p, r8p,
    w_image, w_text, wq, wk, wv, vec, hid, embedded, normed, q, k, v, small,
):
    unpack(
        at,
        (s8, r8, s8p, r8p),
        (
            (0, (0,), 1, w_image),
            (48, (0,), 1, w_text),
            (96, (0,), 0, small),
            (112, (0,), 1, wq),
            (160, (0,), 1, wk),
            (208, (0,), 1, wv),
        ),
    )
    for f in range(16):
        piece = small[f >> 2, (f >> 1) & 1, f & 1].astype(FULL)
        vec[:, f * 48 : (f + 1) * 48] = piece[:, :48]
        hid[:, f * 192 : (f + 1) * 192] = piece[11:12, :192]
    embedded[0:1, :] = vec[2:3, :]
    embedded[1 : 1 + IMAGE, :] = matmul(image[...], square(w_image)) + vec[0:1, :]
    embedded[1 + IMAGE : ROWS, :] = matmul(text[...], square(w_text)) + vec[1:2, :]
    for rows in row_chunks(64):
        unit, unused_scale = standard(embedded[rows, :])
        normed[rows, :] = to_low(unit * vec[3:4, :] + vec[4:5, :])
    for out in (q, k, v):
        out[832:PADDED, :] = jnp.zeros((PADDED - 832, WIDTH), LOW)
    rows = normed[...]
    low = to_low(matmul(rows, square(wq)) + vec[5:6, :])
    q[0:ROWS, :] = to_low(low.astype(FULL) * HEAD_DIM**-0.5)
    k[0:ROWS, :] = to_low(matmul(rows, square(wk)))
    v[0:ROWS, :] = to_low(matmul(rows, square(wv)) + vec[6:7, :])


def embed(place, image, text, pieces):
    outs = [shape((4, 2, 2, 48, WIDTH))] * 5
    outs += [shape((VEC_ROWS, WIDTH), FULL), shape((1, HIDDEN), FULL)]
    outs += [shape((ROWS, WIDTH), FULL), shape((ROWS, WIDTH))] + [shape((PADDED, WIDTH))] * 3
    scratch = (pltpu.VMEM((4, 2, 2, VEC_ROWS, LANES), LOW),)
    return call(embed_kernel, 12, outs, place.scalars, image, text, *pieces, scratch=scratch)


def mask_column(live):
    position = lax.broadcasted_iota(jnp.int32, (KEYS, 1), 0)
    patches = jnp.where(live[0] == 1, PATCH_BIG, PATCH_SMALL).astype(jnp.int32)
    image_live = (position >= 1) & (position <= patches)
    text_live = (position >= 1 + PATCH_BIG) & (position < 1 + PATCH_BIG + live[1])
    return jnp.where((position == 0) | image_live | text_live, 0.0, NEGATIVE).astype(FULL)


def one_head(ref_value, head):
    lane = lax.broadcasted_iota(jnp.int32, ref_value.shape, 1)
    keep = (lane < HEAD_DIM) if head == 0 else (lane >= HEAD_DIM)
    return jnp.where(keep, ref_value, jnp.zeros_like(ref_value))


def across(values):
    return jnp.transpose(values.astype(FULL))


def fold_rows(values, op):
    return op(values.reshape(values.shape[0] // 8, 8, values.shape[1]), 0)


def attend_kernel(live, q, k, v, attended, totals, keys, scores, probs, mixed):
    bias = mask_column(live)
    for h in range(2):
        keys[h] = one_head(k[0:KEYS, :], h)
    values_t = to_low(across(v[0:KEYS, :]))
    totals[...] = jnp.zeros_like(totals)
    parts = [(piece, h) for piece in row_chunks(256, PADDED) for h in range(2)]
    tiles = row_chunks(128, KEYS)
    tops = {}

    def score(n, tile):
        piece, h = parts[n]
        made = right_product(keys[h, tile, :], q[piece, :]) + bias[tile, :]
        scores[n % 2, tile, 0 : made.shape[1]] = made
        top = fold_rows(made, jnp.max)
        tops[n] = jnp.maximum(tops[n], top) if n in tops else top

    for tile in tiles:
        score(0, tile)
    for n, (piece, h) in enumerate(parts):
        width = piece.stop - piece.start
        top = jnp.max(tops[n], 0, keepdims=True)
        total = jnp.zeros((8, width), FULL)
        for tile in tiles:
            if n + 1 < len(parts):
                score(n + 1, tile)
            exps = jnp.exp(scores[n % 2, tile, 0:width] - top)
            total = total + fold_rows(exps, jnp.sum)
            probs[n % 2, tile, 0:width] = to_low(exps)
        total = jnp.sum(total, 0, keepdims=True)
        rows = slice(h * HEAD_DIM, (h + 1) * HEAD_DIM)
        out = matmul(values_t[rows, :], probs[n % 2, :, 0:width])
        mixed[rows, piece] = out * (1.0 / total)
        totals[0, h : h + 1, piece] = top + jnp.log(total)
    attended[...] = to_low(jnp.transpose(mixed[...]))


def attend(live, q, k, v, first, count, earlier=()):
    spec = pl.BlockSpec((PADDED, 2 * HEAD_DIM), lambda i: (0, i + first))
    anywhere = pl.BlockSpec(memory_space=pl.ANY)

    def kernel(live, q, k, v, *refs):
        attend_kernel(live, q, k, v, *refs[len(earlier) :])

    return pl.pallas_call(
        kernel,
        grid=(count,),
        out_shape=(shape((PADDED, WIDTH)), shape((HEADS // 2, 8, PADDED), FULL)),
        in_specs=[SCALARS] + [spec] * 3 + [anywhere] * len(earlier),
        out_specs=(spec, pl.BlockSpec((1, 8, PADDED), lambda i: (i + first, 0, 0))),
        scratch_shapes=[
            pltpu.VMEM((2, KEYS, 2 * HEAD_DIM), LOW),
            pltpu.VMEM((2, KEYS, 256), FULL),
            pltpu.VMEM((2, KEYS, 256), LOW),
            pltpu.VMEM((2 * HEAD_DIM, PADDED), FULL),
        ],
        input_output_aliases={4 + n: n for n in range(len(earlier))},
        compiler_params=pltpu.CompilerParams(vmem_limit_bytes=60 * 2**20),
        cost_estimate=cost(3 * count),
    )(live, q, k, v, *earlier)


def attend_back_kernel(
    live, q, k, v, incoming, attended, totals, q_grad, k_grad, v_grad,
    keys, values, probs, score_grads, mixed,
):
    bias = mask_column(live)
    for h in range(2):
        keys[h] = one_head(k[0:KEYS, :], h)
        values[h] = one_head(v[0:KEYS, :], h)
    keys_t = to_low(across(k[0:KEYS, :]))
    product = jnp.transpose(incoming[...].astype(FULL) * attended[...].astype(FULL))
    for h in range(2):
        rows = slice(h * HEAD_DIM, (h + 1) * HEAD_DIM)
        along = jnp.sum(product[rows], 0, keepdims=True)
        for piece in row_chunks(256, PADDED):
            for tile in row_chunks(256, KEYS):
                made = right_product(keys[h, tile, :], q[piece, :]) + bias[tile, :]
                prob = jnp.exp(made - totals[0, h : h + 1, piece])
                prob_grad = right_product(values[h, tile, :], incoming[piece, :])
                probs[h, tile, piece] = to_low(prob)
                score_grads[h, tile, piece] = to_low(prob * (prob_grad - along[:, piece]))
        mixed[rows, :] = matmul(keys_t[rows, :], score_grads[h])
    lane = lax.broadcasted_iota(jnp.int32, (KEYS, 2 * HEAD_DIM), 1) < HEAD_DIM
    for out, left, right in ((k_grad, score_grads, q), (v_grad, probs, incoming)):
        right = right[...]
        out[0:KEYS, :] = to_low(jnp.where(lane, matmul(left[0], right), matmul(left[1], right)))
    q_grad[...] = to_low(jnp.transpose(mixed[...]) * HEAD_DIM**-0.5)


def attend_back(live, q, k, v, incoming, attended, totals):
    spec = pl.BlockSpec((PADDED, 2 * HEAD_DIM), lambda i: (0, i))
    return pl.pallas_call(
        attend_back_kernel,
        grid=(HEADS // 2,),
        out_shape=(shape((PADDED, WIDTH)),) * 3,
        in_specs=[SCALARS] + [spec] * 5 + [pl.BlockSpec((1, 8, PADDED), lambda i: (i, 0, 0))],
        out_specs=(spec,) * 3,
        scratch_shapes=[
            pltpu.VMEM((2, KEYS, 2 * HEAD_DIM), LOW),
            pltpu.VMEM((2, KEYS, 2 * HEAD_DIM), LOW),
            pltpu.VMEM((2, KEYS, PADDED), LOW),
            pltpu.VMEM((2, KEYS, PADDED), LOW),
            pltpu.VMEM((2 * HEAD_DIM, PADDED), FULL),
        ],
        compiler_params=pltpu.CompilerParams(vmem_limit_bytes=60 * 2**20),
        cost_estimate=cost(28),
    )(live, q, k, v, incoming, attended, totals)


def middle_kernel(
    at, attended, embedded, vec, s8, r8, s8p, r8p, s_hi, r_hi, sp_hi, rp_hi,
    w_out, w_hid, middle, second,
):
    unpack(at, (s8, r8, s8p, r8p), ((0, (0,), 1, w_out), (48, (0, 1), 4, w_hid)))
    unpack(at, (s_hi, r_hi, sp_hi, rp_hi), ((0, (2, 3), 4, w_hid),))
    middle[...] = embedded[...] + matmul(attended[0:ROWS, :], square(w_out)) + vec[7:8, :]
    for rows in row_chunks(64):
        unit, unused_scale = standard(middle[rows, :])
        second[rows, :] = to_low(unit * vec[8:9, :] + vec[9:10, :])


def middle_of(place, attended, embedded, vec, pieces):
    outs = [
        shape((4, 2, 2, 48, WIDTH)),
        shape((4, 2, 2, 48, HIDDEN)),
        shape((ROWS, WIDTH), FULL),
        shape((ROWS, WIDTH)),
    ]
    return call(middle_kernel, 8, outs, place.scalars, attended, embedded, vec, *pieces)


def gelu_parts(u):
    cumulative = 0.5 * (1.0 + lax.erf(u * (2.0**-0.5)))
    slope = cumulative + u * (jnp.exp(-0.5 * u * u) * (2.0 * math.pi) ** -0.5)
    return u * cumulative, slope


def feed_kernel(
    at, second, cot, middle, vec, w_hid, hid, s8, r8, s8p, r8p,
    layer_out, second_grad, ret_keep, ret_send, hid_keep, hid_send, hid_sum, ret_sum,
    w_ret, act, inner, total,
):
    step = pl.program_id(0)
    core, x, y = at[0], at[1], at[2]

    def fill(zero_s, zero_r, one_s, one_r):
        for b in range(2):
            w_ret[y, x ^ b, :, 0:LANES] = zero_s[b, 0]
            w_ret[1 - y, x ^ b, :, 0:LANES] = zero_r[b, 0]
            w_ret[y ^ b, x, :, LANES:] = one_s[b, 0]
            w_ret[y ^ b, 1 - x, :, LANES:] = one_r[b, 0]

    @pl.when(core == 0)
    def _():
        fill(s8, r8, s8p, r8p)

    @pl.when(core == 1)
    def _():
        fill(s8p, r8p, s8, r8)

    ret = w_ret[...].reshape(WIDTH, WIDTH)
    inward = w_hid[...]
    for rows in row_chunks(432):
        pre = matmul(second[rows, :], inward) + hid[...]
        back = right_product(cot[rows, :], ret)
        value, slope = gelu_parts(pre)
        act[rows, :] = to_low(value)
        inner[rows, :] = to_low(back * slope)
        out = matmul(act[rows, :], ret)
        back = right_product(inner[rows, :], inward)

        @pl.when(step == 0)
        def _():
            total[rows, :] = out
            second_grad[rows, :] = back

        @pl.when(step > 0)
        def _():
            total[rows, :] += out
            second_grad[rows, :] += back

    hid_sum[...] = sum_rows(inner[...])
    ret_grad = to_low(left_product(act[...], cot[...])).reshape(4, 192, WIDTH)
    hid_grad = to_low(left_product(second[...], inner[...])).reshape(16, 48, WIDTH)

    @pl.when(core == 0)
    def _():
        ret_keep[...] = ret_grad[:, :, 0:LANES]
        ret_send[...] = ret_grad[:, :, LANES:]

    @pl.when(core == 1)
    def _():
        ret_keep[...] = ret_grad[:, :, LANES:]
        ret_send[...] = ret_grad[:, :, 0:LANES]

    @pl.when(step < 2)
    def _():
        hid_send[:, 0:48, :] = hid_grad[:, :, 0:LANES]
        hid_send[:, 48:96, :] = hid_grad[:, :, LANES:]

    @pl.when(step >= 2)
    def _():
        hid_keep[:, 0:48, :] = hid_grad[:, :, 0:LANES]
        hid_keep[:, 48:96, :] = hid_grad[:, :, LANES:]

    @pl.when(step == 3)
    def _():
        layer_out[...] = to_low(middle[...] + total[...] + vec[10:11, :])
        ret_sum[...] = sum_rows(cot[...])


def feed(place, second, cot, middle, vec, w_hid, hid, pieces):
    def column(i, at):
        half = jnp.where(i < 2, 1 - at[0], at[0])
        return 2 * half + lax.rem(i, 2)

    def whole(dims):
        return pl.BlockSpec(dims, lambda i, at: (0,) * len(dims))

    piece = pl.BlockSpec((2, 1, 192, LANES), lambda i, at: (0, column(i, at) ^ at[3], 0, 0))
    ret_spec = pl.BlockSpec((4, 192, LANES), lambda i, at: (column(i, at), 0, 0))
    outs = (
        shape((ROWS, WIDTH)),
        shape((ROWS, WIDTH), FULL),
        shape((16, 192, LANES)),
        shape((16, 192, LANES)),
        shape((16, 192, LANES)),
        shape((16, 192, LANES)),
        shape((1, HIDDEN), FULL),
        shape((1, WIDTH), FULL),
    )
    grid = pltpu.PrefetchScalarGridSpec(
        num_scalar_prefetch=1,
        grid=(4,),
        in_specs=[
            whole((ROWS, WIDTH)),
            whole((ROWS, WIDTH)),
            whole((ROWS, WIDTH)),
            whole((VEC_ROWS, WIDTH)),
            pl.BlockSpec((WIDTH, WIDTH), lambda i, at: (0, column(i, at))),
            pl.BlockSpec((1, WIDTH), lambda i, at: (0, column(i, at))),
            piece,
            piece,
            piece,
            piece,
        ],
        out_specs=(
            whole((ROWS, WIDTH)),
            whole((ROWS, WIDTH)),
            ret_spec,
            ret_spec,
            pl.BlockSpec((16, 96, LANES), lambda i, at: (0, jnp.maximum(i - 2, 0), 0)),
            pl.BlockSpec((16, 96, LANES), lambda i, at: (0, jnp.minimum(i, 1), 0)),
            pl.BlockSpec((1, WIDTH), lambda i, at: (0, column(i, at))),
            whole((1, WIDTH)),
        ),
        scratch_shapes=[
            pltpu.VMEM((2, 2, 192, WIDTH), LOW),
            pltpu.VMEM((ROWS, WIDTH), LOW),
            pltpu.VMEM((ROWS, WIDTH), LOW),
            pltpu.VMEM((ROWS, WIDTH), FULL),
        ],
    )
    return pl.pallas_call(
        feed_kernel,
        grid_spec=grid,
        out_shape=outs,
        compiler_params=pltpu.CompilerParams(vmem_limit_bytes=63 * 2**20),
        cost_estimate=cost(40),
    )(place.scalars, second, cot, middle, vec, w_hid, hid, *pieces)


def branch_kernel(middle, second_grad, cot, vec, w_out, middle_grad, branch, incoming, sums):
    parts = [jnp.zeros((1, WIDTH), FULL)] * 3
    for rows in row_chunks(64):
        e = second_grad[rows, :]
        back, unit = norm_back(middle[rows, :], vec[8:9, :], e)
        grad = cot[rows, :].astype(FULL) + back
        middle_grad[rows, :] = grad
        branch[rows, :] = to_low(grad)
        for n, term in enumerate((e * unit, e, to_low(grad))):
            parts[n] = parts[n] + sum_rows(term)
    for n in range(3):
        sums[n : n + 1, :] = parts[n]
    incoming[832:PADDED, :] = jnp.zeros((PADDED - 832, WIDTH), LOW)
    incoming[0:ROWS, :] = to_low(right_product(branch[...], square(w_out)))


def branch_of(middle, second_grad, cot, vec, w_out):
    outs = [
        shape((ROWS, WIDTH), FULL),
        shape((ROWS, WIDTH)),
        shape((PADDED, WIDTH)),
        shape((8, WIDTH), FULL),
    ]
    return call(branch_kernel, 8, outs, middle, second_grad, cot, vec, w_out)


def both_halves(core, left_t, right_ref, first, keep, send, offset):
    for half, out in ((core, keep), (1 - core, send)):
        columns = pl.ds(pl.multiple_of(half * LANES, LANES), LANES)
        grad = matmul(left_t, right_ref[first, columns])
        out[:, offset : offset + 48, :] = to_low(grad).reshape(16, 48, LANES)


def square_grads_kernel(at, attended, branch, normed, dq, dk, dv, keep, send):
    rows = slice(0, ROWS)
    both_halves(at[0], jnp.transpose(attended[rows, :]), branch, rows, keep, send, 0)
    left_t = jnp.transpose(normed[...])
    for n, ref in enumerate((dq, dk, dv)):
        both_halves(at[0], left_t, ref, rows, keep, send, 48 * (n + 1))


def square_grads(place, attended, branch, normed, grads):
    outs = [shape((16, 192, LANES))] * 2
    return call(
        square_grads_kernel, 11, outs, place.scalars, attended, branch, normed, *grads
    )


def norm_one_kernel(
    dq, dk, dv, wq, wk, wv, embedded, middle_grad, vec, image_low, text_low, late, grad
):
    rows = slice(0, ROWS)
    grad[...] = (
        right_product(dq[rows, :], square(wq))
        + right_product(dk[rows, :], square(wk))
        + right_product(dv[rows, :], square(wv))
    )
    parts = [jnp.zeros((1, WIDTH), FULL)] * 4
    for piece in row_chunks(64):
        e = grad[piece, :]
        back, unit = norm_back(embedded[piece, :], vec[3:4, :], e)
        for n, term in enumerate((e * unit, e, dq[piece, :], dv[piece, :])):
            parts[n] = parts[n] + sum_rows(term)
        grad[piece, :] = middle_grad[piece, :] + back
    image_low[...] = to_low(grad[1 : 1 + IMAGE, :])
    text_low[...] = to_low(grad[1 + IMAGE : ROWS, :])
    late[...] = jnp.zeros_like(late)
    late[0:1, :] = grad[0:1, :]
    for n in range(4):
        late[n + 1 : n + 2, :] = parts[n]


def norm_one(grads, projs, embedded, middle_grad, vec):
    outs = [shape((IMAGE, WIDTH)), shape((TEXTS, WIDTH)), shape((8, WIDTH), FULL)]
    scratch = (pltpu.VMEM((ROWS, WIDTH), FULL),)
    return call(
        norm_one_kernel, 11, outs, *grads, *projs, embedded, middle_grad, vec, scratch=scratch
    )


def last_kernel(
    at, image, text, image_low, text_low, sums, hid_sum, ret_sum, late,
    keep, send, rows16, packed,
):
    both_halves(at[0], jnp.transpose(image[...]), image_low, slice(0, IMAGE), keep, send, 0)
    both_halves(at[0], jnp.transpose(text[...]), text_low, slice(0, TEXTS), keep, send, 48)
    rows16[...] = jnp.zeros_like(rows16)
    found = (
        sum_rows(image_low[...]), sum_rows(text_low[...]), late[0:1, :], late[1:2, :], late[2:3, :],
        late[3:4, :], late[4:5, :], sums[2:3, :], sums[0:1, :], sums[1:2, :], ret_sum[...],
    )
    for n, value in enumerate(found):
        rows16[n : n + 1, :] = value
    packed[...] = jnp.zeros_like(packed)
    for f in range(16):
        packed[f, :, 0:48] = rows16[:, f * 48 : (f + 1) * 48]
        packed[f, 11:12, 0:192] = hid_sum[:, f * 192 : (f + 1) * 192]
    low = to_low(packed[...])
    keep[:, 96:112, :] = low
    send[:, 96:112, :] = low


def last(place, image, text, image_low, text_low, sums, hid_sum, ret_sum, late):
    outs = [shape((16, 112, LANES)), shape((16, 112, LANES))]
    scratch = (pltpu.VMEM((VEC_ROWS, WIDTH), FULL), pltpu.VMEM((16, VEC_ROWS, LANES), FULL))
    return call(
        last_kernel, 5.5, outs, place.scalars, image, text, image_low, text_low, sums, hid_sum, ret_sum,
        late, scratch=scratch,
    )


def inputs_kernel(image_low, text_low, w_image, w_text, image_grad, text_grad):
    image_grad[:, 0, :] = right_product(image_low[...], square(w_image))
    text_grad[:, 0, :] = right_product(text_low[...], square(w_text))


def input_grads(image_low, text_low, w_image, w_text):
    outs = [shape((IMAGE, 1, WIDTH), FULL), shape((TEXTS, 1, WIDTH), FULL)]
    return call(inputs_kernel, 4.4, outs, image_low, text_low, w_image, w_text)


def add_low(*values):
    total = values[0].astype(FULL)
    for value in values[1:]:
        total = total + value.astype(FULL)
    return to_low(total)


def pick(values, at, axis):
    return lax.dynamic_index_in_dim(values, at, axis, keepdims=False)


class Scatter:
    def __init__(self, place, pairs):
        self.place = place
        self.kept = [keep for keep, unused_send in pairs]
        self.sent = [send for unused_keep, send in pairs]
        self.got = None

    def state(self):
        return self.kept, self.got

    def summed(self, q):
        parts = []
        for keep, more in zip(self.kept, self.swapped):
            keep, more = (pick(v.reshape(4, 4, v.shape[1], LANES), q, 1) for v in (keep, more))
            parts.append(keep.astype(FULL) + more.astype(FULL))
        return jnp.concatenate(parts, 1) if len(parts) > 1 else parts[0]

    def first(self):
        zero, x, y = self.place.core == 0, self.place.x, self.place.y
        self.swapped = self.got
        far = [jnp.where(zero, 2 * (1 - y) + s, 2 * s + (1 - x)) for s in (0, 1)]
        self.sent = jnp.stack([to_low(self.summed(q)) for q in far], 1)

    def second(self):
        zero, x, y = self.place.core == 0, self.place.x, self.place.y
        mine = jnp.where(zero, x, y)

        def added(s):
            near = self.summed(jnp.where(zero, 2 * y + s, 2 * s + x))
            return to_low(near + pick(self.got, s, 1).astype(FULL))

        self.sent, self.kept = added(1 - mine), added(mine)

    def third(self):
        z = self.place.z
        total = add_low(self.kept, self.got)
        self.kept = pick(total, z, 0)
        self.sent = [pick(total, z ^ s, 0) for s in (1, 2, 3)]

    def fourth(self):
        self.sent = self.kept = add_low(self.kept, *self.got)

    def swap(self):
        self.got = jax.tree.map(swap_cores, self.sent)

    def send_first(self):
        self.got = to_chip(self.sent, 2, 1)

    def send_second(self):
        self.got = to_chip(self.sent, 1, 2)

    def send_third(self, steps=(1, 2, 3)):
        self.got = [to_chip(self.sent[s - 1], 4 * s, 4 * s) for s in steps]

    def sides(self):
        zero = self.place.core == 0
        mine, other = self.kept, self.got
        return jnp.where(zero, mine, other).astype(FULL), jnp.where(zero, other, mine).astype(FULL)


def owned_rows(chunk, left, right):
    result, at = {}, 0
    for index in chunk:
        rows = block_rows(index)
        if index == "vec":
            for n, vector in enumerate(VECTORS):
                result[vector] = left[at + n, : 192 if vector == 17 else 48]
        else:
            count = sub_blocks(index)
            step = rows // count
            sides = [
                side[at + s * step : at + (s + 1) * step] for side in (left, right) for s in range(count)
            ]
            result[index] = jnp.concatenate(sides, 1)
        at += rows
    return result


def by_kernels(shards, image, text, size_code, length, cot):
    place = Place()
    live = jnp.concatenate([size_code, length]).astype(jnp.int32)
    own_one = pack(place, shards, GATHER_CHUNKS[0])

    z_one = all_z(own_one)
    owns = [pack(place, shards, chunk) for chunk in GATHER_CHUNKS[1:]]
    z_one, owns = settle(z_one, owns)

    z_one = jnp.stack(z_one)
    b_one, z_a, z_one, owns = settle(to_chip(z_one, 1, 2), all_z(owns[0]), z_one, owns)

    s_one, z_a = jnp.stack([z_one, b_one]), jnp.stack(z_a)
    r_one, sp_one, z_b, s_one, z_a = settle(
        to_chip(s_one, 2, 1), swap_cores(s_one), all_z(owns[1]), s_one, z_a
    )

    rp_one, b_a = swap_cores(r_one), to_chip(z_a, 1, 2)
    z_b = jnp.stack(z_b)
    b_b = to_chip(z_b, 1, 2)
    w_image, w_text, wq, wk, wv, vec, hid, embedded, normed, q, k, v = embed(
        place, image, after(text, z_a, z_b), (s_one, r_one, sp_one, rp_one)
    )
    b_a, b_b, z_a, z_b, q = settle(b_a, b_b, z_a, z_b, q)

    s_a, s_b = jnp.stack([z_a, b_a]), jnp.stack([z_b[:, :96], b_b[:, :96]])
    s_c = jnp.stack([z_b[:, 96:], b_b[:, 96:]])
    r_a, r_b, sp_a = to_chip(s_a, 2, 1), to_chip(s_b, 2, 1), swap_cores(s_a)
    both = attend(live, after(q, s_a, s_b, s_c), k, v, 0, 3)
    r_a, r_b, sp_a, both, s_b, s_c = settle(r_a, r_b, sp_a, both, s_b, s_c)

    r_c, sp_b, sp_c = to_chip(s_c, 2, 1), swap_cores(s_b), swap_cores(s_c)
    rp_a, rp_b = swap_cores(r_a), swap_cores(r_b)
    attended, totals = attend(live, q, k, v, 3, 3, both)
    r_c, sp_b, sp_c, rp_a, rp_b, attended = settle(r_c, sp_b, sp_c, rp_a, rp_b, attended)

    rp_c = swap_cores(r_c)
    w_out, w_hid, middle, second = middle_of(
        place, attended, embedded, vec, (s_a, r_a, sp_a, rp_a, s_b, r_b, sp_b, rp_b)
    )
    rp_c, second = settle(rp_c, second)

    layer_out, second_grad, ret_keep, ret_send, hid_keep, hid_send, hid_sum, ret_sum = feed(
        place, second, cot, middle, vec, w_hid.reshape(WIDTH, HIDDEN), hid,
        (s_c, r_c, sp_c, rp_c),
    )

    feeding = Scatter(place, ((ret_keep, ret_send), (hid_keep, hid_send)))
    feeding.swap()
    middle_grad, branch, incoming, sums = branch_of(middle, second_grad, cot, vec, w_out)
    feeding.got, feeding.kept, incoming = settle(feeding.got, feeding.kept, incoming)

    feeding.first()
    feeding.send_first()
    incoming = after(incoming, feeding.sent, feeding.kept)
    grads = attend_back(live, q, k, v, incoming, attended, totals)
    pair = square_grads(place, attended, branch, normed, grads)
    feeding.got, feeding.kept, grads, pair = settle(feeding.got, feeding.kept, grads, pair)

    feeding.second()
    feeding.send_second()
    squares = Scatter(place, (pair,))
    squares.swap()
    grads = after(grads, feeding.sent, feeding.kept, squares.kept)
    image_low, text_low, late = norm_one(grads, (wq, wk, wv), embedded, middle_grad, vec)
    feeding.got, feeding.kept, squares.got, squares.kept, image_low, text_low = settle(
        feeding.got, feeding.kept, squares.got, squares.kept, image_low, text_low
    )

    feeding.third()
    feeding.send_third((1, 3))
    squares.first()
    squares.send_first()
    image_low, text_low = after(
        (image_low, text_low), squares.sent, squares.kept, feeding.sent, feeding.kept
    )
    pair = last(place, image, text, image_low, text_low, sums, hid_sum, ret_sum, late)
    image_grad, text_grad = input_grads(image_low, text_low, w_image, w_text)
    early, feeding.sent, squares.got, squares.kept, pair, image_grad, text_grad = settle(
        feeding.got, feeding.sent, squares.got, squares.kept, pair, image_grad, text_grad
    )

    feeding.send_third((2,))
    ending = Scatter(place, (pair,))
    ending.swap()
    squares.second()
    squares.send_second()
    feeding.got, ending.got, ending.kept, squares.got, squares.kept = settle(
        feeding.got + early, ending.got, ending.kept, squares.got, squares.kept
    )

    ending.first()
    ending.send_first()
    squares.third()
    squares.send_third()
    feeding.fourth()
    ending.got, ending.kept, squares.got, squares.kept, feeding.sent = settle(
        ending.got, ending.kept, squares.got, squares.kept, feeding.sent
    )

    feeding.kept = feeding.sent
    feeding.swap()
    ending.second()
    ending.send_second()
    squares.fourth()
    squares.swap()
    ending.got, ending.kept, squares.got, feeding.got = settle(
        ending.got, ending.kept, squares.got, feeding.got
    )

    owned = owned_rows(SCATTER_CHUNKS[0], *feeding.sides())
    ending.third()
    ending.send_third()
    owned.update(owned_rows(SCATTER_CHUNKS[1], *squares.sides()))
    ending.got, ending.kept, owned = settle(ending.got, ending.kept, owned)

    ending.fourth()
    ending.swap()
    owned.update(owned_rows(SCATTER_CHUNKS[2], *ending.sides()))
    image_grad, text_grad = (jnp.transpose(grad, (1, 0, 2)) for grad in (image_grad, text_grad))
    return (layer_out[None], image_grad, text_grad) + tuple(owned[i] for i in range(20))


def gather_any(shards):
    return tuple(lax.all_gather(shard, "fsdp", axis=0, tiled=True) for shard in shards)


def scatter_any(grads):
    pieces = [lax.psum_scatter(g, "fsdp", scatter_dimension=0, tiled=True) for g in grads]
    return tuple(lax.psum(to_low(p), "dp").astype(jnp.float32) for p in pieces)


def on_device(
    chips,
    cores,
    image_states,
    text_states,
    size_group,
    caption_len,
    cotangent,
    image_proj,
    image_bias,
    text_proj,
    text_bias,
    cls_token,
    first_gain,
    first_shift,
    query_proj,
    query_bias,
    key_proj,
    value_proj,
    value_bias,
    output_proj,
    output_bias,
    second_gain,
    second_shift,
    hidden_proj,
    hidden_bias,
    return_proj,
    return_bias,
):
    shards = (
        image_proj,
        image_bias,
        text_proj,
        text_bias,
        cls_token,
        first_gain,
        first_shift,
        query_proj,
        query_bias,
        key_proj,
        value_proj,
        value_bias,
        output_proj,
        output_bias,
        second_gain,
        second_shift,
        hidden_proj,
        hidden_bias,
        return_proj,
        return_bias,
    )
    fits = chips == 16 and cores == 2 and image_states.shape == (1, IMAGE, WIDTH)
    if fits and text_states.shape == (1, TEXTS, WIDTH) and hidden_proj.shape == (48, HIDDEN):
        image, text, cot = image_states[0], text_states[0], cotangent[0]
        return by_kernels(shards, image, text, size_group, caption_len, cot)
    weights = gather_any(shards)
    results, summed = [], None
    for item in range(image_states.shape[0]):
        image_rows, text_rows = image_states[item], text_states[item]
        code, length = size_group[item], caption_len[item]
        result, kept_rows = item_forward(weights, image_rows, text_rows, code, length)
        image_grad, text_grad, grads = item_backward(
            weights, image_rows, text_rows, code, length, kept_rows, cotangent[item]
        )
        results.append((result, image_grad, text_grad))
        summed = grads if summed is None else jax.tree.map(jnp.add, summed, grads)
    owned = scatter_any(summed)
    return tuple(jnp.stack(parts) for parts in zip(*results)) + owned


def solution(mesh):
    placed = (
        P(("fsdp", "dp"), None, None),
        P(("fsdp", "dp"), None, None),
        P(("fsdp", "dp")),
        P(("fsdp", "dp")),
        P(("fsdp", "dp"), None, None),
        P("fsdp", None),
        P("fsdp"),
        P("fsdp", None),
        P("fsdp"),
        P("fsdp"),
        P("fsdp"),
        P("fsdp"),
        P("fsdp", None),
        P("fsdp"),
        P("fsdp", None),
        P("fsdp", None),
        P("fsdp"),
        P("fsdp", None),
        P("fsdp"),
        P("fsdp"),
        P("fsdp"),
        P("fsdp", None),
        P("fsdp"),
        P("fsdp", None),
        P("fsdp"),
    )
    chips, cores = mesh.shape["fsdp"], mesh.shape["dp"]
    return jax.shard_map(
        functools.partial(on_device, chips, cores),
        mesh=mesh,
        in_specs=placed,
        out_specs=(
            P(("fsdp", "dp"), None, None),
            P(("fsdp", "dp"), None, None),
            P(("fsdp", "dp"), None, None),
            P("fsdp", None),
            P("fsdp"),
            P("fsdp", None),
            P("fsdp"),
            P("fsdp"),
            P("fsdp"),
            P("fsdp"),
            P("fsdp", None),
            P("fsdp"),
            P("fsdp", None),
            P("fsdp", None),
            P("fsdp"),
            P("fsdp", None),
            P("fsdp"),
            P("fsdp"),
            P("fsdp"),
            P("fsdp", None),
            P("fsdp"),
            P("fsdp", None),
            P("fsdp"),
        ),
        check_vma=False,
    )
```
